32 devices in a mesh: layer: 4 (over y, x), row: 2 (over core), col: 4 (over z).
Axes of the slice: x: 2, y: 2, z: 4, core: 2. Of those that a mesh axis runs over, the one named last changes fastest.
Arguments:
- partial_top: float32 [4, 4096, 4096], P('layer', 'row', 'col'), as said below
- partial_mid: float32 [4, 3072, 3072], P('layer', 'row', 'col'), may hold values from -6 to 6
- partial_low: float32 [4, 2048, 2048], P('layer', 'row', 'col'), may hold values from -6 to 6
- pattern_top: int32 [4, 32, 32], P('layer', 'row', 'col'), may hold values 0 or 1
- pattern_mid: int32 [4, 24, 24], P('layer', 'row', 'col'), may hold values 0 or 1
- pattern_low: int32 [4, 16, 16], P('layer', 'row', 'col'), may hold values 0 or 1
- pivots: int32 [4096], P('row'), may hold values from 0 to 4095, as said below
Outputs:
- top_factor: float32 [4096, 4096], P('row', 'col')
- mid_sums: float32 [4, 3072, 3072], P('layer', 'row', 'col')
- low_sums: float32 [4, 2048, 2048], P('layer', 'row', 'col')
The draws below stay inside these ranges and needn't reach their ends.
Inputs may be any that keep to these rules, and one draw needn't show every extreme that they name: `pivots`: each aligned block of 128 positions holds a permutation of the same 128 row numbers. `partial_top`: each column has one larger positive entry, at row pivots[column].
All inputs are finite; a program needn't handle non-finite values. No bound on the sum of `pattern_top` or of `pattern_mid` or of `pattern_low` on one device may be relied on, other than what follows from the above.
Results may differ from the reference program's by a relative error of at most 0.0017.
Values may be sent and summed in bfloat16 or wider, within the bound.
No kernel may reach another device: no remote copies, remote signals or barrier semaphores. Data moves between devices by JAX's collectives and lax.ppermute only.
A program may use at most 128 MiB of HBM per device.

```python
import jax
import jax.numpy as jnp
from jax import lax

S1 = 4096
S2 = 3072
S3 = 2048
PANEL = 128
BLK = 128
LAYERS = 4
N_LAYER = 4


def pivot_order(key):
    block_count = S1 // BLK
    block_keys = jax.random.split(key, block_count)
    within = jax.vmap(lambda single: jax.random.permutation(single, BLK))(block_keys)
    offsets = (jnp.arange(block_count, dtype=jnp.int32) * BLK)[:, None]
    return (within.astype(jnp.int32) + offsets).reshape(S1)


def draw_pivots(key, part):
    return pivot_order(key)


def draw_partial_top(key, part):
    row_order = pivot_order(key)
    key = jax.random.fold_in(key, 7)
    normal_key, diag_key = jax.random.split(key, 2)
    spread = 0.75 / jnp.sqrt(jnp.float32(PANEL * N_LAYER))
    entries = jnp.clip(jax.random.normal(normal_key, (N_LAYER, S1, S1), jnp.float32), -6.0, 6.0)
    diagonal = jax.random.uniform(diag_key, (N_LAYER, S1), jnp.float32, 0.4, 0.6) * (3.0 / N_LAYER)
    columns = jnp.arange(S1, dtype=jnp.int32)
    return (entries * spread).at[:, row_order, columns].add(diagonal)


def set_ends(array, own_key, smallest, top_value):
    longest = array.shape.index(max(array.shape))
    spots = []
    for shift in (0, 1):
        where = [jax.random.randint(jax.random.fold_in(own_key, axis), (), 0, length) for axis, length in enumerate(array.shape)]
        where[longest] = (where[longest] + shift) % array.shape[longest]
        spots.append(tuple(where))
    return array.at[spots[0]].set(smallest).at[spots[1]].set(top_value)


def level_of(rng, shape, cuts, least, largest):
    level, own = 1.0, jax.random.fold_in(rng, 6)
    for position, shards_of in cuts:
        steps = jnp.exp(jax.random.uniform(jax.random.fold_in(own, position), (shards_of,), jnp.float32, least / len(cuts), largest / len(cuts)))
        level = level * jnp.repeat(steps, shape[position] // shards_of).reshape([-1 if axis == position else 1 for axis in range(len(shape))])
    return level


def centred(stream_key, shape, scale, bound, cuts=(), kind=jnp.bfloat16):
    result = jax.random.normal(stream_key, shape, jnp.float32) * scale
    if len(cuts) > 0:
        result = level_of(stream_key, shape, cuts, -0.22, 0.18) * result
    return jnp.clip(result, min=-bound, max=bound).astype(kind)


def setup_inputs(seed: int = 0) -> dict:
    splits = jax.random.split(jax.random.key(seed), 8)
    return {
        "partial_top": draw_partial_top(jax.random.fold_in(splits[7], 71), 0),
        "partial_mid": centred(splits[1], (LAYERS, S2, S2), 1.0, 6.0, ((0, 4), (1, 2), (2, 4)), jnp.float32),
        "partial_low": centred(splits[2], (LAYERS, S3, S3), 1.0, 6.0, ((0, 4), (1, 2), (2, 4)), jnp.float32),
        "pattern_top": set_ends((jax.random.randint(splits[3], (LAYERS, S1 // BLK, S1 // BLK), 0, 4) < 3).astype(jnp.int32), jax.random.fold_in(splits[3], 1), 0, 1),
        "pattern_mid": set_ends((jax.random.randint(splits[4], (LAYERS, S2 // BLK, S2 // BLK), 0, 4) < 3).astype(jnp.int32), jax.random.fold_in(splits[4], 1), 0, 1),
        "pattern_low": set_ends((jax.random.randint(splits[5], (LAYERS, S3 // BLK, S3 // BLK), 0, 4) < 3).astype(jnp.int32), jax.random.fold_in(splits[5], 1), 0, 1),
        "pivots": draw_pivots(jax.random.fold_in(splits[7], 71), 0),
    }


def split_factors(packed):
    order = packed.shape[0]
    lower_unit = jnp.tril(packed, -1) + jnp.eye(order, dtype=packed.dtype)
    upper_part = jnp.triu(packed)
    return lower_unit, upper_part


def highest_dot(left, right):
    return jnp.dot(left, right, precision=lax.Precision.HIGHEST)


def invert_lower_leaf(lower):
    order = lower.shape[0]
    positions = lax.broadcasted_iota(jnp.int32, (order,), 0)

    def substitute(step, current):
        row = lax.dynamic_index_in_dim(lower, step, 0, keepdims=False)
        row = jnp.where(positions < step, row, jnp.zeros_like(row))
        unit = (positions == step).astype(lower.dtype)
        fresh = unit - highest_dot(row, current)
        return lax.dynamic_update_index_in_dim(current, fresh, step, 0)

    return lax.fori_loop(0, order, substitute, jnp.zeros_like(lower))


def invert_upper_leaf(upper):
    order = upper.shape[0]
    positions = lax.broadcasted_iota(jnp.int32, (order,), 0)

    def substitute(count, current):
        step = order - 1 - count
        row = lax.dynamic_index_in_dim(upper, step, 0, keepdims=False)
        pivot_value = lax.dynamic_index_in_dim(row, step, 0, keepdims=False)
        row = jnp.where(positions > step, row, jnp.zeros_like(row))
        unit = (positions == step).astype(upper.dtype)
        fresh = (unit - highest_dot(row, current)) / pivot_value
        return lax.dynamic_update_index_in_dim(current, fresh, step, 0)

    return lax.fori_loop(0, order, substitute, jnp.zeros_like(upper))


def invert_lower(lower):
    order = lower.shape[0]
    if order <= 128:
        return invert_lower_leaf(lower)
    middle = order // 2
    first = invert_lower(lower[:middle, :middle])
    second = invert_lower(lower[middle:, middle:])
    below = -highest_dot(second, highest_dot(lower[middle:, :middle], first))
    top_rows = jnp.concatenate([first, jnp.zeros((middle, order - middle), lower.dtype)], axis=1)
    bottom_rows = jnp.concatenate([below, second], axis=1)
    return jnp.concatenate([top_rows, bottom_rows], axis=0)


def invert_upper(upper):
    order = upper.shape[0]
    if order <= 128:
        return invert_upper_leaf(upper)
    middle = order // 2
    first = invert_upper(upper[:middle, :middle])
    second = invert_upper(upper[middle:, middle:])
    above = -highest_dot(first, highest_dot(upper[:middle, middle:], second))
    top_rows = jnp.concatenate([first, above], axis=1)
    bottom_rows = jnp.concatenate([jnp.zeros((order - middle, middle), upper.dtype), second], axis=1)
    return jnp.concatenate([top_rows, bottom_rows], axis=0)


def factor_leaf(matrix):
    order = matrix.shape[0]
    positions = lax.broadcasted_iota(jnp.int32, (order,), 0)

    def eliminate(step, current):
        pivot_col = lax.dynamic_index_in_dim(current, step, 1, keepdims=False)
        pivot_row = lax.dynamic_index_in_dim(current, step, 0, keepdims=False)
        pivot_value = lax.dynamic_index_in_dim(pivot_row, step, 0, keepdims=False)
        below = positions > step
        multipliers = jnp.where(below, pivot_col / pivot_value, jnp.zeros_like(pivot_col))
        right_row = jnp.where(below, pivot_row, jnp.zeros_like(pivot_row))
        current = current - multipliers[:, None] * right_row[None, :]
        target = below[:, None] & (positions[None, :] == step)
        return jnp.where(target, multipliers[:, None], current)

    return lax.fori_loop(0, order - 1, eliminate, matrix)


def factor_block(matrix):
    order = matrix.shape[0]
    if order <= 128:
        return factor_leaf(matrix)
    middle = order // 2
    leading = factor_block(matrix[:middle, :middle])
    lower_unit, upper_part = split_factors(leading)
    right_part = highest_dot(invert_lower(lower_unit), matrix[:middle, middle:])
    left_part = highest_dot(matrix[middle:, :middle], invert_upper(upper_part))
    remainder = matrix[middle:, middle:] - highest_dot(left_part, right_part)
    closing = factor_block(remainder)
    upper_rows = jnp.concatenate([leading, right_part], axis=1)
    lower_rows = jnp.concatenate([left_part, closing], axis=1)
    return jnp.concatenate([upper_rows, lower_rows], axis=0)


def expand_kept(pattern, row_start, col_start):
    block_rows, block_cols = pattern.shape
    block_row = row_start + lax.broadcasted_iota(jnp.int32, (block_rows, block_cols), 0)
    block_col = col_start + lax.broadcasted_iota(jnp.int32, (block_rows, block_cols), 1)
    kept = (pattern == 1) | (block_row == block_col)
    kept = jnp.broadcast_to(kept[:, None, :, None], (block_rows, BLK, block_cols, BLK))
    return kept.reshape(block_rows * BLK, block_cols * BLK)


def masked_copies(partial_value, pattern):
    kept = jax.vmap(lambda single: expand_kept(single, 0, 0))(pattern)
    return jnp.where(kept, partial_value, jnp.float32(0.0))


def group_sums(stack, group):
    shaped = stack.reshape((N_LAYER // group, group) + stack.shape[1:])
    return jnp.repeat(jnp.sum(shaped, axis=1), group, axis=0)


def reference(partial_top, partial_mid, partial_low, pattern_top, pattern_mid, pattern_low, pivots):
    mid_sums = group_sums(masked_copies(partial_mid, pattern_mid), min(4, N_LAYER))
    low_sums = group_sums(masked_copies(partial_low, pattern_low), min(2, N_LAYER))
    summed = jnp.sum(masked_copies(partial_top, pattern_top), axis=0)
    permuted = jnp.take(summed, pivots.astype(jnp.int32), axis=0)
    packed = factor_block(permuted[:PANEL, :PANEL])
    lower_unit, upper_part = split_factors(packed)
    lower_panel = highest_dot(permuted[:, :PANEL], invert_upper(upper_part))
    upper_panel = highest_dot(invert_lower(lower_unit), permuted[:PANEL, :])
    lower_low = lower_panel.astype(jnp.bfloat16)
    upper_low = upper_panel.astype(jnp.bfloat16)
    trailing = permuted - jnp.dot(lower_low, upper_low, preferred_element_type=jnp.float32)
    global_row = lax.broadcasted_iota(jnp.int32, (S1, S1), 0)
    global_col = lax.broadcasted_iota(jnp.int32, (S1, S1), 1)
    empty = jnp.zeros((S1, S1), jnp.float32)
    corner_full = empty.at[:PANEL, :PANEL].set(packed)
    upper_full = empty.at[:PANEL, :].set(upper_panel)
    lower_full = empty.at[:, :PANEL].set(lower_panel)
    top_factor = jnp.where((global_row < PANEL) & (global_col < PANEL), corner_full,
                           jnp.where(global_row < PANEL, upper_full,
                                     jnp.where(global_col < PANEL, lower_full, trailing)))
    return top_factor, mid_sums, low_sums
```

```python
import jax
import jax.numpy as jnp
from jax import lax
from jax.experimental import pallas as pl
from jax.experimental.pallas import tpu as pltpu
from jax.sharding import PartitionSpec as P

PANEL = 128
BLK = 128
EXTRA = 16
HIGHEST = lax.Precision.HIGHEST
VMEM_LIMIT = 48 * 1024 * 1024

SMEM_SPEC = pl.BlockSpec(memory_space=pltpu.SMEM)
VMEM_SPEC = pl.BlockSpec(memory_space=pltpu.VMEM)


def params():
    return pltpu.CompilerParams(vmem_limit_bytes=VMEM_LIMIT)


def cost(nbytes, flops=0):
    return pl.CostEstimate(flops=int(flops), bytes_accessed=int(nbytes), transcendentals=0)


def swapped(value, bit):
    count = lax.axis_size("layer")
    return lax.ppermute(value, "layer", [(i, i ^ (1 << bit)) for i in range(count)])


def broadcast_from_first(value, axis):
    count = lax.axis_size(axis)
    own = lax.axis_index(axis)
    span = count // 2
    while span >= 1:
        got = lax.ppermute(value, axis, [(i, i + span) for i in range(0, count, 2 * span)])
        value = jnp.where(own % (2 * span) == span, got, value)
        span //= 2
    return value


def exponents(largest):
    return jnp.floor(jnp.log2(jnp.maximum(largest, 1e-30))) - 14.0


def coded(value, inverse):
    scaled = jnp.round(value * inverse)
    scaled = jnp.minimum(jnp.maximum(scaled, -32767.0), 32767.0)
    return scaled.astype(jnp.int32).astype(jnp.int16)


def scales(code_ref, rows, cols):
    held = code_ref[pl.ds(rows, EXTRA), cols].astype(jnp.int32).astype(jnp.float32)
    return jnp.exp2(held[0:1])


def decoded(code_ref, row, scale, cols):
    return code_ref[pl.ds(row, BLK), cols].astype(jnp.int32).astype(jnp.float32) * scale


def encode_columns(load, out_ref, rows, cols):
    largest = jnp.zeros((1, BLK), jnp.float32)
    for i in range(rows // BLK):
        largest = jnp.maximum(largest, jnp.max(jnp.abs(load(i)), axis=0, keepdims=True))
    power = exponents(largest)
    inverse = jnp.exp2(-power)
    for i in range(rows // BLK):
        out_ref[pl.ds(i * BLK, BLK), cols] = coded(load(i), inverse)
    held = jnp.broadcast_to(power, (EXTRA, BLK))
    out_ref[pl.ds(rows, EXTRA), cols] = held.astype(jnp.int32).astype(jnp.int16)


def masked_load(place, pattern_ref, x_ref, rows, block_col, col):
    def load(i):
        block_row = place[0] * (rows // BLK) + i
        kept = (pattern_ref[block_row, block_col] == 1) | (place[1] + block_row == place[2] + block_col)
        value = x_ref[0, pl.ds(i * BLK, BLK), col]
        return jnp.where(kept, value, 0.0)

    return load


def encode_partial(partial, pattern, place, rows, first_block, blocks, received=None):
    width = partial.shape[2]

    def kernel(place_ref, pattern_ref, x_ref, *refs):
        out_ref = refs[-1]

        @pl.loop(0, blocks)
        def _(j):
            col_in = pl.ds(pl.multiple_of((j + first_block) * BLK, BLK), BLK)
            col_out = pl.ds(pl.multiple_of(j * BLK, BLK), BLK)
            load = masked_load(place_ref, pattern_ref, x_ref, rows, j + first_block, col_in)
            if received is not None:
                scale = scales(refs[0], rows, col_out)
                own = load
                load = lambda i: own(i) + decoded(refs[0], i * BLK, scale, col_out)
            encode_columns(load, out_ref, rows, col_out)

    if first_block == 0 and blocks * BLK < width:
        width = blocks * BLK
    shape = (rows + EXTRA, blocks * BLK)
    extra = [] if received is None else [received]
    return pl.pallas_call(
        kernel,
        grid_spec=pltpu.PrefetchScalarGridSpec(
            num_scalar_prefetch=2,
            grid=(1,),
            in_specs=[pl.BlockSpec((1, rows, width), lambda g, place_ref, pattern_ref: (0, place_ref[0], 0))]
            + [VMEM_SPEC] * len(extra),
            out_specs=VMEM_SPEC,
        ),
        out_shape=jax.ShapeDtypeStruct(shape, jnp.int16),
        compiler_params=params(),
        cost_estimate=cost(rows * width * 4 + rows * blocks * BLK * 2 * (1 + len(extra))),
    )(place, pattern, partial, *extra)


def merge(first, second):
    rows = first.shape[0] - EXTRA

    def kernel(a_ref, b_ref, out_ref):
        @pl.loop(0, first.shape[1] // BLK)
        def _(j):
            cols = pl.ds(pl.multiple_of(j * BLK, BLK), BLK)
            a_scale = scales(a_ref, rows, cols)
            b_scale = scales(b_ref, rows, cols)
            load = lambda i: decoded(a_ref, i * BLK, a_scale, cols) + decoded(b_ref, i * BLK, b_scale, cols)
            encode_columns(load, out_ref, rows, cols)

    return pl.pallas_call(
        kernel,
        in_specs=[VMEM_SPEC] * 2,
        out_specs=VMEM_SPEC,
        out_shape=jax.ShapeDtypeStruct(first.shape, jnp.int16),
        compiler_params=params(),
        cost_estimate=cost(first.size * 6),
    )(first, second)


def low_total(partial, pattern, place, received):
    _, rows, width = partial.shape

    def kernel(place_ref, pattern_ref, x_ref, code_ref, out_ref):
        @pl.loop(0, width // BLK)
        def _(j):
            cols = pl.ds(pl.multiple_of(j * BLK, BLK), BLK)
            scale = scales(code_ref, rows, cols)
            load = masked_load(place_ref, pattern_ref, x_ref, rows, j, cols)
            for i in range(rows // BLK):
                out_ref[0, pl.ds(i * BLK, BLK), cols] = load(i) + decoded(code_ref, i * BLK, scale, cols)

    return pl.pallas_call(
        kernel,
        in_specs=[SMEM_SPEC, SMEM_SPEC, VMEM_SPEC, VMEM_SPEC],
        out_specs=VMEM_SPEC,
        out_shape=jax.ShapeDtypeStruct(partial.shape, jnp.float32),
        compiler_params=params(),
        cost_estimate=cost(partial.size * 10),
    )(place, pattern, partial, received)


def mid_total(owner, own, received):
    rows, width = own.shape[0] - EXTRA, own.shape[1]

    def kernel(owner_ref, own_ref, got_ref, out_ref):
        def write(code_ref):
            @pl.loop(0, width // BLK)
            def _(j):
                cols = pl.ds(pl.multiple_of(j * BLK, BLK), BLK)
                scale = scales(code_ref, rows, cols)
                for i in range(rows // BLK):
                    out_ref[0, pl.ds(i * BLK, BLK), cols] = decoded(code_ref, i * BLK, scale, cols)

        is_own = pl.program_id(0) == owner_ref[0]
        pl.when(is_own)(lambda: write(own_ref))
        pl.when(jnp.logical_not(is_own))(lambda: write(got_ref))

    return pl.pallas_call(
        kernel,
        grid=(2,),
        in_specs=[SMEM_SPEC, VMEM_SPEC, VMEM_SPEC],
        out_specs=pl.BlockSpec((1, rows, width), lambda g: (0, g, 0)),
        out_shape=jax.ShapeDtypeStruct((1, 2 * rows, width), jnp.float32),
        compiler_params=params(),
        cost_estimate=cost(own.size * 12),
    )(owner, own, received)


def factor(corner):
    order = corner.shape[0]

    def kernel(a_ref, packed_ref, lower_ref, upper_ref, direct, direct_unit, turned, turned_unit):
        lane = lax.broadcasted_iota(jnp.int32, (order, order), 1)
        sub = lax.broadcasted_iota(jnp.int32, (order, order), 0)
        lane_row = lax.broadcasted_iota(jnp.int32, (1, order), 1)
        sub_col = lax.broadcasted_iota(jnp.int32, (order, 1), 0)
        unit = (lane == sub).astype(jnp.float32)
        direct[...] = a_ref[...]
        direct_unit[...] = unit
        turned[...] = a_ref[...].T
        turned_unit[...] = unit

        @pl.loop(0, order - 1)
        def _(k):
            for held, held_unit in ((direct, direct_unit), (turned, turned_unit)):
                left = held[...]
                row_left = held[pl.ds(k, 1), :]
                row_right = held_unit[pl.ds(k, 1), :]
                col = jnp.sum(jnp.where(lane == k, left, 0.0), axis=1, keepdims=True)
                pivot = jnp.sum(jnp.where(lane_row == k, row_left, 0.0), axis=1, keepdims=True)
                below = sub_col > k
                multipliers = jnp.where(below, col / pivot, 0.0)
                fresh = left - multipliers * jnp.where(lane_row > k, row_left, 0.0)
                held[...] = jnp.where((lane == k) & below, multipliers, fresh)
                held_unit[...] = held_unit[...] - multipliers * row_right

        packed_ref[...] = direct[...]
        lower_ref[...] = direct_unit[...]
        pivots = jnp.sum(jnp.where(lane == sub, turned[...], 0.0), axis=1, keepdims=True)
        upper_ref[...] = (turned_unit[...] / pivots).T

    shape = jax.ShapeDtypeStruct((order, order), jnp.float32)
    return pl.pallas_call(
        kernel,
        in_specs=[VMEM_SPEC],
        out_specs=[VMEM_SPEC] * 3,
        out_shape=[shape] * 3,
        scratch_shapes=[pltpu.VMEM((order, order), jnp.float32)] * 4,
        compiler_params=params(),
        cost_estimate=cost(order * order * 16, 2e9),
    )(corner)


def exact_dot(left, right):
    return jnp.dot(left, right, precision=HIGHEST, preferred_element_type=jnp.float32)


def low_dot(left, right):
    return jnp.dot(left, right, preferred_element_type=jnp.float32)


def permuted_codes(order_block, codes, scale):
    codes = codes.astype(jnp.int32)
    high = (codes >> 8).astype(jnp.float32).astype(jnp.bfloat16)
    low = (codes & 255).astype(jnp.float32).astype(jnp.bfloat16)
    return (low_dot(order_block, high) * 256.0 + low_dot(order_block, low)) * scale


def lower_panel(flags, order, own, received, upper_inverse):
    rows = own.shape[0] - EXTRA

    def kernel(flag_ref, order_ref, own_ref, got_ref, inverse_ref, slab_ref, low_ref):
        cols = pl.ds(0, PANEL)
        own_scale = scales(own_ref, rows, cols)
        got_scale = scales(got_ref, rows, cols)
        first_col = flag_ref[3] == 0

        @pl.loop(0, rows // BLK)
        def _(i):
            row = pl.multiple_of(i * BLK, BLK)
            summed = decoded(own_ref, row, own_scale, cols) + decoded(got_ref, row, got_scale, cols)
            summed = exact_dot(order_ref[pl.ds(row, BLK), :].astype(jnp.float32), summed)
            panel = exact_dot(summed, inverse_ref[...])
            low_ref[pl.ds(row, BLK), :] = panel.astype(jnp.bfloat16)
            slab_ref[pl.ds(row, BLK), :] = jnp.where(first_col, panel, summed)

    return pl.pallas_call(
        kernel,
        in_specs=[SMEM_SPEC] + [VMEM_SPEC] * 4,
        out_specs=[VMEM_SPEC] * 2,
        out_shape=[
            jax.ShapeDtypeStruct((rows, PANEL), jnp.float32),
            jax.ShapeDtypeStruct((rows, PANEL), jnp.bfloat16),
        ],
        compiler_params=params(),
        cost_estimate=cost(rows * PANEL * 14, rows * PANEL * PANEL * 24),
    )(flags, order, own, received, upper_inverse)


def upper_panel(flags, order, slab, own, received, lower_inverse):
    rows, rest = own.shape[0] - EXTRA, own.shape[1]
    width = rest + PANEL

    def kernel(flag_ref, order_ref, slab_ref, own_ref, own_scale, got_ref, got_scale, inverse_ref, up_ref, low_ref):
        first = exact_dot(inverse_ref[...], slab_ref[...])
        up_ref[:, :PANEL] = first
        low_ref[:, :PANEL] = first.astype(jnp.bfloat16)

        def write(code_ref, scale_ref):
            scale = jnp.exp2(scale_ref[...].astype(jnp.int32).astype(jnp.float32)[0:1])
            value = permuted_codes(order_ref[...], code_ref[...], scale)
            value = exact_dot(inverse_ref[...], value)
            up_ref[:, PANEL:] = value
            low_ref[:, PANEL:] = value.astype(jnp.bfloat16)

        pl.when(flag_ref[0] == 0)(lambda: write(own_ref, own_scale))
        pl.when(flag_ref[0] == 1)(lambda: write(got_ref, got_scale))

    first_block = lambda g: (0, 0)
    code_spec = pl.BlockSpec((BLK, rest), first_block)
    scale_spec = pl.BlockSpec((EXTRA, rest), lambda g: (rows // EXTRA, 0))
    square = pl.BlockSpec((BLK, BLK), first_block)
    return pl.pallas_call(
        kernel,
        grid=(1,),
        in_specs=[SMEM_SPEC, square, square, code_spec, scale_spec, code_spec, scale_spec, square],
        out_specs=[pl.BlockSpec((BLK, width), first_block)] * 2,
        out_shape=[
            jax.ShapeDtypeStruct((PANEL, width), jnp.float32),
            jax.ShapeDtypeStruct((PANEL, width), jnp.bfloat16),
        ],
        compiler_params=params(),
        cost_estimate=cost(BLK * width * 10, BLK * BLK * width * 16),
    )(flags, order, slab, own, own, received, received, lower_inverse)


def top_total(flags, order, codes, slab, lower_low, upper_low, upper, packed):
    total_rows = slab.shape[0]
    rows, rest = codes[0].shape[0] - EXTRA, codes[0].shape[1]
    width = rest + PANEL
    part_blocks = rows // BLK

    def kernel(flag_ref, order_ref, own_a, got_a, own_b, got_b, slab_ref, low_ref, up_low_ref, up_ref, packed_ref, out_ref):
        i = pl.program_id(0)
        part = i // part_blocks
        row = pl.multiple_of((i % part_blocks) * BLK, BLK)
        first_row = (flag_ref[2] == 0) & (i == 0)
        first_col = flag_ref[3] == 0
        rest_cols = pl.ds(0, rest)

        @pl.when(jnp.logical_not(first_row))
        def _():
            low = low_ref[...]

            def write(code_ref):
                scale = scales(code_ref, rows, rest_cols)
                value = permuted_codes(order_ref[...], code_ref[pl.ds(row, BLK), :], scale)
                out_ref[:, PANEL:] = value - low_dot(low, up_low_ref[:, PANEL:])

            owned_a = part == flag_ref[0]
            owned_b = part == 2 + flag_ref[1]
            pl.when(owned_a)(lambda: write(own_a))
            pl.when((part < 2) & jnp.logical_not(owned_a))(lambda: write(got_a))
            pl.when(owned_b)(lambda: write(own_b))
            pl.when((part >= 2) & jnp.logical_not(owned_b))(lambda: write(got_b))
            product = low_dot(low, up_low_ref[:, :PANEL])
            out_ref[:, :PANEL] = jnp.where(first_col, slab_ref[...], slab_ref[...] - product)

        @pl.when(first_row)
        def _():
            out_ref[:, PANEL:] = up_ref[:, PANEL:]
            out_ref[:, :PANEL] = jnp.where(first_col, packed_ref[...], up_ref[:, :PANEL])

    square = pl.BlockSpec((BLK, BLK), lambda i: (i, 0))
    return pl.pallas_call(
        kernel,
        grid=(total_rows // BLK,),
        in_specs=[SMEM_SPEC, square] + [VMEM_SPEC] * 4 + [square, square] + [VMEM_SPEC] * 3,
        out_specs=pl.BlockSpec((BLK, width), lambda i: (i, 0)),
        out_shape=jax.ShapeDtypeStruct((total_rows, width), jnp.float32),
        compiler_params=params(),
        cost_estimate=cost(total_rows * width * 6, total_rows * width * BLK * 6),
    )(flags, order, *codes, slab, lower_low, upper_low, upper, packed)


def reduced(partial, pattern, first_place, own_place, rows, first_block, blocks, first_bit, bits):
    sent = encode_partial(partial, pattern, first_place, rows, first_block, blocks)
    own = encode_partial(partial, pattern, own_place, rows, first_block, blocks, swapped(sent, first_bit))
    for bit in bits:
        if bit != first_bit:
            own = merge(own, swapped(own, bit))
    return own, swapped(own, first_bit)


def on_device(partial_top, partial_mid, partial_low, pattern_top, pattern_mid, pattern_low, pivots):
    layer, row, col = (lax.axis_index(name) for name in ("layer", "row", "col"))
    bits = range(lax.axis_size("layer").bit_length() - 1)
    low_bit, high_bit = layer & 1, (layer >> 1) & 1
    flags = jnp.stack([low_bit, high_bit, row, col]).astype(jnp.int32)
    order = ((pivots % BLK)[:, None] == jnp.arange(BLK, dtype=jnp.int32)[None, :]).astype(jnp.bfloat16)

    def place(part, pattern):
        first_row, first_col = row * pattern.shape[1], col * pattern.shape[2]
        return jnp.stack([jnp.asarray(part, jnp.int32), first_row, first_col]).astype(jnp.int32)

    corner = exact_dot(order[:BLK].astype(jnp.float32), partial_top[0, :BLK, :BLK])
    for bit in bits:
        corner = corner + swapped(corner, bit)
    corner = broadcast_from_first(broadcast_from_first(corner, "row"), "col")

    mid_rows = partial_mid.shape[1] // 2
    mid_blocks = partial_mid.shape[2] // BLK
    mid_own, mid_got = reduced(
        partial_mid, pattern_mid[0], place(1 - high_bit, pattern_mid), place(high_bit, pattern_mid),
        mid_rows, 0, mid_blocks, 1, bits[:2],
    )

    top_rows = partial_top.shape[1]
    top_blocks = partial_top.shape[2] // BLK
    pattern = pattern_top[0]
    slab_own = encode_partial(partial_top, pattern, place(0, pattern_top), top_rows, 0, 1)
    for bit in bits[:-1]:
        slab_own = merge(slab_own, swapped(slab_own, bit))
    slab_got = swapped(slab_own, bits[-1])

    part_rows = top_rows // 4
    a_own, a_got = reduced(
        partial_top, pattern, place(1 - low_bit, pattern_top), place(low_bit, pattern_top),
        part_rows, 1, top_blocks - 1, 0, bits,
    )
    b_own, b_got = reduced(
        partial_top, pattern, place(3 - high_bit, pattern_top), place(2 + high_bit, pattern_top),
        part_rows, 1, top_blocks - 1, 1, bits,
    )

    low_rows = partial_low.shape[1]
    low_place = place(0, pattern_low)
    low_sent = encode_partial(partial_low, pattern_low[0], low_place, low_rows, 0, partial_low.shape[2] // BLK)
    low_sums = low_total(partial_low, pattern_low[0], low_place, swapped(low_sent, 0))

    packed, lower_inverse, upper_inverse = factor(corner)
    slab, lower_low = lower_panel(flags, order, slab_own, slab_got, upper_inverse)
    lower_low = broadcast_from_first(lower_low, "col")
    upper, upper_low = upper_panel(flags, order, slab, a_own, a_got, lower_inverse)
    upper_low = broadcast_from_first(upper_low, "row")
    top_factor = top_total(flags, order, (a_own, a_got, b_own, b_got), slab, lower_low, upper_low, upper, packed)
    mid_sums = mid_total(high_bit[None].astype(jnp.int32), mid_own, mid_got)
    return top_factor, mid_sums, low_sums


def solution(mesh):
    placed = (
        P("layer", "row", "col"),
        P("layer", "row", "col"),
        P("layer", "row", "col"),
        P("layer", "row", "col"),
        P("layer", "row", "col"),
        P("layer", "row", "col"),
        P("row"),
    )
    return jax.shard_map(
        on_device,
        mesh=mesh,
        in_specs=placed,
        out_specs=(P("row", "col"), P("layer", "row", "col"), P("layer", "row", "col")),
        check_vma=False,
    )
```

```python
import jax
import jax.numpy as jnp
from jax import lax
from jax.experimental import pallas as pl
from jax.experimental.pallas import tpu as pltpu
from jax.sharding import PartitionSpec as P

PANEL = 128
BLK = 128
EXTRA = 16
HIGHEST = lax.Precision.HIGHEST
VMEM_LIMIT = 48 * 1024 * 1024

SMEM_SPEC = pl.BlockSpec(memory_space=pltpu.SMEM)
VMEM_SPEC = pl.BlockSpec(memory_space=pltpu.VMEM)


def swapped(value, bit):
    count = lax.axis_size("layer")
    return lax.ppermute(value, "layer", [(i, i ^ (1 << bit)) for i in range(count)])


def broadcast_from_first(value, axis):
    count = lax.axis_size(axis)
    own = lax.axis_index(axis)
    span = count // 2
    while span >= 1:
        got = lax.ppermute(value, axis, [(i, i + span) for i in range(0, count, 2 * span)])
        value = jnp.where(own % (2 * span) == span, got, value)
        span //= 2
    return value


def exponents(largest):
    return jnp.floor(jnp.log2(jnp.maximum(largest, 1e-30))) - 14.0


def coded(value, inverse):
    scaled = jnp.round(value * inverse)
    scaled = jnp.minimum(jnp.maximum(scaled, -32767.0), 32767.0)
    return scaled.astype(jnp.int32).astype(jnp.int16)


def scales(code_ref, rows, cols):
    held = code_ref[pl.ds(rows, EXTRA), cols].astype(jnp.int32).astype(jnp.float32)
    return jnp.exp2(held[0:1])


def decoded(code_ref, row, scale, cols):
    return code_ref[pl.ds(row, BLK), cols].astype(jnp.int32).astype(jnp.float32) * scale


def run(kernel, after, operands, specs, out_specs, out_shape, nbytes, flops=0, grid=(1,), scalars=(), scratch=(), aliases=None):
    taken = len(scalars) + len(operands)
    after = [] if after is None else [after]

    def body(*refs):
        kernel(*refs[:taken], *refs[taken + len(after):])

    return pl.pallas_call(
        body,
        grid_spec=pltpu.PrefetchScalarGridSpec(
            num_scalar_prefetch=len(scalars),
            grid=grid,
            in_specs=list(specs) + [pl.BlockSpec(memory_space=pl.ANY)] * len(after),
            out_specs=out_specs,
            scratch_shapes=list(scratch),
        ),
        out_shape=out_shape,
        input_output_aliases=aliases or {},
        compiler_params=pltpu.CompilerParams(vmem_limit_bytes=VMEM_LIMIT),
        cost_estimate=pl.CostEstimate(flops=0, bytes_accessed=1024, transcendentals=0),
    )(*scalars, *operands, *after)


def encode_all(load, out_ref, value_ref, scale_ref, rows, blocks):
    @pl.loop(0, blocks)
    def _(j):
        cols = pl.ds(pl.multiple_of(j * BLK, BLK), BLK)
        fetch = load(j)
        largest = jnp.zeros((1, BLK), jnp.float32)
        for i in range(rows // BLK):
            value = fetch(i)
            value_ref[pl.ds(i * BLK, BLK), cols] = value
            largest = jnp.maximum(largest, jnp.max(jnp.abs(value), axis=0, keepdims=True))
        scale_ref[0:1, cols] = largest

    power = exponents(scale_ref[0:1, :])
    scale_ref[0:1, :] = jnp.exp2(-power)
    held = jnp.broadcast_to(power, (EXTRA, blocks * BLK))
    out_ref[pl.ds(rows, EXTRA), :] = held.astype(jnp.int32).astype(jnp.int16)

    @pl.loop(0, blocks)
    def _(j):
        cols = pl.ds(pl.multiple_of(j * BLK, BLK), BLK)
        inverse = scale_ref[0:1, cols]
        for i in range(rows // BLK):
            here = pl.ds(i * BLK, BLK)
            out_ref[here, cols] = coded(value_ref[here, cols], inverse)


def message_scratch(rows, blocks):
    return [pltpu.VMEM((rows, blocks * BLK), jnp.float32), pltpu.VMEM((8, blocks * BLK), jnp.float32)]


def masked_load(place, pattern_ref, x_ref, rows, block_col):
    col = pl.ds(pl.multiple_of(block_col * BLK, BLK), BLK)

    def load(i):
        block_row = place[0] * (rows // BLK) + i
        kept = (pattern_ref[block_row, block_col] == 1) | (place[1] + block_row == place[2] + block_col)
        value = x_ref[0, pl.ds(i * BLK, BLK), col]
        return jnp.where(kept, value, 0.0)

    return load


def encode_partial(after, partial, pattern, place, rows, first_block, blocks, received=None):
    width = partial.shape[2] if first_block > 0 else blocks * BLK
    extra = [] if received is None else [received]

    def kernel(place_ref, pattern_ref, x_ref, *refs):
        out_ref, value_ref, scale_ref = refs[-3:]

        def load(j):
            own = masked_load(place_ref, pattern_ref, x_ref, rows, j + first_block)
            if received is None:
                return own
            cols = pl.ds(pl.multiple_of(j * BLK, BLK), BLK)
            scale = scales(refs[0], rows, cols)
            return lambda i: own(i) + decoded(refs[0], i * BLK, scale, cols)

        encode_all(load, out_ref, value_ref, scale_ref, rows, blocks)

    return run(
        kernel, after, [partial] + extra,
        [pl.BlockSpec((1, rows, width), lambda g, place_ref, pattern_ref: (0, place_ref[0], 0))]
        + [VMEM_SPEC] * len(extra),
        VMEM_SPEC, jax.ShapeDtypeStruct((rows + EXTRA, blocks * BLK), jnp.int16),
        rows * width * 4 + rows * blocks * BLK * 2 * (1 + len(extra)),
        scalars=(place, pattern), scratch=message_scratch(rows, blocks),
    )


def merge(after, first, second):
    rows, blocks = first.shape[0] - EXTRA, first.shape[1] // BLK

    def kernel(a_ref, b_ref, out_ref, value_ref, scale_ref):
        def load(j):
            cols = pl.ds(pl.multiple_of(j * BLK, BLK), BLK)
            a_scale = scales(a_ref, rows, cols)
            b_scale = scales(b_ref, rows, cols)
            return lambda i: decoded(a_ref, i * BLK, a_scale, cols) + decoded(b_ref, i * BLK, b_scale, cols)

        encode_all(load, out_ref, value_ref, scale_ref, rows, blocks)

    return run(
        kernel, after, [first, second], [VMEM_SPEC] * 2, VMEM_SPEC,
        jax.ShapeDtypeStruct(first.shape, jnp.int16), first.size * 6, scratch=message_scratch(rows, blocks),
    )


def low_total(after, partial, pattern, place, received):
    _, total_rows, width = partial.shape
    rows = total_rows // len(received)

    def kernel(place_ref, pattern_ref, x_ref, *refs):
        out_ref = refs[-1]

        @pl.loop(0, width // BLK)
        def _(j):
            cols = pl.ds(pl.multiple_of(j * BLK, BLK), BLK)
            load = masked_load(place_ref, pattern_ref, x_ref, total_rows, j)
            for part, code_ref in enumerate(refs[:-1]):
                scale = scales(code_ref, rows, cols)
                for i in range(rows // BLK):
                    block = part * (rows // BLK) + i
                    out_ref[0, pl.ds(block * BLK, BLK), cols] = load(block) + decoded(code_ref, i * BLK, scale, cols)

    return run(
        kernel, after, [partial, *received], [VMEM_SPEC] * (1 + len(received)), VMEM_SPEC,
        jax.ShapeDtypeStruct(partial.shape, jnp.float32), partial.size * 10, scalars=(place, pattern),
    )


def mid_half(after, owner, code, base=None):
    rows, width = code.shape[0] - EXTRA, code.shape[1]
    extra = [] if base is None else [base]

    def kernel(owner_ref, code_ref, *refs):
        @pl.loop(0, width // BLK)
        def _(j):
            cols = pl.ds(pl.multiple_of(j * BLK, BLK), BLK)
            scale = scales(code_ref, rows, cols)
            for i in range(rows // BLK):
                refs[-1][0, pl.ds(i * BLK, BLK), cols] = decoded(code_ref, i * BLK, scale, cols)

    return run(
        kernel, after, [code] + extra, [VMEM_SPEC] + [pl.BlockSpec(memory_space=pl.ANY)] * len(extra),
        pl.BlockSpec((1, rows, width), lambda g, owner_ref: (0, owner_ref[0], 0)),
        jax.ShapeDtypeStruct((1, 2 * rows, width), jnp.float32), code.size * 6, scalars=(owner,),
        aliases={2: 0} if extra else None,
    )


def factor(after, corner):
    order = corner.shape[0]

    def kernel(a_ref, packed_ref, lower_ref, upper_ref, direct, direct_unit, turned, turned_unit):
        lane = lax.broadcasted_iota(jnp.int32, (order, order), 1)
        sub = lax.broadcasted_iota(jnp.int32, (order, order), 0)
        lane_row = lax.broadcasted_iota(jnp.int32, (1, order), 1)
        sub_col = lax.broadcasted_iota(jnp.int32, (order, 1), 0)
        unit = (lane == sub).astype(jnp.float32)
        direct[...] = a_ref[...]
        direct_unit[...] = unit
        turned[...] = a_ref[...].T
        turned_unit[...] = unit

        @pl.loop(0, order - 1)
        def _(k):
            for held, held_unit in ((direct, direct_unit), (turned, turned_unit)):
                left = held[...]
                row_left = held[pl.ds(k, 1), :]
                row_right = held_unit[pl.ds(k, 1), :]
                col = jnp.sum(jnp.where(lane == k, left, 0.0), axis=1, keepdims=True)
                pivot = jnp.sum(jnp.where(lane_row == k, row_left, 0.0), axis=1, keepdims=True)
                below = sub_col > k
                multipliers = jnp.where(below, col / pivot, 0.0)
                fresh = left - multipliers * jnp.where(lane_row > k, row_left, 0.0)
                held[...] = jnp.where((lane == k) & below, multipliers, fresh)
                held_unit[...] = held_unit[...] - multipliers * row_right

        packed_ref[...] = direct[...]
        lower_ref[...] = direct_unit[...]
        pivots = jnp.sum(jnp.where(lane == sub, turned[...], 0.0), axis=1, keepdims=True)
        upper_ref[...] = (turned_unit[...] / pivots).T

    shape = jax.ShapeDtypeStruct((order, order), jnp.float32)
    return run(
        kernel, after, [corner], [VMEM_SPEC], [VMEM_SPEC] * 3, [shape] * 3, order * order * 16, 2e9,
        scratch=[pltpu.VMEM((order, order), jnp.float32)] * 4,
    )


def exact_dot(left, right):
    return jnp.dot(left, right, precision=HIGHEST, preferred_element_type=jnp.float32)


def low_dot(left, right):
    return jnp.dot(left, right, preferred_element_type=jnp.float32)


def permuted_codes(order_block, codes, scale):
    codes = codes.astype(jnp.int32)
    high = (codes >> 8).astype(jnp.float32).astype(jnp.bfloat16)
    low = (codes & 255).astype(jnp.float32).astype(jnp.bfloat16)
    return (low_dot(order_block, high) * 256.0 + low_dot(order_block, low)) * scale


def lower_panel(after, flags, order, own, received, upper_inverse):
    rows = own.shape[0] - EXTRA

    def kernel(flag_ref, order_ref, own_ref, got_ref, inverse_ref, slab_ref, low_ref):
        cols = pl.ds(0, PANEL)
        own_scale = scales(own_ref, rows, cols)
        got_scale = scales(got_ref, rows, cols)
        first_col = flag_ref[3] == 0

        @pl.loop(0, rows // BLK, unroll=4)
        def _(i):
            here = pl.ds(pl.multiple_of(i * BLK, BLK), BLK)
            order_block = order_ref[here, :]
            slab_ref[here, :] = permuted_codes(order_block, own_ref[here, :], own_scale) + permuted_codes(
                order_block, got_ref[here, :], got_scale
            )

        panel = exact_dot(slab_ref[...], inverse_ref[...])
        low_ref[...] = panel.astype(jnp.bfloat16)

        @pl.when(first_col)
        def _():
            slab_ref[...] = panel

    return run(
        kernel, after, [flags, order, own, received, upper_inverse], [SMEM_SPEC] + [VMEM_SPEC] * 4, [VMEM_SPEC] * 2,
        [jax.ShapeDtypeStruct((rows, PANEL), jnp.float32), jax.ShapeDtypeStruct((rows, PANEL), jnp.bfloat16)],
        rows * PANEL * 14, rows * PANEL * PANEL * 20,
    )


def upper_panel(after, flags, order, slab, own, received, lower_inverse):
    rows, rest = own.shape[0] - EXTRA, own.shape[1]
    width = rest + PANEL

    def kernel(flag_ref, order_ref, slab_ref, own_ref, own_scale, got_ref, got_scale, inverse_ref, up_ref, low_ref):
        first = exact_dot(inverse_ref[...], slab_ref[...])
        up_ref[:, :PANEL] = first
        low_ref[:, :PANEL] = first.astype(jnp.bfloat16)

        def write(code_ref, scale_ref):
            scale = jnp.exp2(scale_ref[...].astype(jnp.int32).astype(jnp.float32)[0:1])
            value = permuted_codes(order_ref[...], code_ref[...], scale)
            value = exact_dot(inverse_ref[...], value)
            up_ref[:, PANEL:] = value
            low_ref[:, PANEL:] = value.astype(jnp.bfloat16)

        pl.when(flag_ref[0] == 0)(lambda: write(own_ref, own_scale))
        pl.when(flag_ref[0] == 1)(lambda: write(got_ref, got_scale))

    first_block = lambda g: (0, 0)
    code_spec = pl.BlockSpec((BLK, rest), first_block)
    scale_spec = pl.BlockSpec((EXTRA, rest), lambda g: (rows // EXTRA, 0))
    square = pl.BlockSpec((BLK, BLK), first_block)
    return run(
        kernel, after, [flags, order, slab, own, own, received, received, lower_inverse],
        [SMEM_SPEC, square, square, code_spec, scale_spec, code_spec, scale_spec, square],
        [pl.BlockSpec((BLK, width), first_block)] * 2,
        [jax.ShapeDtypeStruct((PANEL, width), jnp.float32), jax.ShapeDtypeStruct((PANEL, width), jnp.bfloat16)],
        BLK * width * 10, BLK * BLK * width * 16,
    )


def top_total(after, flags, order, codes, slab, lower_low, upper_low, upper, packed):
    total_rows = slab.shape[0]
    rows, rest = codes[0].shape[0] - EXTRA, codes[0].shape[1]
    width = rest + PANEL
    part_blocks = rows // BLK

    def kernel(flag_ref, order_ref, own_a, got_a, own_b, got_b, slab_ref, low_ref, up_low_ref, up_ref, packed_ref, out_ref):
        i = pl.program_id(0)
        part = i // part_blocks
        row = pl.multiple_of((i % part_blocks) * BLK, BLK)
        first_row = (flag_ref[2] == 0) & (i == 0)
        first_col = flag_ref[3] == 0
        rest_cols = pl.ds(0, rest)

        @pl.when(jnp.logical_not(first_row))
        def _():
            low = low_ref[...]

            def write(code_ref):
                scale = scales(code_ref, rows, rest_cols)
                value = permuted_codes(order_ref[...], code_ref[pl.ds(row, BLK), :], scale)
                out_ref[:, PANEL:] = value - low_dot(low, up_low_ref[:, PANEL:])

            owned_a = part == flag_ref[0]
            owned_b = part == 2 + flag_ref[1]
            pl.when(owned_a)(lambda: write(own_a))
            pl.when((part < 2) & jnp.logical_not(owned_a))(lambda: write(got_a))
            pl.when(owned_b)(lambda: write(own_b))
            pl.when((part >= 2) & jnp.logical_not(owned_b))(lambda: write(got_b))
            product = low_dot(low, up_low_ref[:, :PANEL])
            out_ref[:, :PANEL] = jnp.where(first_col, slab_ref[...], slab_ref[...] - product)

        @pl.when(first_row)
        def _():
            out_ref[:, PANEL:] = up_ref[:, PANEL:]
            out_ref[:, :PANEL] = jnp.where(first_col, packed_ref[...], up_ref[:, :PANEL])

    square = pl.BlockSpec((BLK, BLK), lambda i: (i, 0))
    return run(
        kernel, after, [flags, order, *codes, slab, lower_low, upper_low, upper, packed],
        [SMEM_SPEC, square] + [VMEM_SPEC] * 4 + [square, square] + [VMEM_SPEC] * 3,
        pl.BlockSpec((BLK, width), lambda i: (i, 0)),
        jax.ShapeDtypeStruct((total_rows, width), jnp.float32),
        total_rows * width * 6, total_rows * width * BLK * 6, grid=(total_rows // BLK,),
    )


def on_device(partial_top, partial_mid, partial_low, pattern_top, pattern_mid, pattern_low, pivots):
    layer, row, col = (lax.axis_index(name) for name in ("layer", "row", "col"))
    bits = list(range(lax.axis_size("layer").bit_length() - 1))
    low_bit, high_bit = layer & 1, (layer >> 1) & 1
    flags = jnp.stack([low_bit, high_bit, row, col]).astype(jnp.int32)
    order = ((pivots % BLK)[:, None] == jnp.arange(BLK, dtype=jnp.int32)[None, :]).astype(jnp.bfloat16)

    def sender(partial, pattern, rows, first_block, blocks):
        corner_block = [row * pattern.shape[1], col * pattern.shape[2]]

        def encode(after, part, received=None):
            place = jnp.stack([jnp.asarray(part, jnp.int32), *corner_block]).astype(jnp.int32)
            return encode_partial(after, partial, pattern[0], place, rows, first_block, blocks, received)

        return encode

    def exchanged(after, own, some):
        for bit in some:
            own = after = merge(after, own, swapped(own, bit))
        return own

    top_rows, top_blocks = partial_top.shape[1], partial_top.shape[2] // BLK
    mid_blocks, low_blocks = partial_mid.shape[2] // BLK, partial_low.shape[2] // BLK
    low_rows = partial_low.shape[1]
    encode_mid = sender(partial_mid, pattern_mid, partial_mid.shape[1] // 2, 0, mid_blocks)
    encode_slab = sender(partial_top, pattern_top, top_rows, 0, 1)
    encode_top = sender(partial_top, pattern_top, top_rows // 4, 1, top_blocks - 1)
    encode_low = sender(partial_low, pattern_low, low_rows // 2, 0, low_blocks)

    mid_sent = encode_mid(None, 1 - high_bit)
    mid_got = swapped(mid_sent, 1)
    slab = last = encode_slab(mid_sent, 0)
    slab_got = swapped(slab, 0)

    corner = exact_dot(order[:BLK].astype(jnp.float32), partial_top[0, :BLK, :BLK])
    for bit in bits:
        corner = corner + swapped(corner, bit)
    corner = broadcast_from_first(broadcast_from_first(corner, "row"), "col")

    last = encode_top(last, 1 - low_bit)
    a_got = swapped(last, 0)
    last = encode_top(last, 3 - high_bit)
    b_got = swapped(last, 1)
    slab = last = merge(last, slab, slab_got)
    slab = exchanged(last, slab, bits[1:-1])
    slab_got = swapped(slab, bits[-1])
    mid = last = encode_mid(last, high_bit, mid_got)
    mid_got = swapped(mid, 0)
    a = last = encode_top(last, low_bit, a_got)
    a_got = swapped(a, 1)
    packed, lower_inverse, upper_inverse = factor(last, corner)
    b = last = encode_top(packed, 2 + high_bit, b_got)
    b_got = swapped(b, 0)
    last = low_first = encode_low(last, 0)
    low_first = swapped(low_first, 0)
    panel, lower_low = lower_panel(last, flags, order, slab, slab_got, upper_inverse)
    lower_low = broadcast_from_first(lower_low, "col")
    b = last = merge(panel, b, b_got)
    b = last = exchanged(last, b, bits[2:])
    b_got = swapped(b, 1)
    a = last = merge(last, a, a_got)
    a = last = exchanged(last, a, bits[2:])
    a_got = swapped(a, 0)
    mid = last = merge(last, mid, mid_got)
    mid_got = swapped(mid, 1)
    last = low_second = encode_low(last, 1)
    low_second = swapped(low_second, 0)
    mid_sums = mid_half(last, high_bit[None].astype(jnp.int32), mid)
    upper, upper_low = upper_panel(mid_sums, flags, order, panel, a, a_got, lower_inverse)
    upper_low = broadcast_from_first(upper_low, "row")
    top_factor = top_total(None, flags, order, (a, a_got, b, b_got), panel, lower_low, upper_low, upper, packed)
    low_place = jnp.stack([jnp.int32(0), row * pattern_low.shape[1], col * pattern_low.shape[2]]).astype(jnp.int32)
    low_sums = low_total(top_factor, partial_low, pattern_low[0], low_place, [low_first, low_second])
    mid_sums = mid_half(top_factor, (1 - high_bit)[None].astype(jnp.int32), mid_got, mid_sums)
    return top_factor, mid_sums, low_sums


def solution(mesh):
    placed = (
        P("layer", "row", "col"),
        P("layer", "row", "col"),
        P("layer", "row", "col"),
        P("layer", "row", "col"),
        P("layer", "row", "col"),
        P("layer", "row", "col"),
        P("row"),
    )
    return jax.shard_map(
        on_device,
        mesh=mesh,
        in_specs=placed,
        out_specs=(P("row", "col"), P("layer", "row", "col"), P("layer", "row", "col")),
        check_vma=False,
    )
```

```python
import jax
import jax.numpy as jnp
from jax import lax
from jax.experimental import pallas as pl
from jax.experimental.pallas import tpu as pltpu
from jax.sharding import PartitionSpec as P

PANEL = 128
BLK = 128
EXTRA = 16
HIGHEST = lax.Precision.HIGHEST
VMEM_LIMIT = 48 * 1024 * 1024

SMEM_SPEC = pl.BlockSpec(memory_space=pltpu.SMEM)
VMEM_SPEC = pl.BlockSpec(memory_space=pltpu.VMEM)


def swapped(value, bit):
    count = lax.axis_size("layer")
    pairs = [(i, i ^ (1 << bit)) for i in range(count)]
    return jax.tree.map(lambda piece: lax.ppermute(piece, "layer", pairs), value)


def broadcast_stages(value, axis):
    count = lax.axis_size(axis)
    own = lax.axis_index(axis)
    span = count // 2
    stages = []
    while span >= 1:
        got = lax.ppermute(value, axis, [(i, i + span) for i in range(0, count, 2 * span)])
        takes = own % (2 * span) == span
        value = jnp.where(takes, got, value)
        stages.append(value)
        span //= 2
    return stages


def exponents(largest):
    return jnp.floor(jnp.log2(jnp.maximum(largest, 1e-30))) - 14.0


def coded(value, inverse):
    scaled = jnp.round(value * inverse)
    scaled = jnp.minimum(jnp.maximum(scaled, -32767.0), 32767.0)
    return scaled.astype(jnp.int32).astype(jnp.int16)


def scales(code_ref, rows, cols):
    held = code_ref[pl.ds(rows, EXTRA), cols].astype(jnp.int32).astype(jnp.float32)
    return jnp.exp2(held[0:1])


def decoded(code_ref, row, scale, cols):
    return code_ref[pl.ds(row, BLK), cols].astype(jnp.int32).astype(jnp.float32) * scale


def run(kernel, after, operands, specs, out_specs, out_shape, nbytes, flops=0, grid=(1,), scalars=(), scratch=(), aliases=None):
    taken = len(scalars) + len(operands)

    def body(*refs):
        kernel(*refs[:taken], *refs[taken + len(after):])

    return pl.pallas_call(
        body,
        grid_spec=pltpu.PrefetchScalarGridSpec(
            num_scalar_prefetch=len(scalars),
            grid=grid,
            in_specs=list(specs) + [pl.BlockSpec(memory_space=pl.ANY)] * len(after),
            out_specs=out_specs,
            scratch_shapes=list(scratch),
        ),
        out_shape=out_shape,
        input_output_aliases=aliases or {},
        compiler_params=pltpu.CompilerParams(vmem_limit_bytes=VMEM_LIMIT),
        cost_estimate=pl.CostEstimate(flops=0, bytes_accessed=1024, transcendentals=0),
    )(*scalars, *operands, *after)


def spans(pieces):
    first, result = 0, []
    for piece in pieces:
        blocks = piece.shape[1] // BLK
        result.append((piece, first, blocks))
        first += blocks
    return result


def encode_all(segments, out_refs, value_ref, scale_ref, rows):
    for first, blocks, load in segments:

        @pl.loop(0, blocks)
        def _(j):
            cols = pl.ds(pl.multiple_of((j + first) * BLK, BLK), BLK)
            fetch = load(j)
            largest = jnp.zeros((1, BLK), jnp.float32)
            for i in range(rows // BLK):
                value = fetch(i)
                value_ref[pl.ds(i * BLK, BLK), cols] = value
                largest = jnp.maximum(largest, jnp.max(jnp.abs(value), axis=0, keepdims=True))
            scale_ref[0:1, cols] = largest

    for out_ref, first, blocks in spans(out_refs):
        width = pl.ds(first * BLK, blocks * BLK)
        power = exponents(scale_ref[0:1, width])
        scale_ref[0:1, width] = jnp.exp2(-power)
        held = jnp.broadcast_to(power, (EXTRA, blocks * BLK))
        out_ref[pl.ds(rows, EXTRA), :] = held.astype(jnp.int32).astype(jnp.int16)

        @pl.loop(0, blocks)
        def _(j):
            source = pl.ds(pl.multiple_of((j + first) * BLK, BLK), BLK)
            cols = pl.ds(pl.multiple_of(j * BLK, BLK), BLK)
            inverse = scale_ref[0:1, source]
            for i in range(rows // BLK):
                here = pl.ds(i * BLK, BLK)
                out_ref[here, cols] = coded(value_ref[here, source], inverse)


def message_shapes(rows, blocks, pieces):
    counts = [blocks] if pieces == 1 else [blocks // 2, blocks - blocks // 2]
    return [jax.ShapeDtypeStruct((rows + EXTRA, count * BLK), jnp.int16) for count in counts]


def message_scratch(rows, blocks):
    return [pltpu.VMEM((rows, blocks * BLK), jnp.float32), pltpu.VMEM((8, blocks * BLK), jnp.float32)]


def masked_load(place, pattern_ref, x_ref, rows, block_col):
    col = pl.ds(pl.multiple_of(block_col * BLK, BLK), BLK)

    def load(i):
        block_row = place[0] * (rows // BLK) + i
        kept = (pattern_ref[block_row, block_col] == 1) | (place[1] + block_row == place[2] + block_col)
        value = x_ref[0, pl.ds(i * BLK, BLK), col]
        return jnp.where(kept, value, 0.0)

    return load


def encode_partial(after, partial, pattern, place, rows, first_block, blocks, received=(), pieces=1):
    width = partial.shape[2] if first_block > 0 else blocks * BLK

    def kernel(place_ref, pattern_ref, x_ref, *refs):
        got_refs, out_refs, (value_ref, scale_ref) = refs[:len(received)], refs[len(received):-2], refs[-2:]

        def segment(code_ref, first):
            def load(j):
                own = masked_load(place_ref, pattern_ref, x_ref, rows, j + first + first_block)
                if code_ref is None:
                    return own
                cols = pl.ds(pl.multiple_of(j * BLK, BLK), BLK)
                scale = scales(code_ref, rows, cols)
                return lambda i: own(i) + decoded(code_ref, i * BLK, scale, cols)

            return load

        segments = [(first, count, segment(code_ref, first)) for code_ref, first, count in spans(got_refs)]
        encode_all(segments or [(0, blocks, segment(None, 0))], out_refs, value_ref, scale_ref, rows)

    shapes = message_shapes(rows, blocks, pieces)
    return run(
        kernel, after, [partial, *received],
        [pl.BlockSpec((1, rows, width), lambda g, place_ref, pattern_ref: (0, place_ref[0], 0))]
        + [VMEM_SPEC] * len(received),
        [VMEM_SPEC] * len(shapes), shapes, rows * width * 4 + rows * blocks * BLK * 2 * (1 + len(received)),
        scalars=(place, pattern), scratch=message_scratch(rows, blocks),
    )


def merge(after, first, second):
    rows, blocks = first[0].shape[0] - EXTRA, sum(piece.shape[1] for piece in first) // BLK

    def kernel(*refs):
        count = len(first)
        out_refs, (value_ref, scale_ref) = refs[2 * count:-2], refs[-2:]

        def segment(a_ref, b_ref):
            def load(j):
                cols = pl.ds(pl.multiple_of(j * BLK, BLK), BLK)
                a_scale = scales(a_ref, rows, cols)
                b_scale = scales(b_ref, rows, cols)
                return lambda i: decoded(a_ref, i * BLK, a_scale, cols) + decoded(b_ref, i * BLK, b_scale, cols)

            return load

        segments = [
            (start, blocks, segment(a_ref, b_ref))
            for (a_ref, start, blocks), b_ref in zip(spans(refs[:count]), refs[count:2 * count])
        ]
        encode_all(segments, out_refs, value_ref, scale_ref, rows)

    return run(
        kernel, after, [*first, *second], [VMEM_SPEC] * (2 * len(first)), [VMEM_SPEC] * len(first),
        [jax.ShapeDtypeStruct(piece.shape, jnp.int16) for piece in first],
        rows * blocks * BLK * 6, scratch=message_scratch(rows, blocks),
    )


def low_total(after, partial, pattern, place, received):
    _, rows, width = partial.shape

    def kernel(place_ref, pattern_ref, x_ref, *refs):
        for code_ref, first, blocks in spans(refs[:-1]):

            @pl.loop(0, blocks)
            def _(j):
                cols = pl.ds(pl.multiple_of(j * BLK, BLK), BLK)
                target = pl.ds(pl.multiple_of((j + first) * BLK, BLK), BLK)
                scale = scales(code_ref, rows, cols)
                load = masked_load(place_ref, pattern_ref, x_ref, rows, j + first)
                for i in range(rows // BLK):
                    refs[-1][0, pl.ds(i * BLK, BLK), target] = load(i) + decoded(code_ref, i * BLK, scale, cols)

    return run(
        kernel, after, [partial, *received], [VMEM_SPEC] * (1 + len(received)), VMEM_SPEC,
        jax.ShapeDtypeStruct(partial.shape, jnp.float32), partial.size * 10, scalars=(place, pattern),
    )


def mid_half(after, owner, code, base=None):
    rows, width = code[0].shape[0] - EXTRA, sum(piece.shape[1] for piece in code)
    extra = [] if base is None else [base]

    def kernel(owner_ref, *refs):
        for code_ref, first, blocks in spans(refs[:len(code)]):

            @pl.loop(0, blocks)
            def _(j):
                cols = pl.ds(pl.multiple_of(j * BLK, BLK), BLK)
                target = pl.ds(pl.multiple_of((j + first) * BLK, BLK), BLK)
                scale = scales(code_ref, rows, cols)
                for i in range(rows // BLK):
                    refs[-1][0, pl.ds(i * BLK, BLK), target] = decoded(code_ref, i * BLK, scale, cols)

    return run(
        kernel, after, [*code] + extra,
        [VMEM_SPEC] * len(code) + [pl.BlockSpec(memory_space=pl.ANY)] * len(extra),
        pl.BlockSpec((1, rows, width), lambda g, owner_ref: (0, owner_ref[0], 0)),
        jax.ShapeDtypeStruct((1, 2 * rows, width), jnp.float32), rows * width * 6, scalars=(owner,),
        aliases={1 + len(code): 0} if extra else None,
    )


def factor(after, corner):
    order = corner.shape[0]

    def kernel(a_ref, packed_ref, lower_ref, upper_ref, direct, direct_unit, turned, turned_unit):
        lane = lax.broadcasted_iota(jnp.int32, (order, order), 1)
        sub = lax.broadcasted_iota(jnp.int32, (order, order), 0)
        lane_row = lax.broadcasted_iota(jnp.int32, (1, order), 1)
        sub_col = lax.broadcasted_iota(jnp.int32, (order, 1), 0)
        unit = (lane == sub).astype(jnp.float32)
        direct[...] = a_ref[...]
        direct_unit[...] = unit
        turned[...] = a_ref[...].T
        turned_unit[...] = unit

        @pl.loop(0, order - 1)
        def _(k):
            for held, held_unit in ((direct, direct_unit), (turned, turned_unit)):
                left = held[...]
                row_left = held[pl.ds(k, 1), :]
                row_right = held_unit[pl.ds(k, 1), :]
                col = jnp.sum(jnp.where(lane == k, left, 0.0), axis=1, keepdims=True)
                pivot = jnp.sum(jnp.where(lane_row == k, row_left, 0.0), axis=1, keepdims=True)
                below = sub_col > k
                multipliers = jnp.where(below, col / pivot, 0.0)
                fresh = left - multipliers * jnp.where(lane_row > k, row_left, 0.0)
                held[...] = jnp.where((lane == k) & below, multipliers, fresh)
                held_unit[...] = held_unit[...] - multipliers * row_right

        packed_ref[...] = direct[...]
        lower_ref[...] = direct_unit[...]
        pivots = jnp.sum(jnp.where(lane == sub, turned[...], 0.0), axis=1, keepdims=True)
        upper_ref[...] = (turned_unit[...] / pivots).T

    shape = jax.ShapeDtypeStruct((order, order), jnp.float32)
    return run(
        kernel, after, [corner], [VMEM_SPEC], [VMEM_SPEC] * 3, [shape] * 3, order * order * 16, 2e9,
        scratch=[pltpu.VMEM((order, order), jnp.float32)] * 4,
    )


def exact_dot(left, right):
    return jnp.dot(left, right, precision=HIGHEST, preferred_element_type=jnp.float32)


def low_dot(left, right):
    return jnp.dot(left, right, preferred_element_type=jnp.float32)


def permuted_codes(order_block, codes, scale):
    codes = codes.astype(jnp.int32)
    high = (codes >> 8).astype(jnp.float32).astype(jnp.bfloat16)
    low = (codes & 255).astype(jnp.float32).astype(jnp.bfloat16)
    return (low_dot(order_block, high) * 256.0 + low_dot(order_block, low)) * scale


def lower_panel(after, flags, order, own, received, upper_inverse):
    rows = own.shape[0] - EXTRA

    def kernel(flag_ref, order_ref, own_ref, got_ref, inverse_ref, slab_ref, low_ref):
        cols = pl.ds(0, PANEL)
        own_scale = scales(own_ref, rows, cols)
        got_scale = scales(got_ref, rows, cols)
        first_col = flag_ref[3] == 0

        @pl.loop(0, rows // BLK, unroll=4)
        def _(i):
            here = pl.ds(pl.multiple_of(i * BLK, BLK), BLK)
            order_block = order_ref[here, :]
            slab_ref[here, :] = permuted_codes(order_block, own_ref[here, :], own_scale) + permuted_codes(
                order_block, got_ref[here, :], got_scale
            )

        panel = exact_dot(slab_ref[...], inverse_ref[...])
        low_ref[...] = panel.astype(jnp.bfloat16)

        @pl.when(first_col)
        def _():
            slab_ref[...] = panel

    return run(
        kernel, after, [flags, order, own, received, upper_inverse], [SMEM_SPEC] + [VMEM_SPEC] * 4, [VMEM_SPEC] * 2,
        [jax.ShapeDtypeStruct((rows, PANEL), jnp.float32), jax.ShapeDtypeStruct((rows, PANEL), jnp.bfloat16)],
        rows * PANEL * 14, rows * PANEL * PANEL * 20,
    )


def upper_panel(after, flags, order, slab, own, received, lower_inverse):
    rows, rest = own.shape[0] - EXTRA, own.shape[1]
    width = rest + PANEL

    def kernel(flag_ref, order_ref, slab_ref, own_ref, own_scale, got_ref, got_scale, inverse_ref, up_ref, low_ref):
        first = exact_dot(inverse_ref[...], slab_ref[...])
        up_ref[:, :PANEL] = first
        low_ref[:, :PANEL] = first.astype(jnp.bfloat16)

        def write(code_ref, scale_ref):
            scale = jnp.exp2(scale_ref[...].astype(jnp.int32).astype(jnp.float32)[0:1])
            value = permuted_codes(order_ref[...], code_ref[...], scale)
            value = exact_dot(inverse_ref[...], value)
            up_ref[:, PANEL:] = value
            low_ref[:, PANEL:] = value.astype(jnp.bfloat16)

        pl.when(flag_ref[1] == 0)(lambda: write(own_ref, own_scale))
        pl.when(flag_ref[1] == 1)(lambda: write(got_ref, got_scale))

    first_block = lambda g: (0, 0)
    code_spec = pl.BlockSpec((BLK, rest), first_block)
    scale_spec = pl.BlockSpec((EXTRA, rest), lambda g: (rows // EXTRA, 0))
    square = pl.BlockSpec((BLK, BLK), first_block)
    return run(
        kernel, after, [flags, order, slab, own, own, received, received, lower_inverse],
        [SMEM_SPEC, square, square, code_spec, scale_spec, code_spec, scale_spec, square],
        [pl.BlockSpec((BLK, width), first_block)] * 2,
        [jax.ShapeDtypeStruct((PANEL, width), jnp.float32), jax.ShapeDtypeStruct((PANEL, width), jnp.bfloat16)],
        BLK * width * 10, BLK * BLK * width * 16,
    )


def top_total(after, flags, order, codes, slab, lower_low, upper_low, upper, packed):
    total_rows = slab.shape[0]
    rows, rest = codes[0].shape[0] - EXTRA, codes[0].shape[1]
    width = rest + PANEL
    part_blocks = rows // BLK

    def kernel(flag_ref, order_ref, own_a, got_a, own_b, got_b, slab_ref, low_ref, up_low_ref, up_ref, packed_ref, out_ref):
        i = pl.program_id(0)
        part = i // part_blocks
        row = pl.multiple_of((i % part_blocks) * BLK, BLK)
        first_row = (flag_ref[2] == 0) & (i == 0)
        first_col = flag_ref[3] == 0
        rest_cols = pl.ds(0, rest)

        @pl.when(jnp.logical_not(first_row))
        def _():
            low = low_ref[...]

            def write(code_ref):
                scale = scales(code_ref, rows, rest_cols)
                value = permuted_codes(order_ref[...], code_ref[pl.ds(row, BLK), :], scale)
                out_ref[:, PANEL:] = value - low_dot(low, up_low_ref[:, PANEL:])

            owned_b = part == flag_ref[1]
            owned_a = part == 2 + flag_ref[0]
            pl.when(owned_b)(lambda: write(own_b))
            pl.when((part < 2) & jnp.logical_not(owned_b))(lambda: write(got_b))
            pl.when(owned_a)(lambda: write(own_a))
            pl.when((part >= 2) & jnp.logical_not(owned_a))(lambda: write(got_a))
            product = low_dot(low, up_low_ref[:, :PANEL])
            out_ref[:, :PANEL] = jnp.where(first_col, slab_ref[...], slab_ref[...] - product)

        @pl.when(first_row)
        def _():
            out_ref[:, PANEL:] = up_ref[:, PANEL:]
            out_ref[:, :PANEL] = jnp.where(first_col, packed_ref[...], up_ref[:, :PANEL])

    square = pl.BlockSpec((BLK, BLK), lambda i: (i, 0))
    return run(
        kernel, after, [flags, order, *codes, slab, lower_low, upper_low, upper, packed],
        [SMEM_SPEC, square] + [VMEM_SPEC] * 4 + [square, square] + [VMEM_SPEC] * 3,
        pl.BlockSpec((BLK, width), lambda i: (i, 0)),
        jax.ShapeDtypeStruct((total_rows, width), jnp.float32),
        total_rows * width * 6, total_rows * width * BLK * 6, grid=(total_rows // BLK,),
    )


def on_device(partial_top, partial_mid, partial_low, pattern_top, pattern_mid, pattern_low, pivots):
    layer, row, col = (lax.axis_index(name) for name in ("layer", "row", "col"))
    bits = list(range(lax.axis_size("layer").bit_length() - 1))
    low_bit, high_bit = layer & 1, (layer >> 1) & 1
    flags = jnp.stack([low_bit, high_bit, row, col]).astype(jnp.int32)
    order = ((pivots % BLK)[:, None] == jnp.arange(BLK, dtype=jnp.int32)[None, :]).astype(jnp.bfloat16)

    def sender(partial, pattern, rows, first_block, blocks):
        corner_block = [row * pattern.shape[1], col * pattern.shape[2]]

        def encode(after, part, received=(), pieces=1):
            place = jnp.stack([jnp.asarray(part, jnp.int32), *corner_block]).astype(jnp.int32)
            return encode_partial(after, partial, pattern[0], place, rows, first_block, blocks, received, pieces)

        return encode

    def exchanged(after, own, got, some):
        own = merge(after, own, got)
        for bit in some:
            own = merge([], own, swapped(own, bit))
        return own

    top_rows, top_blocks = partial_top.shape[1], partial_top.shape[2] // BLK
    mid_blocks, low_blocks = partial_mid.shape[2] // BLK, partial_low.shape[2] // BLK
    low_rows = partial_low.shape[1]
    encode_mid = sender(partial_mid, pattern_mid, partial_mid.shape[1] // 2, 0, mid_blocks)
    encode_slab = sender(partial_top, pattern_top, top_rows, 0, 1)
    encode_top = sender(partial_top, pattern_top, top_rows // 4, 1, top_blocks - 1)
    encode_low = sender(partial_low, pattern_low, low_rows, 0, low_blocks)


    corner = exact_dot(order[:BLK].astype(jnp.float32), partial_top[0, :BLK, :BLK])
    count = lax.axis_size("layer")
    beside = [lax.ppermute(corner, "layer", [(i, i ^ apart) for i in range(count)]) for apart in (1, 2, 3)]

    slab = encode_slab([corner], 0)
    slab_got = swapped(slab, 0)
    corner = (corner + beside[0]) + (beside[1] + beside[2])
    for bit in bits[2:]:
        corner = corner + swapped(corner, bit)
    corner_row = broadcast_stages(corner, "row")
    corner_col = broadcast_stages(corner_row[-1], "col")

    mid_sent = encode_mid([*[*slab]], 1 - high_bit, (), 1)
    mid_got = swapped(mid_sent, 1)
    a_sent = encode_top([*mid_sent, corner_row[-1]], 3 - low_bit)
    a_got = swapped(a_sent, 0)
    b_sent = encode_top([*a_sent, corner_col[0]], 1 - high_bit)
    b_got = swapped(b_sent, 1)
    slab = exchanged([*b_sent, corner_col[-1]], slab, slab_got, bits[1:-1])
    slab_got = swapped(slab, bits[-1])
    mid = encode_mid([*slab], high_bit, mid_got, 1)
    mid_got = swapped(mid, 0)
    packed, lower_inverse, upper_inverse = factor([*mid, *a_got], corner_col[-1])
    b = encode_top([*[packed]], high_bit, b_got)
    b_got = swapped(b, 0)
    a = encode_top([*b], 2 + low_bit, a_got)
    a_got = swapped(a, 1)
    panel, lower_low = lower_panel([*a, *mid_got], flags, order, *slab, *slab_got, upper_inverse)
    lower_low = broadcast_stages(lower_low, "col")[-1]
    mid = merge([*[panel]], mid, mid_got)
    mid_got = swapped(mid, 1)
    a = exchanged([*mid], a, a_got, bits[2:])
    a_got = swapped(a, 0)
    b = exchanged([*a], b, b_got, bits[2:])
    b_got = swapped(b, 1)
    mid_sums = mid_half([*b], high_bit[None].astype(jnp.int32), mid)
    low = encode_low([*[mid_sums]], 0, (), 2)
    low_got = swapped(low, 0)
    upper, upper_low = upper_panel([*low], flags, order, panel, *b, *b_got, lower_inverse)
    upper_low = broadcast_stages(upper_low, "row")[-1]
    top_factor = top_total([*[upper]], flags, order, (*a, *a_got, *b, *b_got), panel, lower_low, upper_low, upper, packed)
    low_place = jnp.stack([jnp.int32(0), row * pattern_low.shape[1], col * pattern_low.shape[2]]).astype(jnp.int32)
    low_sums = low_total([*[top_factor]], partial_low, pattern_low[0], low_place, low_got)
    mid_sums = mid_half([top_factor], (1 - high_bit)[None].astype(jnp.int32), mid_got, mid_sums)
    return top_factor, mid_sums, low_sums


def solution(mesh):
    placed = (
        P("layer", "row", "col"),
        P("layer", "row", "col"),
        P("layer", "row", "col"),
        P("layer", "row", "col"),
        P("layer", "row", "col"),
        P("layer", "row", "col"),
        P("row"),
    )
    return jax.shard_map(
        on_device,
        mesh=mesh,
        in_specs=placed,
        out_specs=(P("row", "col"), P("layer", "row", "col"), P("layer", "row", "col")),
        check_vma=False,
    )
```

```python
import jax
import jax.numpy as jnp
from jax import lax
from jax.experimental import pallas as pl
from jax.experimental.pallas import tpu as pltpu
from jax.sharding import PartitionSpec as P

PANEL = 128
BLK = 128
EXTRA = 16
HIGHEST = lax.Precision.HIGHEST
VMEM_LIMIT = 48 * 1024 * 1024

SMEM_SPEC = pl.BlockSpec(memory_space=pltpu.SMEM)
VMEM_SPEC = pl.BlockSpec(memory_space=pltpu.VMEM)


def swapped(value, bit):
    count = lax.axis_size("layer")
    pairs = [(i, i ^ (1 << bit)) for i in range(count)]
    return jax.tree.map(lambda piece: lax.ppermute(piece, "layer", pairs), value)


def broadcast_stages(value, axis):
    count = lax.axis_size(axis)
    own = lax.axis_index(axis)
    span = count // 2
    stages = []
    while span >= 1:
        got = lax.ppermute(value, axis, [(i, i + span) for i in range(0, count, 2 * span)])
        takes = own % (2 * span) == span
        value = jnp.where(takes, got, value)
        stages.append(value)
        span //= 2
    return stages


def exponents(largest):
    return jnp.floor(jnp.log2(jnp.maximum(largest, 1e-30))) - 14.0


def coded(value, inverse):
    scaled = jnp.round(value * inverse)
    scaled = jnp.minimum(jnp.maximum(scaled, -32767.0), 32767.0)
    return scaled.astype(jnp.int32).astype(jnp.int16)


def scales(code_ref, rows, cols):
    held = code_ref[pl.ds(rows, EXTRA), cols].astype(jnp.int32).astype(jnp.float32)
    return jnp.exp2(held[0:1])


def decoded(code_ref, row, scale, cols):
    return code_ref[pl.ds(row, BLK), cols].astype(jnp.int32).astype(jnp.float32) * scale


def run(kernel, after, operands, specs, out_specs, out_shape, nbytes, flops=0, grid=(1,), scalars=(), scratch=(), aliases=None):
    taken = len(scalars) + len(operands)

    def body(*refs):
        kernel(*refs[:taken], *refs[taken + len(after):])

    return pl.pallas_call(
        body,
        grid_spec=pltpu.PrefetchScalarGridSpec(
            num_scalar_prefetch=len(scalars),
            grid=grid,
            in_specs=list(specs) + [pl.BlockSpec(memory_space=pl.ANY)] * len(after),
            out_specs=out_specs,
            scratch_shapes=list(scratch),
        ),
        out_shape=out_shape,
        input_output_aliases=aliases or {},
        compiler_params=pltpu.CompilerParams(vmem_limit_bytes=VMEM_LIMIT),
        cost_estimate=pl.CostEstimate(flops=0, bytes_accessed=1024, transcendentals=0),
    )(*scalars, *operands, *after)


def spans(pieces):
    first, result = 0, []
    for piece in pieces:
        blocks = piece.shape[1] // BLK
        result.append((piece, first, blocks))
        first += blocks
    return result


def encode_all(segments, out_refs, value_ref, scale_ref, rows):
    for first, blocks, load in segments:

        @pl.loop(0, blocks)
        def _(j):
            cols = pl.ds(pl.multiple_of((j + first) * BLK, BLK), BLK)
            fetch = load(j)
            largest = jnp.zeros((1, BLK), jnp.float32)
            for i in range(rows // BLK):
                value = fetch(i)
                value_ref[pl.ds(i * BLK, BLK), cols] = value
                largest = jnp.maximum(largest, jnp.max(jnp.abs(value), axis=0, keepdims=True))
            scale_ref[0:1, cols] = largest

    for out_ref, first, blocks in spans(out_refs):
        width = pl.ds(first * BLK, blocks * BLK)
        power = exponents(scale_ref[0:1, width])
        scale_ref[0:1, width] = jnp.exp2(-power)
        held = jnp.broadcast_to(power, (EXTRA, blocks * BLK))
        out_ref[pl.ds(rows, EXTRA), :] = held.astype(jnp.int32).astype(jnp.int16)

        @pl.loop(0, blocks)
        def _(j):
            source = pl.ds(pl.multiple_of((j + first) * BLK, BLK), BLK)
            cols = pl.ds(pl.multiple_of(j * BLK, BLK), BLK)
            inverse = scale_ref[0:1, source]
            for i in range(rows // BLK):
                here = pl.ds(i * BLK, BLK)
                out_ref[here, cols] = coded(value_ref[here, source], inverse)


def message_shapes(rows, blocks, pieces):
    counts = [blocks] if pieces == 1 else [blocks // 2, blocks - blocks // 2]
    return [jax.ShapeDtypeStruct((rows + EXTRA, count * BLK), jnp.int16) for count in counts]


def message_scratch(rows, blocks):
    return [pltpu.VMEM((rows, blocks * BLK), jnp.float32), pltpu.VMEM((8, blocks * BLK), jnp.float32)]


def masked_load(place, pattern_ref, x_ref, rows, block_col):
    col = pl.ds(pl.multiple_of(block_col * BLK, BLK), BLK)

    def load(i):
        block_row = place[0] * (rows // BLK) + i
        kept = (pattern_ref[block_row, block_col] == 1) | (place[1] + block_row == place[2] + block_col)
        value = x_ref[0, pl.ds(i * BLK, BLK), col]
        return jnp.where(kept, value, 0.0)

    return load


def encode_partial(after, partial, pattern, place, rows, first_block, blocks, received=(), pieces=1):
    width = partial.shape[2] if first_block > 0 else blocks * BLK

    def kernel(place_ref, pattern_ref, x_ref, *refs):
        got_refs, out_refs, (value_ref, scale_ref) = refs[:len(received)], refs[len(received):-2], refs[-2:]

        def segment(code_ref, first):
            def load(j):
                own = masked_load(place_ref, pattern_ref, x_ref, rows, j + first + first_block)
                if code_ref is None:
                    return own
                cols = pl.ds(pl.multiple_of(j * BLK, BLK), BLK)
                scale = scales(code_ref, rows, cols)
                return lambda i: own(i) + decoded(code_ref, i * BLK, scale, cols)

            return load

        segments = [(first, count, segment(code_ref, first)) for code_ref, first, count in spans(got_refs)]
        encode_all(segments or [(0, blocks, segment(None, 0))], out_refs, value_ref, scale_ref, rows)

    shapes = message_shapes(rows, blocks, pieces)
    return run(
        kernel, after, [partial, *received],
        [pl.BlockSpec((1, rows, width), lambda g, place_ref, pattern_ref: (0, place_ref[0], 0))]
        + [VMEM_SPEC] * len(received),
        [VMEM_SPEC] * len(shapes), shapes, rows * width * 4 + rows * blocks * BLK * 2 * (1 + len(received)),
        scalars=(place, pattern), scratch=message_scratch(rows, blocks),
    )


def merge(after, first, second, pieces=1):
    rows, blocks = first[0].shape[0] - EXTRA, sum(piece.shape[1] for piece in first) // BLK

    def kernel(*refs):
        count = len(first)
        out_refs, (value_ref, scale_ref) = refs[2 * count:-2], refs[-2:]

        def segment(a_ref, b_ref):
            def load(j):
                cols = pl.ds(pl.multiple_of(j * BLK, BLK), BLK)
                a_scale = scales(a_ref, rows, cols)
                b_scale = scales(b_ref, rows, cols)
                return lambda i: decoded(a_ref, i * BLK, a_scale, cols) + decoded(b_ref, i * BLK, b_scale, cols)

            return load

        segments = [
            (start, blocks, segment(a_ref, b_ref))
            for (a_ref, start, blocks), b_ref in zip(spans(refs[:count]), refs[count:2 * count])
        ]
        encode_all(segments, out_refs, value_ref, scale_ref, rows)

    shapes = message_shapes(rows, blocks, pieces)
    return run(
        kernel, after, [*first, *second], [VMEM_SPEC] * (2 * len(first)), [VMEM_SPEC] * len(shapes), shapes,
        rows * blocks * BLK * 6, scratch=message_scratch(rows, blocks),
    )


def piece_total(after, part, code, first, base, level=None):
    rows, blocks = code.shape[0] - EXTRA, code.shape[1] // BLK
    partial, pattern, place, shape = level
    inputs, specs = [code], [pl.BlockSpec((rows + EXTRA, BLK), lambda j, *_: (0, j))]
    if partial is not None:
        inputs.append(partial)
        specs.append(pl.BlockSpec((1, rows, BLK), lambda j, *_: (0, 0, first + j)))
    if base is not None:
        inputs.append(base)
        specs.append(pl.BlockSpec(memory_space=pl.ANY))

    def kernel(part_ref, place_ref, pattern_ref, code_ref, *refs):
        out_ref, token_ref = refs[-2:]
        token_ref[...] = jnp.zeros_like(token_ref)
        cols = pl.ds(0, BLK)
        scale = scales(code_ref, rows, cols)
        block_col = first + pl.program_id(0)
        for i in range(rows // BLK):
            here = pl.ds(i * BLK, BLK)
            value = decoded(code_ref, i * BLK, scale, cols)
            if partial is not None:
                kept = (pattern_ref[i, block_col] == 1) | (place_ref[1] + i == place_ref[2] + block_col)
                value = jnp.where(kept, refs[0][0, here, cols], 0.0) + value
            out_ref[0, here, cols] = value

    return run(
        kernel, after, inputs, specs,
        [pl.BlockSpec((1, rows, BLK), lambda j, part_ref, *_: (0, part_ref[0], first + j)),
         pl.BlockSpec((8, BLK), lambda j, *_: (0, 0))],
        [jax.ShapeDtypeStruct(shape, jnp.float32), jax.ShapeDtypeStruct((8, BLK), jnp.float32)],
        rows * blocks * BLK * 6, grid=(blocks,), scalars=(part, place, pattern),
        aliases=None if base is None else {2 + len(inputs): 0},
    )


def corner_rows(after, pivots, partial):
    lines = pivots.reshape(-1, BLK)

    def kernel(pivot_ref, x_ref, out_ref):
        source = pivot_ref[0:1, :] % BLK
        turned = (lax.broadcasted_iota(jnp.int32, (BLK, BLK), 0) == source).astype(jnp.float32)
        out_ref[...] = lax.dot_general(
            turned, x_ref[0], (((0,), (0,)), ((), ())), precision=HIGHEST, preferred_element_type=jnp.float32
        )

    return run(
        kernel, after, [lines, partial],
        [pl.BlockSpec((8, BLK), lambda g: (0, 0)), pl.BlockSpec((1, BLK, BLK), lambda g: (0, 0, 0))],
        pl.BlockSpec((BLK, BLK), lambda g: (0, 0)), jax.ShapeDtypeStruct((BLK, BLK), jnp.float32), BLK * BLK * 8,
    )


def factor(after, corner):
    order = corner.shape[0]

    def kernel(a_ref, packed_ref, lower_ref, upper_ref, direct, direct_unit, turned, turned_unit):
        lane = lax.broadcasted_iota(jnp.int32, (order, order), 1)
        sub = lax.broadcasted_iota(jnp.int32, (order, order), 0)
        lane_row = lax.broadcasted_iota(jnp.int32, (1, order), 1)
        sub_col = lax.broadcasted_iota(jnp.int32, (order, 1), 0)
        unit = (lane == sub).astype(jnp.float32)
        direct[...] = a_ref[...]
        direct_unit[...] = unit
        turned[...] = a_ref[...].T
        turned_unit[...] = unit

        @pl.loop(0, order - 1)
        def _(k):
            for held, held_unit in ((direct, direct_unit), (turned, turned_unit)):
                left = held[...]
                row_left = held[pl.ds(k, 1), :]
                row_right = held_unit[pl.ds(k, 1), :]
                col = jnp.sum(jnp.where(lane == k, left, 0.0), axis=1, keepdims=True)
                pivot = jnp.sum(jnp.where(lane_row == k, row_left, 0.0), axis=1, keepdims=True)
                below = sub_col > k
                multipliers = jnp.where(below, col / pivot, 0.0)
                fresh = left - multipliers * jnp.where(lane_row > k, row_left, 0.0)
                held[...] = jnp.where((lane == k) & below, multipliers, fresh)
                held_unit[...] = held_unit[...] - multipliers * row_right

        packed_ref[...] = direct[...]
        lower_ref[...] = direct_unit[...]
        pivots = jnp.sum(jnp.where(lane == sub, turned[...], 0.0), axis=1, keepdims=True)
        upper_ref[...] = (turned_unit[...] / pivots).T

    shape = jax.ShapeDtypeStruct((order, order), jnp.float32)
    return run(
        kernel, after, [corner], [VMEM_SPEC], [VMEM_SPEC] * 3, [shape] * 3, order * order * 16, 2e9,
        scratch=[pltpu.VMEM((order, order), jnp.float32)] * 4,
    )


def exact_dot(left, right):
    return jnp.dot(left, right, precision=HIGHEST, preferred_element_type=jnp.float32)


def low_dot(left, right):
    return jnp.dot(left, right, preferred_element_type=jnp.float32)


def permuted_codes(order_block, codes, scale):
    codes = codes.astype(jnp.int32)
    high = (codes >> 8).astype(jnp.float32).astype(jnp.bfloat16)
    low = (codes & 255).astype(jnp.float32).astype(jnp.bfloat16)
    return (low_dot(order_block, high) * 256.0 + low_dot(order_block, low)) * scale


def lower_panel(after, flags, order, own, received, upper_inverse):
    rows = own.shape[0] - EXTRA

    def kernel(flag_ref, order_ref, own_ref, got_ref, inverse_ref, slab_ref, low_ref):
        cols = pl.ds(0, PANEL)
        own_scale = scales(own_ref, rows, cols)
        got_scale = scales(got_ref, rows, cols)
        first_col = flag_ref[3] == 0

        @pl.loop(0, rows // BLK, unroll=4)
        def _(i):
            here = pl.ds(pl.multiple_of(i * BLK, BLK), BLK)
            order_block = order_ref[here, :]
            slab_ref[here, :] = permuted_codes(order_block, own_ref[here, :], own_scale) + permuted_codes(
                order_block, got_ref[here, :], got_scale
            )

        panel = exact_dot(slab_ref[...], inverse_ref[...])
        low_ref[...] = panel.astype(jnp.bfloat16)

        @pl.when(first_col)
        def _():
            slab_ref[...] = panel

    return run(
        kernel, after, [flags, order, own, received, upper_inverse], [SMEM_SPEC] + [VMEM_SPEC] * 4, [VMEM_SPEC] * 2,
        [jax.ShapeDtypeStruct((rows, PANEL), jnp.float32), jax.ShapeDtypeStruct((rows, PANEL), jnp.bfloat16)],
        rows * PANEL * 14, rows * PANEL * PANEL * 20,
    )


def upper_panel(after, flags, order, slab, own, received, lower_inverse):
    rows, rest = own.shape[0] - EXTRA, own.shape[1]
    width = rest + PANEL

    def kernel(flag_ref, order_ref, slab_ref, own_ref, own_scale, got_ref, got_scale, inverse_ref, up_ref, low_ref):
        first = exact_dot(inverse_ref[...], slab_ref[...])
        up_ref[:, :PANEL] = first
        low_ref[:, :PANEL] = first.astype(jnp.bfloat16)

        def write(code_ref, scale_ref):
            scale = jnp.exp2(scale_ref[...].astype(jnp.int32).astype(jnp.float32)[0:1])
            value = permuted_codes(order_ref[...], code_ref[...], scale)
            value = exact_dot(inverse_ref[...], value)
            up_ref[:, PANEL:] = value
            low_ref[:, PANEL:] = value.astype(jnp.bfloat16)

        pl.when(flag_ref[1] == 0)(lambda: write(own_ref, own_scale))
        pl.when(flag_ref[1] == 1)(lambda: write(got_ref, got_scale))

    first_block = lambda g: (0, 0)
    code_spec = pl.BlockSpec((BLK, rest), first_block)
    scale_spec = pl.BlockSpec((EXTRA, rest), lambda g: (rows // EXTRA, 0))
    square = pl.BlockSpec((BLK, BLK), first_block)
    return run(
        kernel, after, [flags, order, slab, own, own, received, received, lower_inverse],
        [SMEM_SPEC, square, square, code_spec, scale_spec, code_spec, scale_spec, square],
        [pl.BlockSpec((BLK, width), first_block)] * 2,
        [jax.ShapeDtypeStruct((PANEL, width), jnp.float32), jax.ShapeDtypeStruct((PANEL, width), jnp.bfloat16)],
        BLK * width * 10, BLK * BLK * width * 16,
    )


def top_total(after, flags, order, codes, slab, lower_low, upper_low, upper, packed):
    total_rows = slab.shape[0]
    rows, rest = codes[0].shape[0] - EXTRA, codes[0].shape[1]
    width = rest + PANEL
    part_blocks = rows // BLK

    def kernel(flag_ref, order_ref, own_a, got_a, own_b, got_b, slab_ref, low_ref, up_low_ref, up_ref, packed_ref, out_ref):
        i = pl.program_id(0)
        part = i // part_blocks
        row = pl.multiple_of((i % part_blocks) * BLK, BLK)
        first_row = (flag_ref[2] == 0) & (i == 0)
        first_col = flag_ref[3] == 0
        rest_cols = pl.ds(0, rest)

        @pl.when(jnp.logical_not(first_row))
        def _():
            low = low_ref[...]

            def write(code_ref):
                scale = scales(code_ref, rows, rest_cols)
                value = permuted_codes(order_ref[...], code_ref[pl.ds(row, BLK), :], scale)
                out_ref[:, PANEL:] = value - low_dot(low, up_low_ref[:, PANEL:])

            owned_b = part == flag_ref[1]
            owned_a = part == 2 + flag_ref[0]
            pl.when(owned_b)(lambda: write(own_b))
            pl.when((part < 2) & jnp.logical_not(owned_b))(lambda: write(got_b))
            pl.when(owned_a)(lambda: write(own_a))
            pl.when((part >= 2) & jnp.logical_not(owned_a))(lambda: write(got_a))
            product = low_dot(low, up_low_ref[:, :PANEL])
            out_ref[:, :PANEL] = jnp.where(first_col, slab_ref[...], slab_ref[...] - product)

        @pl.when(first_row)
        def _():
            out_ref[:, PANEL:] = up_ref[:, PANEL:]
            out_ref[:, :PANEL] = jnp.where(first_col, packed_ref[...], up_ref[:, :PANEL])

    square = pl.BlockSpec((BLK, BLK), lambda i: (i, 0))
    return run(
        kernel, after, [flags, order, *codes, slab, lower_low, upper_low, upper, packed],
        [SMEM_SPEC, square] + [VMEM_SPEC] * 4 + [square, square] + [VMEM_SPEC] * 3,
        pl.BlockSpec((BLK, width), lambda i: (i, 0)),
        jax.ShapeDtypeStruct((total_rows, width), jnp.float32),
        total_rows * width * 6, total_rows * width * BLK * 6, grid=(total_rows // BLK,),
    )


def on_device(partial_top, partial_mid, partial_low, pattern_top, pattern_mid, pattern_low, pivots):
    layer, row, col = (lax.axis_index(name) for name in ("layer", "row", "col"))
    bits = list(range(lax.axis_size("layer").bit_length() - 1))
    low_bit, high_bit = layer & 1, (layer >> 1) & 1
    flags = jnp.stack([low_bit, high_bit, row, col]).astype(jnp.int32)
    order = ((pivots % BLK)[:, None] == jnp.arange(BLK, dtype=jnp.int32)[None, :]).astype(jnp.bfloat16)

    def sender(partial, pattern, rows, first_block, blocks):
        corner_block = [row * pattern.shape[1], col * pattern.shape[2]]

        def encode(after, part, received=(), pieces=1):
            place = jnp.stack([jnp.asarray(part, jnp.int32), *corner_block]).astype(jnp.int32)
            return encode_partial(after, partial, pattern[0], place, rows, first_block, blocks, received, pieces)

        return encode

    def exchanged(after, own, got, some):
        own = merge(after, own, got)
        for bit in some:
            own = merge([], own, swapped(own, bit))
        return own

    top_rows, top_blocks = partial_top.shape[1], partial_top.shape[2] // BLK
    mid_blocks, low_blocks = partial_mid.shape[2] // BLK, partial_low.shape[2] // BLK
    low_rows = partial_low.shape[1]
    encode_mid = sender(partial_mid, pattern_mid, partial_mid.shape[1] // 2, 0, mid_blocks)
    encode_slab = sender(partial_top, pattern_top, top_rows, 0, 1)
    encode_top = sender(partial_top, pattern_top, top_rows // 4, 1, top_blocks - 1)
    encode_low = sender(partial_low, pattern_low, low_rows, 0, low_blocks)

    part_of = lambda value: jnp.asarray(value, jnp.int32)[None]
    no_place = jnp.zeros((3,), jnp.int32)
    mid_level = (None, pattern_mid[0], no_place, partial_mid.shape)
    low_place = jnp.stack([jnp.int32(0), row * pattern_low.shape[1], col * pattern_low.shape[2]]).astype(jnp.int32)
    low_level = (partial_low, pattern_low[0], low_place, partial_low.shape)
    count = lax.axis_size("layer")
    slab = encode_slab([], 0)
    slab_got = swapped(slab, 0)
    corner = corner_rows([*slab], pivots, partial_top)
    beside = [lax.ppermute(corner, "layer", [(i, i ^ apart) for i in range(count)]) for apart in (1, 2, 3)]
    corner_own = corner
    corner = (corner + beside[0]) + (beside[1] + beside[2])
    for bit in bits[2:]:
        corner = corner + swapped(corner, bit)
    corner_row = broadcast_stages(corner, "row")
    corner_col = broadcast_stages(corner_row[-1], "col")
    corner_all = corner_col[-1]
    mid_sent = encode_mid([*[corner_own]], 1 - high_bit, (), 1)
    mid_got = swapped(mid_sent, 1)
    a_sent = encode_top([*mid_sent, corner_row[-1], *slab_got], 3 - low_bit)
    a_got = swapped(a_sent, 0)
    b_sent = encode_top([*a_sent, corner_col[0]], 1 - high_bit)
    b_got = swapped(b_sent, 1)
    slab = exchanged([*b_sent, corner_col[-1]], slab, slab_got, bits[1:-1])
    slab_got = swapped(slab, bits[-1])
    mid = encode_mid([*slab, *mid_got], high_bit, mid_got, 1)
    mid_got = swapped(mid, 0)
    packed, lower_inverse, upper_inverse = factor([*mid], corner_all)
    b = encode_top([*[packed]], high_bit, b_got)
    b_got = swapped(b, 0)
    a = encode_top([*b], 2 + low_bit, a_got)
    a_got = swapped(a, 1)
    panel, lower_low = lower_panel([*a, *mid_got], flags, order, *slab, *slab_got, upper_inverse)
    lower_stages = broadcast_stages(lower_low, "col")
    lower_low = lower_stages[-1]
    low = encode_low([*[panel]], 0, (), 2)
    low_got = swapped(low, 0)
    mid = merge([*low], mid, mid_got, 1)
    mid_got = swapped(mid, 1)
    a = exchanged([*mid], a, a_got, bits[2:])
    a_got = swapped(a, 0)
    b = exchanged([*a], b, b_got, bits[2:])
    b_got = swapped(b, 1)
    upper, upper_low = upper_panel([*b, *a_got], flags, order, panel, *b, *b_got, lower_inverse)
    upper_low = broadcast_stages(upper_low, "row")[-1]
    mid_sums, token = piece_total([*[upper]], part_of(high_bit), mid[0], 0, None, mid_level)
    top_factor = top_total([*[token]], flags, order, (*a, *a_got, *b, *b_got), panel, lower_low, upper_low, upper, packed)
    low_sums, token = piece_total([*[top_factor]], part_of(0), low_got[0], 0, None, low_level)
    low_sums, token = piece_total([*[token]], part_of(0), low_got[1], low_got[0].shape[1] // BLK, low_sums, low_level)
    mid_sums, token = piece_total([*[token]], part_of(1 - high_bit), mid_got[0], 0, mid_sums, mid_level)
    return top_factor, mid_sums, low_sums


def solution(mesh):
    placed = (
        P("layer", "row", "col"),
        P("layer", "row", "col"),
        P("layer", "row", "col"),
        P("layer", "row", "col"),
        P("layer", "row", "col"),
        P("layer", "row", "col"),
        P("row"),
    )
    return jax.shard_map(
        on_device,
        mesh=mesh,
        in_specs=placed,
        out_specs=(P("row", "col"), P("layer", "row", "col"), P("layer", "row", "col")),
        check_vma=False,
    )
```

```python
import jax
import jax.numpy as jnp
from jax import lax
from jax.experimental import pallas as pl
from jax.experimental.pallas import tpu as pltpu
from jax.sharding import PartitionSpec as P

PANEL = 128
BLK = 128
EXTRA = 16
HIGHEST = lax.Precision.HIGHEST
VMEM_LIMIT = 48 * 1024 * 1024

SMEM_SPEC = pl.BlockSpec(memory_space=pltpu.SMEM)
VMEM_SPEC = pl.BlockSpec(memory_space=pltpu.VMEM)


def swapped(value, bit):
    count = lax.axis_size("layer")
    pairs = [(i, i ^ (1 << bit)) for i in range(count)]
    return jax.tree.map(lambda piece: lax.ppermute(piece, "layer", pairs), value)


def broadcast_stages(value, axis):
    count = lax.axis_size(axis)
    own = lax.axis_index(axis)
    span = count // 2
    stages = []
    while span >= 1:
        got = lax.ppermute(value, axis, [(i, i + span) for i in range(0, count, 2 * span)])
        takes = own % (2 * span) == span
        value = jnp.where(takes, got, value)
        stages.append(value)
        span //= 2
    return stages


def exponents(largest):
    return jnp.floor(jnp.log2(jnp.maximum(largest, 1e-30))) - 14.0


def coded(value, inverse):
    scaled = jnp.round(value * inverse)
    scaled = jnp.minimum(jnp.maximum(scaled, -32767.0), 32767.0)
    return scaled.astype(jnp.int32).astype(jnp.int16)


def scales(code_ref, rows, cols):
    held = code_ref[pl.ds(rows, EXTRA), cols].astype(jnp.int32).astype(jnp.float32)
    return jnp.exp2(held[0:1])


def decoded(code_ref, row, scale, cols):
    return code_ref[pl.ds(row, BLK), cols].astype(jnp.int32).astype(jnp.float32) * scale


def run(kernel, after, operands, specs, out_specs, out_shape, nbytes, flops=0, grid=(1,), scalars=(), scratch=(), aliases=None):
    taken = len(scalars) + len(operands)

    def body(*refs):
        kernel(*refs[:taken], *refs[taken + len(after):])

    return pl.pallas_call(
        body,
        grid_spec=pltpu.PrefetchScalarGridSpec(
            num_scalar_prefetch=len(scalars),
            grid=grid,
            in_specs=list(specs) + [pl.BlockSpec(memory_space=pl.ANY)] * len(after),
            out_specs=out_specs,
            scratch_shapes=list(scratch),
        ),
        out_shape=out_shape,
        input_output_aliases=aliases or {},
        compiler_params=pltpu.CompilerParams(vmem_limit_bytes=VMEM_LIMIT),
        cost_estimate=pl.CostEstimate(flops=0, bytes_accessed=1024, transcendentals=0),
    )(*scalars, *operands, *after)


def spans(pieces):
    first, result = 0, []
    for piece in pieces:
        blocks = piece.shape[1] // BLK
        result.append((piece, first, blocks))
        first += blocks
    return result


def encode_all(segments, out_refs, value_ref, scale_ref, rows):
    for first, blocks, load in segments:

        @pl.loop(0, blocks)
        def _(j):
            cols = pl.ds(pl.multiple_of((j + first) * BLK, BLK), BLK)
            fetch = load(j)
            largest = jnp.zeros((1, BLK), jnp.float32)
            for i in range(rows // BLK):
                value = fetch(i)
                value_ref[pl.ds(i * BLK, BLK), cols] = value
                largest = jnp.maximum(largest, jnp.max(jnp.abs(value), axis=0, keepdims=True))
            scale_ref[0:1, cols] = largest

    for out_ref, first, blocks in spans(out_refs):
        width = pl.ds(first * BLK, blocks * BLK)
        power = exponents(scale_ref[0:1, width])
        scale_ref[0:1, width] = jnp.exp2(-power)
        held = jnp.broadcast_to(power, (EXTRA, blocks * BLK))
        out_ref[pl.ds(rows, EXTRA), :] = held.astype(jnp.int32).astype(jnp.int16)

        @pl.loop(0, blocks)
        def _(j):
            source = pl.ds(pl.multiple_of((j + first) * BLK, BLK), BLK)
            cols = pl.ds(pl.multiple_of(j * BLK, BLK), BLK)
            inverse = scale_ref[0:1, source]
            for i in range(rows // BLK):
                here = pl.ds(i * BLK, BLK)
                out_ref[here, cols] = coded(value_ref[here, source], inverse)


def message_shapes(rows, blocks, pieces):
    counts = [blocks] if pieces == 1 else [blocks // 2, blocks - blocks // 2]
    return [jax.ShapeDtypeStruct((rows + EXTRA, count * BLK), jnp.int16) for count in counts]


def message_scratch(rows, blocks):
    return [pltpu.VMEM((rows, blocks * BLK), jnp.float32), pltpu.VMEM((8, blocks * BLK), jnp.float32)]


def masked_load(place, pattern_ref, x_ref, rows, block_col):
    col = pl.ds(pl.multiple_of(block_col * BLK, BLK), BLK)

    def load(i):
        block_row = place[0] * (rows // BLK) + i
        kept = (pattern_ref[block_row, block_col] == 1) | (place[1] + block_row == place[2] + block_col)
        value = x_ref[0, pl.ds(i * BLK, BLK), col]
        return jnp.where(kept, value, 0.0)

    return load


def encode_partial(after, partial, pattern, place, rows, first_block, blocks, received=(), pieces=1):
    width = partial.shape[2] if first_block > 0 else blocks * BLK

    def kernel(place_ref, pattern_ref, x_ref, *refs):
        got_refs, out_refs, (value_ref, scale_ref) = refs[:len(received)], refs[len(received):-2], refs[-2:]

        def segment(code_ref, first):
            def load(j):
                own = masked_load(place_ref, pattern_ref, x_ref, rows, j + first + first_block)
                if code_ref is None:
                    return own
                cols = pl.ds(pl.multiple_of(j * BLK, BLK), BLK)
                scale = scales(code_ref, rows, cols)
                return lambda i: own(i) + decoded(code_ref, i * BLK, scale, cols)

            return load

        segments = [(first, count, segment(code_ref, first)) for code_ref, first, count in spans(got_refs)]
        encode_all(segments or [(0, blocks, segment(None, 0))], out_refs, value_ref, scale_ref, rows)

    shapes = message_shapes(rows, blocks, pieces)
    return run(
        kernel, after, [partial, *received],
        [pl.BlockSpec((1, rows, width), lambda g, place_ref, pattern_ref: (0, place_ref[0], 0))]
        + [VMEM_SPEC] * len(received),
        [VMEM_SPEC] * len(shapes), shapes, rows * width * 4 + rows * blocks * BLK * 2 * (1 + len(received)),
        scalars=(place, pattern), scratch=message_scratch(rows, blocks),
    )


def merge(after, first, second, pieces=1):
    rows, blocks = first[0].shape[0] - EXTRA, sum(piece.shape[1] for piece in first) // BLK

    def kernel(*refs):
        count = len(first)
        out_refs, (value_ref, scale_ref) = refs[2 * count:-2], refs[-2:]

        def segment(a_ref, b_ref):
            def load(j):
                cols = pl.ds(pl.multiple_of(j * BLK, BLK), BLK)
                a_scale = scales(a_ref, rows, cols)
                b_scale = scales(b_ref, rows, cols)
                return lambda i: decoded(a_ref, i * BLK, a_scale, cols) + decoded(b_ref, i * BLK, b_scale, cols)

            return load

        segments = [
            (start, blocks, segment(a_ref, b_ref))
            for (a_ref, start, blocks), b_ref in zip(spans(refs[:count]), refs[count:2 * count])
        ]
        encode_all(segments, out_refs, value_ref, scale_ref, rows)

    shapes = message_shapes(rows, blocks, pieces)
    return run(
        kernel, after, [*first, *second], [VMEM_SPEC] * (2 * len(first)), [VMEM_SPEC] * len(shapes), shapes,
        rows * blocks * BLK * 6, scratch=message_scratch(rows, blocks),
    )


def low_total(after, partial, pattern, place, received):
    _, rows, width = partial.shape

    def kernel(place_ref, pattern_ref, x_ref, *refs):
        for code_ref, first, blocks in spans(refs[:-1]):

            @pl.loop(0, blocks)
            def _(j):
                cols = pl.ds(pl.multiple_of(j * BLK, BLK), BLK)
                target = pl.ds(pl.multiple_of((j + first) * BLK, BLK), BLK)
                scale = scales(code_ref, rows, cols)
                load = masked_load(place_ref, pattern_ref, x_ref, rows, j + first)
                for i in range(rows // BLK):
                    refs[-1][0, pl.ds(i * BLK, BLK), target] = load(i) + decoded(code_ref, i * BLK, scale, cols)

    return run(
        kernel, after, [partial, *received], [VMEM_SPEC] * (1 + len(received)), VMEM_SPEC,
        jax.ShapeDtypeStruct(partial.shape, jnp.float32), partial.size * 10, scalars=(place, pattern),
    )


def mid_half(after, owner, code, base=None):
    rows, width = code[0].shape[0] - EXTRA, sum(piece.shape[1] for piece in code)
    extra = [] if base is None else [base]

    def kernel(owner_ref, *refs):
        for code_ref, first, blocks in spans(refs[:len(code)]):

            @pl.loop(0, blocks)
            def _(j):
                cols = pl.ds(pl.multiple_of(j * BLK, BLK), BLK)
                target = pl.ds(pl.multiple_of((j + first) * BLK, BLK), BLK)
                scale = scales(code_ref, rows, cols)
                for i in range(rows // BLK):
                    refs[-1][0, pl.ds(i * BLK, BLK), target] = decoded(code_ref, i * BLK, scale, cols)

    return run(
        kernel, after, [*code] + extra,
        [VMEM_SPEC] * len(code) + [pl.BlockSpec(memory_space=pl.ANY)] * len(extra),
        pl.BlockSpec((1, rows, width), lambda g, owner_ref: (0, owner_ref[0], 0)),
        jax.ShapeDtypeStruct((1, 2 * rows, width), jnp.float32), rows * width * 6, scalars=(owner,),
        aliases={1 + len(code): 0} if extra else None,
    )


def corner_rows(after, pivots, partial):
    lines = pivots.reshape(-1, BLK)

    def kernel(pivot_ref, x_ref, out_ref):
        source = pivot_ref[0:1, :] % BLK
        turned = (lax.broadcasted_iota(jnp.int32, (BLK, BLK), 0) == source).astype(jnp.float32)
        out_ref[...] = lax.dot_general(
            turned, x_ref[0], (((0,), (0,)), ((), ())), precision=HIGHEST, preferred_element_type=jnp.float32
        )

    return run(
        kernel, after, [lines, partial],
        [pl.BlockSpec((8, BLK), lambda g: (0, 0)), pl.BlockSpec((1, BLK, BLK), lambda g: (0, 0, 0))],
        pl.BlockSpec((BLK, BLK), lambda g: (0, 0)), jax.ShapeDtypeStruct((BLK, BLK), jnp.float32), BLK * BLK * 8,
    )


def corner_sum(after, parts):
    def kernel(a_ref, b_ref, c_ref, d_ref, out_ref):
        out_ref[...] = (a_ref[...] + b_ref[...]) + (c_ref[...] + d_ref[...])

    shape = jax.ShapeDtypeStruct((BLK, BLK), jnp.float32)
    return run(kernel, after, parts, [VMEM_SPEC] * 4, VMEM_SPEC, shape, BLK * BLK * 20)


def factor(after, corner):
    order = corner.shape[0]

    def kernel(a_ref, packed_ref, lower_ref, upper_ref, direct, direct_unit, turned, turned_unit):
        lane = lax.broadcasted_iota(jnp.int32, (order, order), 1)
        sub = lax.broadcasted_iota(jnp.int32, (order, order), 0)
        lane_row = lax.broadcasted_iota(jnp.int32, (1, order), 1)
        sub_col = lax.broadcasted_iota(jnp.int32, (order, 1), 0)
        unit = (lane == sub).astype(jnp.float32)
        direct[...] = a_ref[...]
        direct_unit[...] = unit
        turned[...] = a_ref[...].T
        turned_unit[...] = unit

        @pl.loop(0, order - 1)
        def _(k):
            for held, held_unit in ((direct, direct_unit), (turned, turned_unit)):
                left = held[...]
                row_left = held[pl.ds(k, 1), :]
                row_right = held_unit[pl.ds(k, 1), :]
                col = jnp.sum(jnp.where(lane == k, left, 0.0), axis=1, keepdims=True)
                pivot = jnp.sum(jnp.where(lane_row == k, row_left, 0.0), axis=1, keepdims=True)
                below = sub_col > k
                multipliers = jnp.where(below, col / pivot, 0.0)
                fresh = left - multipliers * jnp.where(lane_row > k, row_left, 0.0)
                held[...] = jnp.where((lane == k) & below, multipliers, fresh)
                held_unit[...] = held_unit[...] - multipliers * row_right

        packed_ref[...] = direct[...]
        lower_ref[...] = direct_unit[...]
        pivots = jnp.sum(jnp.where(lane == sub, turned[...], 0.0), axis=1, keepdims=True)
        upper_ref[...] = (turned_unit[...] / pivots).T

    shape = jax.ShapeDtypeStruct((order, order), jnp.float32)
    return run(
        kernel, after, [corner], [VMEM_SPEC], [VMEM_SPEC] * 3, [shape] * 3, order * order * 16, 2e9,
        scratch=[pltpu.VMEM((order, order), jnp.float32)] * 4,
    )


def exact_dot(left, right):
    return jnp.dot(left, right, precision=HIGHEST, preferred_element_type=jnp.float32)


def low_dot(left, right):
    return jnp.dot(left, right, preferred_element_type=jnp.float32)


def permuted_codes(order_block, codes, scale):
    codes = codes.astype(jnp.int32)
    high = (codes >> 8).astype(jnp.float32).astype(jnp.bfloat16)
    low = (codes & 255).astype(jnp.float32).astype(jnp.bfloat16)
    return (low_dot(order_block, high) * 256.0 + low_dot(order_block, low)) * scale


def lower_panel(after, flags, order, own, received, upper_inverse):
    rows = own.shape[0] - EXTRA

    def kernel(flag_ref, order_ref, own_ref, got_ref, inverse_ref, slab_ref, low_ref):
        cols = pl.ds(0, PANEL)
        own_scale = scales(own_ref, rows, cols)
        got_scale = scales(got_ref, rows, cols)
        first_col = flag_ref[3] == 0

        @pl.loop(0, rows // BLK, unroll=4)
        def _(i):
            here = pl.ds(pl.multiple_of(i * BLK, BLK), BLK)
            order_block = order_ref[here, :]
            slab_ref[here, :] = permuted_codes(order_block, own_ref[here, :], own_scale) + permuted_codes(
                order_block, got_ref[here, :], got_scale
            )

        panel = exact_dot(slab_ref[...], inverse_ref[...])
        low_ref[...] = panel.astype(jnp.bfloat16)

        @pl.when(first_col)
        def _():
            slab_ref[...] = panel

    return run(
        kernel, after, [flags, order, own, received, upper_inverse], [SMEM_SPEC] + [VMEM_SPEC] * 4, [VMEM_SPEC] * 2,
        [jax.ShapeDtypeStruct((rows, PANEL), jnp.float32), jax.ShapeDtypeStruct((rows, PANEL), jnp.bfloat16)],
        rows * PANEL * 14, rows * PANEL * PANEL * 20,
    )


def upper_panel(after, flags, order, slab, own, received, lower_inverse):
    rows, rest = own.shape[0] - EXTRA, own.shape[1]
    width = rest + PANEL

    def kernel(flag_ref, order_ref, slab_ref, own_ref, own_scale, got_ref, got_scale, inverse_ref, up_ref, low_ref):
        first = exact_dot(inverse_ref[...], slab_ref[...])
        up_ref[:, :PANEL] = first
        low_ref[:, :PANEL] = first.astype(jnp.bfloat16)

        def write(code_ref, scale_ref):
            scale = jnp.exp2(scale_ref[...].astype(jnp.int32).astype(jnp.float32)[0:1])
            value = permuted_codes(order_ref[...], code_ref[...], scale)
            value = exact_dot(inverse_ref[...], value)
            up_ref[:, PANEL:] = value
            low_ref[:, PANEL:] = value.astype(jnp.bfloat16)

        pl.when(flag_ref[1] == 0)(lambda: write(own_ref, own_scale))
        pl.when(flag_ref[1] == 1)(lambda: write(got_ref, got_scale))

    first_block = lambda g: (0, 0)
    code_spec = pl.BlockSpec((BLK, rest), first_block)
    scale_spec = pl.BlockSpec((EXTRA, rest), lambda g: (rows // EXTRA, 0))
    square = pl.BlockSpec((BLK, BLK), first_block)
    return run(
        kernel, after, [flags, order, slab, own, own, received, received, lower_inverse],
        [SMEM_SPEC, square, square, code_spec, scale_spec, code_spec, scale_spec, square],
        [pl.BlockSpec((BLK, width), first_block)] * 2,
        [jax.ShapeDtypeStruct((PANEL, width), jnp.float32), jax.ShapeDtypeStruct((PANEL, width), jnp.bfloat16)],
        BLK * width * 10, BLK * BLK * width * 16,
    )


def top_total(after, flags, order, codes, slab, lower_low, upper_low, upper, packed):
    total_rows = slab.shape[0]
    rows, rest = codes[0].shape[0] - EXTRA, codes[0].shape[1]
    width = rest + PANEL
    part_blocks = rows // BLK

    def kernel(flag_ref, order_ref, own_a, got_a, own_b, got_b, slab_ref, low_ref, up_low_ref, up_ref, packed_ref, out_ref):
        i = pl.program_id(0)
        part = i // part_blocks
        row = pl.multiple_of((i % part_blocks) * BLK, BLK)
        first_row = (flag_ref[2] == 0) & (i == 0)
        first_col = flag_ref[3] == 0
        rest_cols = pl.ds(0, rest)

        @pl.when(jnp.logical_not(first_row))
        def _():
            low = low_ref[...]

            def write(code_ref):
                scale = scales(code_ref, rows, rest_cols)
                value = permuted_codes(order_ref[...], code_ref[pl.ds(row, BLK), :], scale)
                out_ref[:, PANEL:] = value - low_dot(low, up_low_ref[:, PANEL:])

            owned_b = part == flag_ref[1]
            owned_a = part == 2 + flag_ref[0]
            pl.when(owned_b)(lambda: write(own_b))
            pl.when((part < 2) & jnp.logical_not(owned_b))(lambda: write(got_b))
            pl.when(owned_a)(lambda: write(own_a))
            pl.when((part >= 2) & jnp.logical_not(owned_a))(lambda: write(got_a))
            product = low_dot(low, up_low_ref[:, :PANEL])
            out_ref[:, :PANEL] = jnp.where(first_col, slab_ref[...], slab_ref[...] - product)

        @pl.when(first_row)
        def _():
            out_ref[:, PANEL:] = up_ref[:, PANEL:]
            out_ref[:, :PANEL] = jnp.where(first_col, packed_ref[...], up_ref[:, :PANEL])

    square = pl.BlockSpec((BLK, BLK), lambda i: (i, 0))
    return run(
        kernel, after, [flags, order, *codes, slab, lower_low, upper_low, upper, packed],
        [SMEM_SPEC, square] + [VMEM_SPEC] * 4 + [square, square] + [VMEM_SPEC] * 3,
        pl.BlockSpec((BLK, width), lambda i: (i, 0)),
        jax.ShapeDtypeStruct((total_rows, width), jnp.float32),
        total_rows * width * 6, total_rows * width * BLK * 6, grid=(total_rows // BLK,),
    )


def on_device(partial_top, partial_mid, partial_low, pattern_top, pattern_mid, pattern_low, pivots):
    layer, row, col = (lax.axis_index(name) for name in ("layer", "row", "col"))
    bits = list(range(lax.axis_size("layer").bit_length() - 1))
    low_bit, high_bit = layer & 1, (layer >> 1) & 1
    flags = jnp.stack([low_bit, high_bit, row, col]).astype(jnp.int32)
    order = ((pivots % BLK)[:, None] == jnp.arange(BLK, dtype=jnp.int32)[None, :]).astype(jnp.bfloat16)

    def sender(partial, pattern, rows, first_block, blocks):
        corner_block = [row * pattern.shape[1], col * pattern.shape[2]]

        def encode(after, part, received=(), pieces=1):
            place = jnp.stack([jnp.asarray(part, jnp.int32), *corner_block]).astype(jnp.int32)
            return encode_partial(after, partial, pattern[0], place, rows, first_block, blocks, received, pieces)

        return encode

    def exchanged(after, own, got, some):
        own = merge(after, own, got)
        for bit in some:
            own = merge([], own, swapped(own, bit))
        return own

    top_rows, top_blocks = partial_top.shape[1], partial_top.shape[2] // BLK
    mid_blocks, low_blocks = partial_mid.shape[2] // BLK, partial_low.shape[2] // BLK
    low_rows = partial_low.shape[1]
    encode_mid = sender(partial_mid, pattern_mid, partial_mid.shape[1] // 2, 0, mid_blocks)
    encode_slab = sender(partial_top, pattern_top, top_rows, 0, 1)
    encode_top = sender(partial_top, pattern_top, top_rows // 4, 1, top_blocks - 1)
    encode_low = sender(partial_low, pattern_low, low_rows, 0, low_blocks)

    count = lax.axis_size("layer")
    corner = corner_rows([], pivots, partial_top)
    beside = [lax.ppermute(corner, "layer", [(i, i ^ apart) for i in range(count)]) for apart in (1, 2, 3)]
    slab = encode_slab([*[corner]], 0)
    slab_got = swapped(slab, 0)
    mid_sent = encode_mid([*slab, *beside], 1 - high_bit, (), 1)
    mid_got = swapped(mid_sent, 1)
    a_sent = encode_top([*mid_sent], 3 - low_bit)
    a_got = swapped(a_sent, 0)
    summed = corner_sum([*a_sent], [corner, *beside])
    corner = summed
    for bit in bits[2:]:
        corner = corner + swapped(corner, bit)
    corner_row = broadcast_stages(corner, "row")
    corner_col = broadcast_stages(corner_row[-1], "col")
    corner_all = corner_col[-1]
    b_sent = encode_top([*[summed]], 1 - high_bit)
    b_got = swapped(b_sent, 1)
    slab = exchanged([*b_sent, corner_row[-1]], slab, slab_got, bits[1:-1])
    slab_got = swapped(slab, bits[-1])
    mid = encode_mid([*slab, corner_col[0]], high_bit, mid_got, 2)
    mid_got = swapped(mid, 0)
    packed, lower_inverse, upper_inverse = factor([*mid], corner_all)
    b = encode_top([*[packed]], high_bit, b_got)
    b_got = swapped(b, 0)
    a = encode_top([*b], 2 + low_bit, a_got)
    a_got = swapped(a, 1)
    panel, lower_low = lower_panel([*a, *mid_got], flags, order, *slab, *slab_got, upper_inverse)
    lower_stages = broadcast_stages(lower_low, "col")
    lower_low = lower_stages[-1]
    mid = merge([*[panel]], mid, mid_got, 1)
    mid_got = swapped(mid, 1)
    a = exchanged([*mid], a, a_got, bits[2:])
    a_got = swapped(a, 0)
    b = exchanged([*a], b, b_got, bits[2:])
    b_got = swapped(b, 1)
    mid_sums = mid_half([*b], high_bit[None].astype(jnp.int32), mid)
    low = encode_low([*[mid_sums]], 0, (), 1)
    low_got = swapped(low, 0)
    upper, upper_low = upper_panel([*low, *a_got], flags, order, panel, *b, *b_got, lower_inverse)
    upper_low = broadcast_stages(upper_low, "row")[-1]
    top_factor = top_total([*[upper]], flags, order, (*a, *a_got, *b, *b_got), panel, lower_low, upper_low, upper, packed)
    low_place = jnp.stack([jnp.int32(0), row * pattern_low.shape[1], col * pattern_low.shape[2]]).astype(jnp.int32)
    low_sums = low_total([*[top_factor]], partial_low, pattern_low[0], low_place, low_got)
    mid_sums = mid_half([top_factor], (1 - high_bit)[None].astype(jnp.int32), mid_got, mid_sums)
    return top_factor, mid_sums, low_sums


def solution(mesh):
    placed = (
        P("layer", "row", "col"),
        P("layer", "row", "col"),
        P("layer", "row", "col"),
        P("layer", "row", "col"),
        P("layer", "row", "col"),
        P("layer", "row", "col"),
        P("row"),
    )
    return jax.shard_map(
        on_device,
        mesh=mesh,
        in_specs=placed,
        out_specs=(P("row", "col"), P("layer", "row", "col"), P("layer", "row", "col")),
        check_vma=False,
    )
```

```python
import jax
import jax.numpy as jnp
from jax import lax
from jax.experimental import pallas as pl
from jax.experimental.pallas import tpu as pltpu
from jax.sharding import PartitionSpec as P

PANEL = 128
BLK = 128
EXTRA = 16
HIGHEST = lax.Precision.HIGHEST
VMEM_LIMIT = 48 * 1024 * 1024

SMEM_SPEC = pl.BlockSpec(memory_space=pltpu.SMEM)
VMEM_SPEC = pl.BlockSpec(memory_space=pltpu.VMEM)


def swapped(value, bit):
    count = lax.axis_size("layer")
    pairs = [(i, i ^ (1 << bit)) for i in range(count)]
    return jax.tree.map(lambda piece: lax.ppermute(piece, "layer", pairs), value)


def broadcast_stages(value, axis):
    count = lax.axis_size(axis)
    own = lax.axis_index(axis)
    span = count // 2
    stages = []
    while span >= 1:
        got = lax.ppermute(value, axis, [(i, i + span) for i in range(0, count, 2 * span)])
        takes = own % (2 * span) == span
        value = jnp.where(takes, got, value)
        stages.append(value)
        span //= 2
    return stages


def exponents(largest):
    return jnp.floor(jnp.log2(jnp.maximum(largest, 1e-30))) - 14.0


def coded(value, inverse):
    scaled = jnp.round(value * inverse)
    scaled = jnp.minimum(jnp.maximum(scaled, -32767.0), 32767.0)
    return scaled.astype(jnp.int32).astype(jnp.int16)


def scales(code_ref, rows, cols):
    held = code_ref[pl.ds(rows, EXTRA), cols].astype(jnp.int32).astype(jnp.float32)
    return jnp.exp2(held[0:1])


def decoded(code_ref, row, scale, cols):
    return code_ref[pl.ds(row, BLK), cols].astype(jnp.int32).astype(jnp.float32) * scale


def run(kernel, after, operands, specs, out_specs, out_shape, nbytes, flops=0, grid=(1,), scalars=(), scratch=(), aliases=None):
    taken = len(scalars) + len(operands)

    def body(*refs):
        kernel(*refs[:taken], *refs[taken + len(after):])

    return pl.pallas_call(
        body,
        grid_spec=pltpu.PrefetchScalarGridSpec(
            num_scalar_prefetch=len(scalars),
            grid=grid,
            in_specs=list(specs) + [pl.BlockSpec(memory_space=pl.ANY)] * len(after),
            out_specs=out_specs,
            scratch_shapes=list(scratch),
        ),
        out_shape=out_shape,
        input_output_aliases=aliases or {},
        compiler_params=pltpu.CompilerParams(vmem_limit_bytes=VMEM_LIMIT),
        cost_estimate=pl.CostEstimate(flops=0, bytes_accessed=1024, transcendentals=0),
    )(*scalars, *operands, *after)


def spans(pieces):
    first, result = 0, []
    for piece in pieces:
        blocks = piece.shape[1] // BLK
        result.append((piece, first, blocks))
        first += blocks
    return result


def encode_all(segments, out_refs, value_ref, scale_ref, rows):
    for first, blocks, load in segments:

        @pl.loop(0, blocks)
        def _(j):
            cols = pl.ds(pl.multiple_of((j + first) * BLK, BLK), BLK)
            fetch = load(j)
            largest = jnp.zeros((1, BLK), jnp.float32)
            for i in range(rows // BLK):
                value = fetch(i)
                value_ref[pl.ds(i * BLK, BLK), cols] = value
                largest = jnp.maximum(largest, jnp.max(jnp.abs(value), axis=0, keepdims=True))
            scale_ref[0:1, cols] = largest

    for out_ref, first, blocks in spans(out_refs):
        width = pl.ds(first * BLK, blocks * BLK)
        power = exponents(scale_ref[0:1, width])
        scale_ref[0:1, width] = jnp.exp2(-power)
        held = jnp.broadcast_to(power, (EXTRA, blocks * BLK))
        out_ref[pl.ds(rows, EXTRA), :] = held.astype(jnp.int32).astype(jnp.int16)

        @pl.loop(0, blocks)
        def _(j):
            source = pl.ds(pl.multiple_of((j + first) * BLK, BLK), BLK)
            cols = pl.ds(pl.multiple_of(j * BLK, BLK), BLK)
            inverse = scale_ref[0:1, source]
            for i in range(rows // BLK):
                here = pl.ds(i * BLK, BLK)
                out_ref[here, cols] = coded(value_ref[here, source], inverse)


def message_shapes(rows, blocks, pieces):
    counts = [blocks] if pieces == 1 else [blocks // 2, blocks - blocks // 2]
    return [jax.ShapeDtypeStruct((rows + EXTRA, count * BLK), jnp.int16) for count in counts]


def message_scratch(rows, blocks):
    return [pltpu.VMEM((rows, blocks * BLK), jnp.float32), pltpu.VMEM((8, blocks * BLK), jnp.float32)]


def masked_load(place, pattern_ref, x_ref, rows, block_col):
    col = pl.ds(pl.multiple_of(block_col * BLK, BLK), BLK)

    def load(i):
        block_row = place[0] * (rows // BLK) + i
        kept = (pattern_ref[block_row, block_col] == 1) | (place[1] + block_row == place[2] + block_col)
        value = x_ref[0, pl.ds(i * BLK, BLK), col]
        return jnp.where(kept, value, 0.0)

    return load


def encode_partial(after, partial, pattern, place, rows, first_block, blocks, received=(), pieces=1):
    width = partial.shape[2] if first_block > 0 else blocks * BLK

    def kernel(place_ref, pattern_ref, x_ref, *refs):
        got_refs, out_refs, (value_ref, scale_ref) = refs[:len(received)], refs[len(received):-2], refs[-2:]

        def segment(code_ref, first):
            def load(j):
                own = masked_load(place_ref, pattern_ref, x_ref, rows, j + first + first_block)
                if code_ref is None:
                    return own
                cols = pl.ds(pl.multiple_of(j * BLK, BLK), BLK)
                scale = scales(code_ref, rows, cols)
                return lambda i: own(i) + decoded(code_ref, i * BLK, scale, cols)

            return load

        segments = [(first, count, segment(code_ref, first)) for code_ref, first, count in spans(got_refs)]
        encode_all(segments or [(0, blocks, segment(None, 0))], out_refs, value_ref, scale_ref, rows)

    shapes = message_shapes(rows, blocks, pieces)
    return run(
        kernel, after, [partial, *received],
        [pl.BlockSpec((1, rows, width), lambda g, place_ref, pattern_ref: (0, place_ref[0], 0))]
        + [VMEM_SPEC] * len(received),
        [VMEM_SPEC] * len(shapes), shapes, rows * width * 4 + rows * blocks * BLK * 2 * (1 + len(received)),
        scalars=(place, pattern), scratch=message_scratch(rows, blocks),
    )


def merge(after, first, second, pieces=1):
    rows, blocks = first[0].shape[0] - EXTRA, sum(piece.shape[1] for piece in first) // BLK

    def kernel(*refs):
        count = len(first)
        out_refs, (value_ref, scale_ref) = refs[2 * count:-2], refs[-2:]

        def segment(a_ref, b_ref):
            def load(j):
                cols = pl.ds(pl.multiple_of(j * BLK, BLK), BLK)
                a_scale = scales(a_ref, rows, cols)
                b_scale = scales(b_ref, rows, cols)
                return lambda i: decoded(a_ref, i * BLK, a_scale, cols) + decoded(b_ref, i * BLK, b_scale, cols)

            return load

        segments = [
            (start, blocks, segment(a_ref, b_ref))
            for (a_ref, start, blocks), b_ref in zip(spans(refs[:count]), refs[count:2 * count])
        ]
        encode_all(segments, out_refs, value_ref, scale_ref, rows)

    shapes = message_shapes(rows, blocks, pieces)
    return run(
        kernel, after, [*first, *second], [VMEM_SPEC] * (2 * len(first)), [VMEM_SPEC] * len(shapes), shapes,
        rows * blocks * BLK * 6, scratch=message_scratch(rows, blocks),
    )


def low_total(after, partial, pattern, place, received):
    _, rows, width = partial.shape

    def kernel(place_ref, pattern_ref, x_ref, *refs):
        for code_ref, first, blocks in spans(refs[:-1]):

            @pl.loop(0, blocks)
            def _(j):
                cols = pl.ds(pl.multiple_of(j * BLK, BLK), BLK)
                target = pl.ds(pl.multiple_of((j + first) * BLK, BLK), BLK)
                scale = scales(code_ref, rows, cols)
                load = masked_load(place_ref, pattern_ref, x_ref, rows, j + first)
                for i in range(rows // BLK):
                    refs[-1][0, pl.ds(i * BLK, BLK), target] = load(i) + decoded(code_ref, i * BLK, scale, cols)

    return run(
        kernel, after, [partial, *received], [VMEM_SPEC] * (1 + len(received)), VMEM_SPEC,
        jax.ShapeDtypeStruct(partial.shape, jnp.float32), partial.size * 10, scalars=(place, pattern),
    )


def mid_half(after, owner, code, base=None):
    rows, width = code[0].shape[0] - EXTRA, sum(piece.shape[1] for piece in code)
    extra = [] if base is None else [base]

    def kernel(owner_ref, *refs):
        for code_ref, first, blocks in spans(refs[:len(code)]):

            @pl.loop(0, blocks)
            def _(j):
                cols = pl.ds(pl.multiple_of(j * BLK, BLK), BLK)
                target = pl.ds(pl.multiple_of((j + first) * BLK, BLK), BLK)
                scale = scales(code_ref, rows, cols)
                for i in range(rows // BLK):
                    refs[-1][0, pl.ds(i * BLK, BLK), target] = decoded(code_ref, i * BLK, scale, cols)

    return run(
        kernel, after, [*code] + extra,
        [VMEM_SPEC] * len(code) + [pl.BlockSpec(memory_space=pl.ANY)] * len(extra),
        pl.BlockSpec((1, rows, width), lambda g, owner_ref: (0, owner_ref[0], 0)),
        jax.ShapeDtypeStruct((1, 2 * rows, width), jnp.float32), rows * width * 6, scalars=(owner,),
        aliases={1 + len(code): 0} if extra else None,
    )


def corner_rows(after, pivots, partial):
    lines = pivots.reshape(-1, BLK)

    def kernel(pivot_ref, x_ref, out_ref):
        source = pivot_ref[0:1, :] % BLK
        turned = (lax.broadcasted_iota(jnp.int32, (BLK, BLK), 0) == source).astype(jnp.float32)
        out_ref[...] = lax.dot_general(
            turned, x_ref[0], (((0,), (0,)), ((), ())), precision=HIGHEST, preferred_element_type=jnp.float32
        )

    return run(
        kernel, after, [lines, partial],
        [pl.BlockSpec((8, BLK), lambda g: (0, 0)), pl.BlockSpec((1, BLK, BLK), lambda g: (0, 0, 0))],
        pl.BlockSpec((BLK, BLK), lambda g: (0, 0)), jax.ShapeDtypeStruct((BLK, BLK), jnp.float32), BLK * BLK * 8,
    )


def corner_sum(after, parts):
    def kernel(a_ref, b_ref, c_ref, d_ref, out_ref):
        out_ref[...] = (a_ref[...] + b_ref[...]) + (c_ref[...] + d_ref[...])

    shape = jax.ShapeDtypeStruct((BLK, BLK), jnp.float32)
    return run(kernel, after, parts, [VMEM_SPEC] * 4, VMEM_SPEC, shape, BLK * BLK * 20)


def factor(after, corner):
    order = corner.shape[0]

    def kernel(a_ref, packed_ref, lower_ref, upper_ref, direct, direct_unit, turned, turned_unit):
        lane = lax.broadcasted_iota(jnp.int32, (order, order), 1)
        sub = lax.broadcasted_iota(jnp.int32, (order, order), 0)
        lane_row = lax.broadcasted_iota(jnp.int32, (1, order), 1)
        sub_col = lax.broadcasted_iota(jnp.int32, (order, 1), 0)
        unit = (lane == sub).astype(jnp.float32)
        direct[...] = a_ref[...]
        direct_unit[...] = unit
        turned[...] = a_ref[...].T
        turned_unit[...] = unit

        @pl.loop(0, order - 1)
        def _(k):
            for held, held_unit in ((direct, direct_unit), (turned, turned_unit)):
                left = held[...]
                row_left = held[pl.ds(k, 1), :]
                row_right = held_unit[pl.ds(k, 1), :]
                col = jnp.sum(jnp.where(lane == k, left, 0.0), axis=1, keepdims=True)
                pivot = jnp.sum(jnp.where(lane_row == k, row_left, 0.0), axis=1, keepdims=True)
                below = sub_col > k
                multipliers = jnp.where(below, col / pivot, 0.0)
                fresh = left - multipliers * jnp.where(lane_row > k, row_left, 0.0)
                held[...] = jnp.where((lane == k) & below, multipliers, fresh)
                held_unit[...] = held_unit[...] - multipliers * row_right

        packed_ref[...] = direct[...]
        lower_ref[...] = direct_unit[...]
        pivots = jnp.sum(jnp.where(lane == sub, turned[...], 0.0), axis=1, keepdims=True)
        upper_ref[...] = (turned_unit[...] / pivots).T

    shape = jax.ShapeDtypeStruct((order, order), jnp.float32)
    return run(
        kernel, after, [corner], [VMEM_SPEC], [VMEM_SPEC] * 3, [shape] * 3, order * order * 16, 2e9,
        scratch=[pltpu.VMEM((order, order), jnp.float32)] * 4,
    )


def exact_dot(left, right):
    return jnp.dot(left, right, precision=HIGHEST, preferred_element_type=jnp.float32)


def low_dot(left, right):
    return jnp.dot(left, right, preferred_element_type=jnp.float32)


def permuted_codes(order_block, codes, scale):
    codes = codes.astype(jnp.int32)
    high = (codes >> 8).astype(jnp.float32).astype(jnp.bfloat16)
    low = (codes & 255).astype(jnp.float32).astype(jnp.bfloat16)
    return (low_dot(order_block, high) * 256.0 + low_dot(order_block, low)) * scale


def lower_panel(after, flags, order, own, received, upper_inverse):
    rows = own.shape[0] - EXTRA

    def kernel(flag_ref, order_ref, own_ref, got_ref, inverse_ref, slab_ref, low_ref):
        cols = pl.ds(0, PANEL)
        own_scale = scales(own_ref, rows, cols)
        got_scale = scales(got_ref, rows, cols)
        first_col = flag_ref[3] == 0

        @pl.loop(0, rows // BLK, unroll=4)
        def _(i):
            here = pl.ds(pl.multiple_of(i * BLK, BLK), BLK)
            order_block = order_ref[here, :]
            slab_ref[here, :] = permuted_codes(order_block, own_ref[here, :], own_scale) + permuted_codes(
                order_block, got_ref[here, :], got_scale
            )

        panel = exact_dot(slab_ref[...], inverse_ref[...])
        low_ref[...] = panel.astype(jnp.bfloat16)

        @pl.when(first_col)
        def _():
            slab_ref[...] = panel

    return run(
        kernel, after, [flags, order, own, received, upper_inverse], [SMEM_SPEC] + [VMEM_SPEC] * 4, [VMEM_SPEC] * 2,
        [jax.ShapeDtypeStruct((rows, PANEL), jnp.float32), jax.ShapeDtypeStruct((rows, PANEL), jnp.bfloat16)],
        rows * PANEL * 14, rows * PANEL * PANEL * 20,
    )


def upper_panel(after, flags, order, slab, own, received, lower_inverse):
    rows, rest = own.shape[0] - EXTRA, own.shape[1]
    width = rest + PANEL

    def kernel(flag_ref, order_ref, slab_ref, own_ref, own_scale, got_ref, got_scale, inverse_ref, up_ref, low_ref):
        first = exact_dot(inverse_ref[...], slab_ref[...])
        up_ref[:, :PANEL] = first
        low_ref[:, :PANEL] = first.astype(jnp.bfloat16)

        def write(code_ref, scale_ref):
            scale = jnp.exp2(scale_ref[...].astype(jnp.int32).astype(jnp.float32)[0:1])
            value = permuted_codes(order_ref[...], code_ref[...], scale)
            value = exact_dot(inverse_ref[...], value)
            up_ref[:, PANEL:] = value
            low_ref[:, PANEL:] = value.astype(jnp.bfloat16)

        pl.when(flag_ref[1] == 0)(lambda: write(own_ref, own_scale))
        pl.when(flag_ref[1] == 1)(lambda: write(got_ref, got_scale))

    first_block = lambda g: (0, 0)
    code_spec = pl.BlockSpec((BLK, rest), first_block)
    scale_spec = pl.BlockSpec((EXTRA, rest), lambda g: (rows // EXTRA, 0))
    square = pl.BlockSpec((BLK, BLK), first_block)
    return run(
        kernel, after, [flags, order, slab, own, own, received, received, lower_inverse],
        [SMEM_SPEC, square, square, code_spec, scale_spec, code_spec, scale_spec, square],
        [pl.BlockSpec((BLK, width), first_block)] * 2,
        [jax.ShapeDtypeStruct((PANEL, width), jnp.float32), jax.ShapeDtypeStruct((PANEL, width), jnp.bfloat16)],
        BLK * width * 10, BLK * BLK * width * 16,
    )


def top_total(after, flags, order, codes, slab, lower_low, upper_low, upper, packed):
    total_rows = slab.shape[0]
    rows, rest = codes[0].shape[0] - EXTRA, codes[0].shape[1]
    width = rest + PANEL
    part_blocks = rows // BLK

    def kernel(flag_ref, order_ref, own_a, got_a, own_b, got_b, slab_ref, low_ref, up_low_ref, up_ref, packed_ref, out_ref):
        i = pl.program_id(0)
        part = i // part_blocks
        row = pl.multiple_of((i % part_blocks) * BLK, BLK)
        first_row = (flag_ref[2] == 0) & (i == 0)
        first_col = flag_ref[3] == 0
        rest_cols = pl.ds(0, rest)

        @pl.when(jnp.logical_not(first_row))
        def _():
            low = low_ref[...]

            def write(code_ref):
                scale = scales(code_ref, rows, rest_cols)
                value = permuted_codes(order_ref[...], code_ref[pl.ds(row, BLK), :], scale)
                out_ref[:, PANEL:] = value - low_dot(low, up_low_ref[:, PANEL:])

            owned_b = part == flag_ref[1]
            owned_a = part == 2 + flag_ref[0]
            pl.when(owned_b)(lambda: write(own_b))
            pl.when((part < 2) & jnp.logical_not(owned_b))(lambda: write(got_b))
            pl.when(owned_a)(lambda: write(own_a))
            pl.when((part >= 2) & jnp.logical_not(owned_a))(lambda: write(got_a))
            product = low_dot(low, up_low_ref[:, :PANEL])
            out_ref[:, :PANEL] = jnp.where(first_col, slab_ref[...], slab_ref[...] - product)

        @pl.when(first_row)
        def _():
            out_ref[:, PANEL:] = up_ref[:, PANEL:]
            out_ref[:, :PANEL] = jnp.where(first_col, packed_ref[...], up_ref[:, :PANEL])

    square = pl.BlockSpec((BLK, BLK), lambda i: (i, 0))
    return run(
        kernel, after, [flags, order, *codes, slab, lower_low, upper_low, upper, packed],
        [SMEM_SPEC, square] + [VMEM_SPEC] * 4 + [square, square] + [VMEM_SPEC] * 3,
        pl.BlockSpec((BLK, width), lambda i: (i, 0)),
        jax.ShapeDtypeStruct((total_rows, width), jnp.float32),
        total_rows * width * 6, total_rows * width * BLK * 6, grid=(total_rows // BLK,),
    )


def on_device(partial_top, partial_mid, partial_low, pattern_top, pattern_mid, pattern_low, pivots):
    layer, row, col = (lax.axis_index(name) for name in ("layer", "row", "col"))
    bits = list(range(lax.axis_size("layer").bit_length() - 1))
    low_bit, high_bit = layer & 1, (layer >> 1) & 1
    flags = jnp.stack([low_bit, high_bit, row, col]).astype(jnp.int32)
    order = ((pivots % BLK)[:, None] == jnp.arange(BLK, dtype=jnp.int32)[None, :]).astype(jnp.bfloat16)

    def sender(partial, pattern, rows, first_block, blocks):
        corner_block = [row * pattern.shape[1], col * pattern.shape[2]]

        def encode(after, part, received=(), pieces=1):
            place = jnp.stack([jnp.asarray(part, jnp.int32), *corner_block]).astype(jnp.int32)
            return encode_partial(after, partial, pattern[0], place, rows, first_block, blocks, received, pieces)

        return encode

    def exchanged(after, own, got, some):
        own = merge(after, own, got)
        for bit in some:
            own = merge([], own, swapped(own, bit))
        return own

    top_rows, top_blocks = partial_top.shape[1], partial_top.shape[2] // BLK
    mid_blocks, low_blocks = partial_mid.shape[2] // BLK, partial_low.shape[2] // BLK
    low_rows = partial_low.shape[1]
    encode_mid = sender(partial_mid, pattern_mid, partial_mid.shape[1] // 2, 0, mid_blocks)
    encode_slab = sender(partial_top, pattern_top, top_rows, 0, 1)
    encode_top = sender(partial_top, pattern_top, top_rows // 4, 1, top_blocks - 1)
    encode_low = sender(partial_low, pattern_low, low_rows, 0, low_blocks)

    count = lax.axis_size("layer")
    corner = corner_rows([], pivots, partial_top)
    beside = [lax.ppermute(corner, "layer", [(i, i ^ apart) for i in range(count)]) for apart in (1, 2, 3)]
    slab = encode_slab([*[corner]], 0)
    slab_got = swapped(slab, 0)
    mid_sent = encode_mid([*slab, *beside], 1 - high_bit, (), 1)
    mid_got = swapped(mid_sent, 1)
    a_sent = encode_top([*mid_sent], 3 - low_bit)
    a_got = swapped(a_sent, 0)
    summed = corner_sum([*a_sent], [corner, *beside])
    corner = summed
    for bit in bits[2:]:
        corner = corner + swapped(corner, bit)
    corner_row = broadcast_stages(corner, "row")
    corner_col = broadcast_stages(corner_row[-1], "col")
    corner_all = corner_col[-1]
    b_sent = encode_top([*[summed]], 1 - high_bit)
    b_got = swapped(b_sent, 1)
    slab = exchanged([*b_sent, corner_row[-1]], slab, slab_got, bits[1:-1])
    slab_got = swapped(slab, bits[-1])
    mid = encode_mid([*slab, corner_col[0]], high_bit, mid_got, 2)
    mid_got = swapped(mid, 0)
    packed, lower_inverse, upper_inverse = factor([*mid], corner_all)
    b = encode_top([*[packed]], high_bit, b_got)
    b_got = swapped(b, 0)
    a = encode_top([*b], 2 + low_bit, a_got)
    a_got = swapped(a, 1)
    panel, lower_low = lower_panel([*a, *mid_got], flags, order, *slab, *slab_got, upper_inverse)
    lower_stages = broadcast_stages(lower_low, "col")
    lower_low = lower_stages[-1]
    mid = merge([*[panel]], mid, mid_got, 1)
    mid_got = swapped(mid, 1)
    b = exchanged([*mid], b, b_got, bits[2:])
    b_got = swapped(b, 1)
    a = exchanged([*b], a, a_got, bits[2:])
    a_got = swapped(a, 0)
    mid_sums = mid_half([*a], high_bit[None].astype(jnp.int32), mid)
    low = encode_low([*[mid_sums]], 0, (), 1)
    low_got = swapped(low, 0)
    upper, upper_low = upper_panel([*low, *a_got], flags, order, panel, *b, *b_got, lower_inverse)
    upper_low = broadcast_stages(upper_low, "row")[-1]
    top_factor = top_total([*[upper]], flags, order, (*a, *a_got, *b, *b_got), panel, lower_low, upper_low, upper, packed)
    low_place = jnp.stack([jnp.int32(0), row * pattern_low.shape[1], col * pattern_low.shape[2]]).astype(jnp.int32)
    low_sums = low_total([*[top_factor]], partial_low, pattern_low[0], low_place, low_got)
    mid_sums = mid_half([top_factor], (1 - high_bit)[None].astype(jnp.int32), mid_got, mid_sums)
    return top_factor, mid_sums, low_sums


def solution(mesh):
    placed = (
        P("layer", "row", "col"),
        P("layer", "row", "col"),
        P("layer", "row", "col"),
        P("layer", "row", "col"),
        P("layer", "row", "col"),
        P("layer", "row", "col"),
        P("row"),
    )
    return jax.shard_map(
        on_device,
        mesh=mesh,
        in_specs=placed,
        out_specs=(P("row", "col"), P("layer", "row", "col"), P("layer", "row", "col")),
        check_vma=False,
    )
```

```python
import jax
import jax.numpy as jnp
from jax import lax
from jax.experimental import pallas as pl
from jax.experimental.pallas import tpu as pltpu
from jax.sharding import PartitionSpec as P

PANEL = 128
BLK = 128
EXTRA = 16
HIGHEST = lax.Precision.HIGHEST
VMEM_LIMIT = 48 * 1024 * 1024

SMEM_SPEC = pl.BlockSpec(memory_space=pltpu.SMEM)
VMEM_SPEC = pl.BlockSpec(memory_space=pltpu.VMEM)


def swapped(value, bit):
    count = lax.axis_size("layer")
    pairs = [(i, i ^ (1 << bit)) for i in range(count)]
    return jax.tree.map(lambda piece: lax.ppermute(piece, "layer", pairs), value)


def broadcast_stages(value, axis):
    count = lax.axis_size(axis)
    own = lax.axis_index(axis)
    span = count // 2
    stages = []
    while span >= 1:
        got = lax.ppermute(value, axis, [(i, i + span) for i in range(0, count, 2 * span)])
        takes = own % (2 * span) == span
        value = jnp.where(takes, got, value)
        stages.append(value)
        span //= 2
    return stages


def exponents(largest):
    return jnp.floor(jnp.log2(jnp.maximum(largest, 1e-30))) - 14.0


def coded(value, inverse):
    scaled = jnp.round(value * inverse)
    scaled = jnp.minimum(jnp.maximum(scaled, -32767.0), 32767.0)
    return scaled.astype(jnp.int32).astype(jnp.int16)


def scales(code_ref, rows, cols):
    held = code_ref[pl.ds(rows, EXTRA), cols].astype(jnp.int32).astype(jnp.float32)
    return jnp.exp2(held[0:1])


def decoded(code_ref, row, scale, cols):
    return code_ref[pl.ds(row, BLK), cols].astype(jnp.int32).astype(jnp.float32) * scale


def run(kernel, after, operands, specs, out_specs, out_shape, nbytes, flops=0, grid=(1,), scalars=(), scratch=(), aliases=None):
    taken = len(scalars) + len(operands)

    def body(*refs):
        kernel(*refs[:taken], *refs[taken + len(after):])

    return pl.pallas_call(
        body,
        grid_spec=pltpu.PrefetchScalarGridSpec(
            num_scalar_prefetch=len(scalars),
            grid=grid,
            in_specs=list(specs) + [pl.BlockSpec(memory_space=pl.ANY)] * len(after),
            out_specs=out_specs,
            scratch_shapes=list(scratch),
        ),
        out_shape=out_shape,
        input_output_aliases=aliases or {},
        compiler_params=pltpu.CompilerParams(vmem_limit_bytes=VMEM_LIMIT),
        cost_estimate=pl.CostEstimate(flops=0, bytes_accessed=1024, transcendentals=0),
    )(*scalars, *operands, *after)


def spans(pieces):
    first, result = 0, []
    for piece in pieces:
        blocks = piece.shape[1] // BLK
        result.append((piece, first, blocks))
        first += blocks
    return result


def encode_all(segments, out_refs, value_ref, scale_ref, rows):
    for first, blocks, load in segments:

        @pl.loop(0, blocks)
        def _(j):
            cols = pl.ds(pl.multiple_of((j + first) * BLK, BLK), BLK)
            fetch = load(j)
            largest = jnp.zeros((1, BLK), jnp.float32)
            for i in range(rows // BLK):
                value = fetch(i)
                value_ref[pl.ds(i * BLK, BLK), cols] = value
                largest = jnp.maximum(largest, jnp.max(jnp.abs(value), axis=0, keepdims=True))
            scale_ref[0:1, cols] = largest

    for out_ref, first, blocks in spans(out_refs):
        width = pl.ds(first * BLK, blocks * BLK)
        power = exponents(scale_ref[0:1, width])
        scale_ref[0:1, width] = jnp.exp2(-power)
        held = jnp.broadcast_to(power, (EXTRA, blocks * BLK))
        out_ref[pl.ds(rows, EXTRA), :] = held.astype(jnp.int32).astype(jnp.int16)

        @pl.loop(0, blocks)
        def _(j):
            source = pl.ds(pl.multiple_of((j + first) * BLK, BLK), BLK)
            cols = pl.ds(pl.multiple_of(j * BLK, BLK), BLK)
            inverse = scale_ref[0:1, source]
            for i in range(rows // BLK):
                here = pl.ds(i * BLK, BLK)
                out_ref[here, cols] = coded(value_ref[here, source], inverse)


def message_shapes(rows, blocks, pieces):
    counts = [blocks] if pieces == 1 else [blocks // 2, blocks - blocks // 2]
    return [jax.ShapeDtypeStruct((rows + EXTRA, count * BLK), jnp.int16) for count in counts]


def message_scratch(rows, blocks):
    return [pltpu.VMEM((rows, blocks * BLK), jnp.float32), pltpu.VMEM((8, blocks * BLK), jnp.float32)]


def masked_load(place, pattern_ref, x_ref, rows, block_col):
    col = pl.ds(pl.multiple_of(block_col * BLK, BLK), BLK)

    def load(i):
        block_row = place[0] * (rows // BLK) + i
        kept = (pattern_ref[block_row, block_col] == 1) | (place[1] + block_row == place[2] + block_col)
        value = x_ref[0, pl.ds(i * BLK, BLK), col]
        return jnp.where(kept, value, 0.0)

    return load


def encode_partial(after, partial, pattern, place, rows, first_block, blocks, received=(), pieces=1):
    width = partial.shape[2] if first_block > 0 else blocks * BLK

    def kernel(place_ref, pattern_ref, x_ref, *refs):
        got_refs, out_refs, (value_ref, scale_ref) = refs[:len(received)], refs[len(received):-2], refs[-2:]

        def segment(code_ref, first):
            def load(j):
                own = masked_load(place_ref, pattern_ref, x_ref, rows, j + first + first_block)
                if code_ref is None:
                    return own
                cols = pl.ds(pl.multiple_of(j * BLK, BLK), BLK)
                scale = scales(code_ref, rows, cols)
                return lambda i: own(i) + decoded(code_ref, i * BLK, scale, cols)

            return load

        segments = [(first, count, segment(code_ref, first)) for code_ref, first, count in spans(got_refs)]
        encode_all(segments or [(0, blocks, segment(None, 0))], out_refs, value_ref, scale_ref, rows)

    shapes = message_shapes(rows, blocks, pieces)
    return run(
        kernel, after, [partial, *received],
        [pl.BlockSpec((1, rows, width), lambda g, place_ref, pattern_ref: (0, place_ref[0], 0))]
        + [VMEM_SPEC] * len(received),
        [VMEM_SPEC] * len(shapes), shapes, rows * width * 4 + rows * blocks * BLK * 2 * (1 + len(received)),
        scalars=(place, pattern), scratch=message_scratch(rows, blocks),
    )


def merge(after, first, second, pieces=1):
    rows, blocks = first[0].shape[0] - EXTRA, sum(piece.shape[1] for piece in first) // BLK

    def kernel(*refs):
        count = len(first)
        out_refs, (value_ref, scale_ref) = refs[2 * count:-2], refs[-2:]

        def segment(a_ref, b_ref):
            def load(j):
                cols = pl.ds(pl.multiple_of(j * BLK, BLK), BLK)
                a_scale = scales(a_ref, rows, cols)
                b_scale = scales(b_ref, rows, cols)
                return lambda i: decoded(a_ref, i * BLK, a_scale, cols) + decoded(b_ref, i * BLK, b_scale, cols)

            return load

        segments = [
            (start, blocks, segment(a_ref, b_ref))
            for (a_ref, start, blocks), b_ref in zip(spans(refs[:count]), refs[count:2 * count])
        ]
        encode_all(segments, out_refs, value_ref, scale_ref, rows)

    shapes = message_shapes(rows, blocks, pieces)
    return run(
        kernel, after, [*first, *second], [VMEM_SPEC] * (2 * len(first)), [VMEM_SPEC] * len(shapes), shapes,
        rows * blocks * BLK * 6, scratch=message_scratch(rows, blocks),
    )


def low_total(after, partial, pattern, place, received):
    _, rows, width = partial.shape

    def kernel(place_ref, pattern_ref, x_ref, *refs):
        for code_ref, first, blocks in spans(refs[:-1]):

            @pl.loop(0, blocks)
            def _(j):
                cols = pl.ds(pl.multiple_of(j * BLK, BLK), BLK)
                target = pl.ds(pl.multiple_of((j + first) * BLK, BLK), BLK)
                scale = scales(code_ref, rows, cols)
                load = masked_load(place_ref, pattern_ref, x_ref, rows, j + first)
                for i in range(rows // BLK):
                    refs[-1][0, pl.ds(i * BLK, BLK), target] = load(i) + decoded(code_ref, i * BLK, scale, cols)

    return run(
        kernel, after, [partial, *received], [VMEM_SPEC] * (1 + len(received)), VMEM_SPEC,
        jax.ShapeDtypeStruct(partial.shape, jnp.float32), partial.size * 10, scalars=(place, pattern),
    )


def mid_half(after, owner, code, base=None):
    rows, width = code[0].shape[0] - EXTRA, sum(piece.shape[1] for piece in code)
    extra = [] if base is None else [base]

    def kernel(owner_ref, *refs):
        for code_ref, first, blocks in spans(refs[:len(code)]):

            @pl.loop(0, blocks)
            def _(j):
                cols = pl.ds(pl.multiple_of(j * BLK, BLK), BLK)
                target = pl.ds(pl.multiple_of((j + first) * BLK, BLK), BLK)
                scale = scales(code_ref, rows, cols)
                for i in range(rows // BLK):
                    refs[-1][0, pl.ds(i * BLK, BLK), target] = decoded(code_ref, i * BLK, scale, cols)

    return run(
        kernel, after, [*code] + extra,
        [VMEM_SPEC] * len(code) + [pl.BlockSpec(memory_space=pl.ANY)] * len(extra),
        pl.BlockSpec((1, rows, width), lambda g, owner_ref: (0, owner_ref[0], 0)),
        jax.ShapeDtypeStruct((1, 2 * rows, width), jnp.float32), rows * width * 6, scalars=(owner,),
        aliases={1 + len(code): 0} if extra else None,
    )


def corner_rows(after, pivots, partial):
    lines = pivots.reshape(-1, BLK)

    def kernel(pivot_ref, x_ref, out_ref):
        source = pivot_ref[0:1, :] % BLK
        turned = (lax.broadcasted_iota(jnp.int32, (BLK, BLK), 0) == source).astype(jnp.float32)
        out_ref[...] = lax.dot_general(
            turned, x_ref[0], (((0,), (0,)), ((), ())), precision=HIGHEST, preferred_element_type=jnp.float32
        )

    return run(
        kernel, after, [lines, partial],
        [pl.BlockSpec((8, BLK), lambda g: (0, 0)), pl.BlockSpec((1, BLK, BLK), lambda g: (0, 0, 0))],
        pl.BlockSpec((BLK, BLK), lambda g: (0, 0)), jax.ShapeDtypeStruct((BLK, BLK), jnp.float32), BLK * BLK * 8,
    )


def corner_sum(after, parts):
    def kernel(a_ref, b_ref, c_ref, d_ref, out_ref):
        out_ref[...] = (a_ref[...] + b_ref[...]) + (c_ref[...] + d_ref[...])

    shape = jax.ShapeDtypeStruct((BLK, BLK), jnp.float32)
    return run(kernel, after, parts, [VMEM_SPEC] * 4, VMEM_SPEC, shape, BLK * BLK * 20)


def factor(after, corner):
    order = corner.shape[0]

    def kernel(a_ref, packed_ref, lower_ref, upper_ref, direct, direct_unit, turned, turned_unit):
        lane = lax.broadcasted_iota(jnp.int32, (order, order), 1)
        sub = lax.broadcasted_iota(jnp.int32, (order, order), 0)
        lane_row = lax.broadcasted_iota(jnp.int32, (1, order), 1)
        sub_col = lax.broadcasted_iota(jnp.int32, (order, 1), 0)
        unit = (lane == sub).astype(jnp.float32)
        direct[...] = a_ref[...]
        direct_unit[...] = unit
        turned[...] = a_ref[...].T
        turned_unit[...] = unit

        @pl.loop(0, order - 1)
        def _(k):
            for held, held_unit in ((direct, direct_unit), (turned, turned_unit)):
                left = held[...]
                row_left = held[pl.ds(k, 1), :]
                row_right = held_unit[pl.ds(k, 1), :]
                col = jnp.sum(jnp.where(lane == k, left, 0.0), axis=1, keepdims=True)
                pivot = jnp.sum(jnp.where(lane_row == k, row_left, 0.0), axis=1, keepdims=True)
                below = sub_col > k
                multipliers = jnp.where(below, col / pivot, 0.0)
                fresh = left - multipliers * jnp.where(lane_row > k, row_left, 0.0)
                held[...] = jnp.where((lane == k) & below, multipliers, fresh)
                held_unit[...] = held_unit[...] - multipliers * row_right

        packed_ref[...] = direct[...]
        lower_ref[...] = direct_unit[...]
        pivots = jnp.sum(jnp.where(lane == sub, turned[...], 0.0), axis=1, keepdims=True)
        upper_ref[...] = (turned_unit[...] / pivots).T

    shape = jax.ShapeDtypeStruct((order, order), jnp.float32)
    return run(
        kernel, after, [corner], [VMEM_SPEC], [VMEM_SPEC] * 3, [shape] * 3, order * order * 16, 2e9,
        scratch=[pltpu.VMEM((order, order), jnp.float32)] * 4,
    )


def exact_dot(left, right):
    return jnp.dot(left, right, precision=HIGHEST, preferred_element_type=jnp.float32)


def low_dot(left, right):
    return jnp.dot(left, right, preferred_element_type=jnp.float32)


def permuted_codes(order_block, codes, scale):
    codes = codes.astype(jnp.int32)
    high = (codes >> 8).astype(jnp.float32).astype(jnp.bfloat16)
    low = (codes & 255).astype(jnp.float32).astype(jnp.bfloat16)
    both = jnp.concatenate([high, low], axis=0)
    return low_dot(jnp.concatenate([order_block * 256.0, order_block], axis=1).astype(jnp.bfloat16), both) * scale


def lower_panel(after, flags, order, own, received, upper_inverse):
    rows = own.shape[0] - EXTRA

    def kernel(flag_ref, order_ref, own_ref, got_ref, inverse_ref, slab_ref, low_ref):
        cols = pl.ds(0, PANEL)
        own_scale = scales(own_ref, rows, cols)
        got_scale = scales(got_ref, rows, cols)
        first_col = flag_ref[3] == 0

        @pl.loop(0, rows // BLK, unroll=4)
        def _(i):
            here = pl.ds(pl.multiple_of(i * BLK, BLK), BLK)
            order_block = order_ref[here, :]
            slab_ref[here, :] = permuted_codes(order_block, own_ref[here, :], own_scale) + permuted_codes(
                order_block, got_ref[here, :], got_scale
            )

        panel = exact_dot(slab_ref[...], inverse_ref[...])
        low_ref[...] = panel.astype(jnp.bfloat16)

        @pl.when(first_col)
        def _():
            slab_ref[...] = panel

    return run(
        kernel, after, [flags, order, own, received, upper_inverse], [SMEM_SPEC] + [VMEM_SPEC] * 4, [VMEM_SPEC] * 2,
        [jax.ShapeDtypeStruct((rows, PANEL), jnp.float32), jax.ShapeDtypeStruct((rows, PANEL), jnp.bfloat16)],
        rows * PANEL * 14, rows * PANEL * PANEL * 20,
    )


def upper_panel(after, flags, order, slab, own, received, lower_inverse):
    rows, rest = own.shape[0] - EXTRA, own.shape[1]
    width = rest + PANEL

    def kernel(flag_ref, order_ref, slab_ref, own_ref, own_scale, got_ref, got_scale, inverse_ref, up_ref, low_ref):
        first = exact_dot(inverse_ref[...], slab_ref[...])
        up_ref[:, :PANEL] = first
        low_ref[:, :PANEL] = first.astype(jnp.bfloat16)

        def write(code_ref, scale_ref):
            scale = jnp.exp2(scale_ref[...].astype(jnp.int32).astype(jnp.float32)[0:1])
            value = permuted_codes(order_ref[...], code_ref[...], scale)
            value = exact_dot(inverse_ref[...], value)
            up_ref[:, PANEL:] = value
            low_ref[:, PANEL:] = value.astype(jnp.bfloat16)

        pl.when(flag_ref[1] == 0)(lambda: write(own_ref, own_scale))
        pl.when(flag_ref[1] == 1)(lambda: write(got_ref, got_scale))

    first_block = lambda g: (0, 0)
    code_spec = pl.BlockSpec((BLK, rest), first_block)
    scale_spec = pl.BlockSpec((EXTRA, rest), lambda g: (rows // EXTRA, 0))
    square = pl.BlockSpec((BLK, BLK), first_block)
    return run(
        kernel, after, [flags, order, slab, own, own, received, received, lower_inverse],
        [SMEM_SPEC, square, square, code_spec, scale_spec, code_spec, scale_spec, square],
        [pl.BlockSpec((BLK, width), first_block)] * 2,
        [jax.ShapeDtypeStruct((PANEL, width), jnp.float32), jax.ShapeDtypeStruct((PANEL, width), jnp.bfloat16)],
        BLK * width * 10, BLK * BLK * width * 16,
    )


def top_total(after, flags, order, codes, slab, lower_low, upper_low, upper, packed):
    total_rows = slab.shape[0]
    rows, rest = codes[0].shape[0] - EXTRA, codes[0].shape[1]
    width = rest + PANEL
    part_blocks = rows // BLK

    def kernel(flag_ref, order_ref, own_a, got_a, own_b, got_b, slab_ref, low_ref, up_low_ref, up_ref, packed_ref, out_ref):
        i = pl.program_id(0)
        part = i // part_blocks
        row = pl.multiple_of((i % part_blocks) * BLK, BLK)
        first_row = (flag_ref[2] == 0) & (i == 0)
        first_col = flag_ref[3] == 0
        rest_cols = pl.ds(0, rest)

        @pl.when(jnp.logical_not(first_row))
        def _():
            low = low_ref[...]

            def write(code_ref):
                scale = scales(code_ref, rows, rest_cols)
                value = permuted_codes(order_ref[...], code_ref[pl.ds(row, BLK), :], scale)
                out_ref[:, PANEL:] = value - low_dot(low, up_low_ref[:, PANEL:])

            owned_b = part == flag_ref[1]
            owned_a = part == 2 + flag_ref[0]
            pl.when(owned_b)(lambda: write(own_b))
            pl.when((part < 2) & jnp.logical_not(owned_b))(lambda: write(got_b))
            pl.when(owned_a)(lambda: write(own_a))
            pl.when((part >= 2) & jnp.logical_not(owned_a))(lambda: write(got_a))
            product = low_dot(low, up_low_ref[:, :PANEL])
            out_ref[:, :PANEL] = jnp.where(first_col, slab_ref[...], slab_ref[...] - product)

        @pl.when(first_row)
        def _():
            out_ref[:, PANEL:] = up_ref[:, PANEL:]
            out_ref[:, :PANEL] = jnp.where(first_col, packed_ref[...], up_ref[:, :PANEL])

    square = pl.BlockSpec((BLK, BLK), lambda i: (i, 0))
    return run(
        kernel, after, [flags, order, *codes, slab, lower_low, upper_low, upper, packed],
        [SMEM_SPEC, square] + [VMEM_SPEC] * 4 + [square, square] + [VMEM_SPEC] * 3,
        pl.BlockSpec((BLK, width), lambda i: (i, 0)),
        jax.ShapeDtypeStruct((total_rows, width), jnp.float32),
        total_rows * width * 6, total_rows * width * BLK * 6, grid=(total_rows // BLK,),
    )


def on_device(partial_top, partial_mid, partial_low, pattern_top, pattern_mid, pattern_low, pivots):
    layer, row, col = (lax.axis_index(name) for name in ("layer", "row", "col"))
    bits = list(range(lax.axis_size("layer").bit_length() - 1))
    low_bit, high_bit = layer & 1, (layer >> 1) & 1
    flags = jnp.stack([low_bit, high_bit, row, col]).astype(jnp.int32)
    order = ((pivots % BLK)[:, None] == jnp.arange(BLK, dtype=jnp.int32)[None, :]).astype(jnp.bfloat16)

    def sender(partial, pattern, rows, first_block, blocks):
        corner_block = [row * pattern.shape[1], col * pattern.shape[2]]

        def encode(after, part, received=(), pieces=1):
            place = jnp.stack([jnp.asarray(part, jnp.int32), *corner_block]).astype(jnp.int32)
            return encode_partial(after, partial, pattern[0], place, rows, first_block, blocks, received, pieces)

        return encode

    def exchanged(after, own, got, some):
        own = merge(after, own, got)
        for bit in some:
            own = merge([], own, swapped(own, bit))
        return own

    top_rows, top_blocks = partial_top.shape[1], partial_top.shape[2] // BLK
    mid_blocks, low_blocks = partial_mid.shape[2] // BLK, partial_low.shape[2] // BLK
    low_rows = partial_low.shape[1]
    encode_mid = sender(partial_mid, pattern_mid, partial_mid.shape[1] // 2, 0, mid_blocks)
    encode_slab = sender(partial_top, pattern_top, top_rows, 0, 1)
    encode_top = sender(partial_top, pattern_top, top_rows // 4, 1, top_blocks - 1)
    encode_low = sender(partial_low, pattern_low, low_rows, 0, low_blocks)

    count = lax.axis_size("layer")
    corner = corner_rows([], pivots, partial_top)
    beside = [lax.ppermute(corner, "layer", [(i, i ^ apart) for i in range(count)]) for apart in (1, 2, 3)]
    slab = encode_slab([*[corner]], 0)
    slab_got = swapped(slab, 0)
    mid_sent = encode_mid([*slab, *beside], 1 - high_bit, (), 1)
    mid_got = swapped(mid_sent, 1)
    a_sent = encode_top([*mid_sent], 3 - low_bit)
    a_got = swapped(a_sent, 0)
    summed = corner_sum([*a_sent], [corner, *beside])
    corner = summed
    for bit in bits[2:]:
        corner = corner + swapped(corner, bit)
    corner_row = broadcast_stages(corner, "row")
    corner_col = broadcast_stages(corner_row[-1], "col")
    corner_all = corner_col[-1]
    b_sent = encode_top([*[summed]], 1 - high_bit)
    b_got = swapped(b_sent, 1)
    slab = exchanged([*b_sent, corner_row[-1]], slab, slab_got, bits[1:-1])
    slab_got = swapped(slab, bits[-1])
    mid = encode_mid([*slab, corner_col[0]], high_bit, mid_got, 2)
    mid_got = swapped(mid, 0)
    packed, lower_inverse, upper_inverse = factor([*mid], corner_all)
    b = encode_top([*[packed]], high_bit, b_got)
    b_got = swapped(b, 0)
    a = encode_top([*b], 2 + low_bit, a_got)
    a_got = swapped(a, 1)
    panel, lower_low = lower_panel([*a, *mid_got], flags, order, *slab, *slab_got, upper_inverse)
    lower_stages = broadcast_stages(lower_low, "col")
    lower_low = lower_stages[-1]
    mid = merge([*[panel]], mid, mid_got, 1)
    mid_got = swapped(mid, 1)
    b = exchanged([*mid], b, b_got, bits[2:])
    b_got = swapped(b, 1)
    a = exchanged([*b], a, a_got, bits[2:])
    a_got = swapped(a, 0)
    mid_sums = mid_half([*a], high_bit[None].astype(jnp.int32), mid)
    low = encode_low([*[mid_sums]], 0, (), 1)
    low_got = swapped(low, 0)
    upper, upper_low = upper_panel([*low, *a_got], flags, order, panel, *b, *b_got, lower_inverse)
    upper_low = broadcast_stages(upper_low, "row")[-1]
    top_factor = top_total([*[upper]], flags, order, (*a, *a_got, *b, *b_got), panel, lower_low, upper_low, upper, packed)
    low_place = jnp.stack([jnp.int32(0), row * pattern_low.shape[1], col * pattern_low.shape[2]]).astype(jnp.int32)
    low_sums = low_total([*[top_factor]], partial_low, pattern_low[0], low_place, low_got)
    mid_sums = mid_half([top_factor], (1 - high_bit)[None].astype(jnp.int32), mid_got, mid_sums)
    return top_factor, mid_sums, low_sums


def solution(mesh):
    placed = (
        P("layer", "row", "col"),
        P("layer", "row", "col"),
        P("layer", "row", "col"),
        P("layer", "row", "col"),
        P("layer", "row", "col"),
        P("layer", "row", "col"),
        P("row"),
    )
    return jax.shard_map(
        on_device,
        mesh=mesh,
        in_specs=placed,
        out_specs=(P("row", "col"), P("layer", "row", "col"), P("layer", "row", "col")),
        check_vma=False,
    )
```

```python
import jax
import jax.numpy as jnp
from jax import lax
from jax.experimental import pallas as pl
from jax.experimental.pallas import tpu as pltpu
from jax.sharding import PartitionSpec as P

PANEL = 128
BLK = 128
EXTRA = 16
HIGHEST = lax.Precision.HIGHEST
VMEM_LIMIT = 48 * 1024 * 1024

SMEM_SPEC = pl.BlockSpec(memory_space=pltpu.SMEM)
VMEM_SPEC = pl.BlockSpec(memory_space=pltpu.VMEM)


def swapped(value, bit):
    count = lax.axis_size("layer")
    pairs = [(i, i ^ (1 << bit)) for i in range(count)]
    return jax.tree.map(lambda piece: lax.ppermute(piece, "layer", pairs), value)


def broadcast_stages(value, axis):
    count = lax.axis_size(axis)
    own = lax.axis_index(axis)
    span = count // 2
    stages = []
    while span >= 1:
        got = lax.ppermute(value, axis, [(i, i + span) for i in range(0, count, 2 * span)])
        takes = own % (2 * span) == span
        value = jnp.where(takes, got, value)
        stages.append(value)
        span //= 2
    return stages


def exponents(largest):
    return jnp.floor(jnp.log2(jnp.maximum(largest, 1e-30))) - 14.0


def coded(value, inverse):
    scaled = jnp.round(value * inverse)
    scaled = jnp.minimum(jnp.maximum(scaled, -32767.0), 32767.0)
    return scaled.astype(jnp.int32).astype(jnp.int16)


def scales(code_ref, rows, cols):
    held = code_ref[pl.ds(rows, EXTRA), cols].astype(jnp.int32).astype(jnp.float32)
    return jnp.exp2(held[0:1])


def decoded(code_ref, row, scale, cols):
    return code_ref[pl.ds(row, BLK), cols].astype(jnp.int32).astype(jnp.float32) * scale


def run(kernel, after, operands, specs, out_specs, out_shape, nbytes, flops=0, grid=(1,), scalars=(), scratch=(), aliases=None):
    taken = len(scalars) + len(operands)

    def body(*refs):
        kernel(*refs[:taken], *refs[taken + len(after):])

    return pl.pallas_call(
        body,
        grid_spec=pltpu.PrefetchScalarGridSpec(
            num_scalar_prefetch=len(scalars),
            grid=grid,
            in_specs=list(specs) + [pl.BlockSpec(memory_space=pl.ANY)] * len(after),
            out_specs=out_specs,
            scratch_shapes=list(scratch),
        ),
        out_shape=out_shape,
        input_output_aliases=aliases or {},
        compiler_params=pltpu.CompilerParams(vmem_limit_bytes=VMEM_LIMIT),
        cost_estimate=pl.CostEstimate(flops=0, bytes_accessed=1024, transcendentals=0),
    )(*scalars, *operands, *after)


def spans(pieces):
    first, result = 0, []
    for piece in pieces:
        blocks = piece.shape[1] // BLK
        result.append((piece, first, blocks))
        first += blocks
    return result


def encode_all(segments, out_refs, value_ref, scale_ref, rows):
    for first, blocks, load in segments:

        @pl.loop(0, blocks)
        def _(j):
            cols = pl.ds(pl.multiple_of((j + first) * BLK, BLK), BLK)
            fetch = load(j)
            largest = jnp.zeros((1, BLK), jnp.float32)
            for i in range(rows // BLK):
                value = fetch(i)
                value_ref[pl.ds(i * BLK, BLK), cols] = value
                largest = jnp.maximum(largest, jnp.max(jnp.abs(value), axis=0, keepdims=True))
            scale_ref[0:1, cols] = largest

    for out_ref, first, blocks in spans(out_refs):
        width = pl.ds(first * BLK, blocks * BLK)
        power = exponents(scale_ref[0:1, width])
        scale_ref[0:1, width] = jnp.exp2(-power)
        held = jnp.broadcast_to(power, (EXTRA, blocks * BLK))
        out_ref[pl.ds(rows, EXTRA), :] = held.astype(jnp.int32).astype(jnp.int16)

        @pl.loop(0, blocks)
        def _(j):
            source = pl.ds(pl.multiple_of((j + first) * BLK, BLK), BLK)
            cols = pl.ds(pl.multiple_of(j * BLK, BLK), BLK)
            inverse = scale_ref[0:1, source]
            for i in range(rows // BLK):
                here = pl.ds(i * BLK, BLK)
                out_ref[here, cols] = coded(value_ref[here, source], inverse)


def message_shapes(rows, blocks, pieces):
    counts = [blocks] if pieces == 1 else [blocks // 2, blocks - blocks // 2]
    return [jax.ShapeDtypeStruct((rows + EXTRA, count * BLK), jnp.int16) for count in counts]


def message_scratch(rows, blocks):
    return [pltpu.VMEM((rows, blocks * BLK), jnp.float32), pltpu.VMEM((8, blocks * BLK), jnp.float32)]


def masked_load(place, pattern_ref, x_ref, rows, block_col):
    col = pl.ds(pl.multiple_of(block_col * BLK, BLK), BLK)

    def load(i):
        block_row = place[0] * (rows // BLK) + i
        kept = (pattern_ref[block_row, block_col] == 1) | (place[1] + block_row == place[2] + block_col)
        value = x_ref[0, pl.ds(i * BLK, BLK), col]
        return jnp.where(kept, value, 0.0)

    return load


def encode_partial(after, partial, pattern, place, rows, first_block, blocks, received=(), pieces=1):
    width = partial.shape[2] if first_block > 0 else blocks * BLK

    def kernel(place_ref, pattern_ref, x_ref, *refs):
        got_refs, out_refs, (value_ref, scale_ref) = refs[:len(received)], refs[len(received):-2], refs[-2:]

        def segment(code_ref, first):
            def load(j):
                own = masked_load(place_ref, pattern_ref, x_ref, rows, j + first + first_block)
                if code_ref is None:
                    return own
                cols = pl.ds(pl.multiple_of(j * BLK, BLK), BLK)
                scale = scales(code_ref, rows, cols)
                return lambda i: own(i) + decoded(code_ref, i * BLK, scale, cols)

            return load

        segments = [(first, count, segment(code_ref, first)) for code_ref, first, count in spans(got_refs)]
        encode_all(segments or [(0, blocks, segment(None, 0))], out_refs, value_ref, scale_ref, rows)

    shapes = message_shapes(rows, blocks, pieces)
    return run(
        kernel, after, [partial, *received],
        [pl.BlockSpec((1, rows, width), lambda g, place_ref, pattern_ref: (0, place_ref[0], 0))]
        + [VMEM_SPEC] * len(received),
        [VMEM_SPEC] * len(shapes), shapes, rows * width * 4 + rows * blocks * BLK * 2 * (1 + len(received)),
        scalars=(place, pattern), scratch=message_scratch(rows, blocks),
    )


def merge(after, first, second, pieces=1):
    rows, blocks = first[0].shape[0] - EXTRA, sum(piece.shape[1] for piece in first) // BLK

    def kernel(*refs):
        count = len(first)
        out_refs, (value_ref, scale_ref) = refs[2 * count:-2], refs[-2:]

        def segment(a_ref, b_ref):
            def load(j):
                cols = pl.ds(pl.multiple_of(j * BLK, BLK), BLK)
                a_scale = scales(a_ref, rows, cols)
                b_scale = scales(b_ref, rows, cols)
                return lambda i: decoded(a_ref, i * BLK, a_scale, cols) + decoded(b_ref, i * BLK, b_scale, cols)

            return load

        segments = [
            (start, blocks, segment(a_ref, b_ref))
            for (a_ref, start, blocks), b_ref in zip(spans(refs[:count]), refs[count:2 * count])
        ]
        encode_all(segments, out_refs, value_ref, scale_ref, rows)

    shapes = message_shapes(rows, blocks, pieces)
    return run(
        kernel, after, [*first, *second], [VMEM_SPEC] * (2 * len(first)), [VMEM_SPEC] * len(shapes), shapes,
        rows * blocks * BLK * 6, scratch=message_scratch(rows, blocks),
    )


def low_total(after, partial, pattern, place, received):
    _, rows, width = partial.shape

    def kernel(place_ref, pattern_ref, x_ref, *refs):
        for code_ref, first, blocks in spans(refs[:-1]):

            @pl.loop(0, blocks)
            def _(j):
                cols = pl.ds(pl.multiple_of(j * BLK, BLK), BLK)
                target = pl.ds(pl.multiple_of((j + first) * BLK, BLK), BLK)
                scale = scales(code_ref, rows, cols)
                load = masked_load(place_ref, pattern_ref, x_ref, rows, j + first)
                for i in range(rows // BLK):
                    refs[-1][0, pl.ds(i * BLK, BLK), target] = load(i) + decoded(code_ref, i * BLK, scale, cols)

    return run(
        kernel, after, [partial, *received], [VMEM_SPEC] * (1 + len(received)), VMEM_SPEC,
        jax.ShapeDtypeStruct(partial.shape, jnp.float32), partial.size * 10, scalars=(place, pattern),
    )


def mid_half(after, owner, code, base=None):
    rows, width = code[0].shape[0] - EXTRA, sum(piece.shape[1] for piece in code)
    extra = [] if base is None else [base]

    def kernel(owner_ref, *refs):
        for code_ref, first, blocks in spans(refs[:len(code)]):

            @pl.loop(0, blocks)
            def _(j):
                cols = pl.ds(pl.multiple_of(j * BLK, BLK), BLK)
                target = pl.ds(pl.multiple_of((j + first) * BLK, BLK), BLK)
                scale = scales(code_ref, rows, cols)
                for i in range(rows // BLK):
                    refs[-1][0, pl.ds(i * BLK, BLK), target] = decoded(code_ref, i * BLK, scale, cols)

    return run(
        kernel, after, [*code] + extra,
        [VMEM_SPEC] * len(code) + [pl.BlockSpec(memory_space=pl.ANY)] * len(extra),
        pl.BlockSpec((1, rows, width), lambda g, owner_ref: (0, owner_ref[0], 0)),
        jax.ShapeDtypeStruct((1, 2 * rows, width), jnp.float32), rows * width * 6, scalars=(owner,),
        aliases={1 + len(code): 0} if extra else None,
    )


def corner_rows(after, pivots, partial):
    lines = pivots.reshape(-1, BLK)

    def kernel(pivot_ref, x_ref, out_ref):
        source = pivot_ref[0:1, :] % BLK
        turned = (lax.broadcasted_iota(jnp.int32, (BLK, BLK), 0) == source).astype(jnp.float32)
        out_ref[...] = lax.dot_general(
            turned, x_ref[0], (((0,), (0,)), ((), ())), precision=HIGHEST, preferred_element_type=jnp.float32
        )

    return run(
        kernel, after, [lines, partial],
        [pl.BlockSpec((8, BLK), lambda g: (0, 0)), pl.BlockSpec((1, BLK, BLK), lambda g: (0, 0, 0))],
        pl.BlockSpec((BLK, BLK), lambda g: (0, 0)), jax.ShapeDtypeStruct((BLK, BLK), jnp.float32), BLK * BLK * 8,
    )


def corner_sum(after, parts):
    def kernel(a_ref, b_ref, c_ref, d_ref, out_ref):
        out_ref[...] = (a_ref[...] + b_ref[...]) + (c_ref[...] + d_ref[...])

    shape = jax.ShapeDtypeStruct((BLK, BLK), jnp.float32)
    return run(kernel, after, parts, [VMEM_SPEC] * 4, VMEM_SPEC, shape, BLK * BLK * 20)


def factor(after, corner):
    order = corner.shape[0]

    def kernel(a_ref, packed_ref, lower_ref, upper_ref, direct, direct_unit, turned, turned_unit):
        lane = lax.broadcasted_iota(jnp.int32, (order, order), 1)
        sub = lax.broadcasted_iota(jnp.int32, (order, order), 0)
        lane_row = lax.broadcasted_iota(jnp.int32, (1, order), 1)
        sub_col = lax.broadcasted_iota(jnp.int32, (order, 1), 0)
        unit = (lane == sub).astype(jnp.float32)
        direct[...] = a_ref[...]
        direct_unit[...] = unit
        turned[...] = a_ref[...].T
        turned_unit[...] = unit

        @pl.loop(0, order - 1)
        def _(k):
            for held, held_unit in ((direct, direct_unit), (turned, turned_unit)):
                left = held[...]
                row_left = held[pl.ds(k, 1), :]
                row_right = held_unit[pl.ds(k, 1), :]
                col = jnp.sum(jnp.where(lane == k, left, 0.0), axis=1, keepdims=True)
                pivot = jnp.sum(jnp.where(lane_row == k, row_left, 0.0), axis=1, keepdims=True)
                below = sub_col > k
                multipliers = jnp.where(below, col / pivot, 0.0)
                fresh = left - multipliers * jnp.where(lane_row > k, row_left, 0.0)
                held[...] = jnp.where((lane == k) & below, multipliers, fresh)
                held_unit[...] = held_unit[...] - multipliers * row_right

        packed_ref[...] = direct[...]
        lower_ref[...] = direct_unit[...]
        pivots = jnp.sum(jnp.where(lane == sub, turned[...], 0.0), axis=1, keepdims=True)
        upper_ref[...] = (turned_unit[...] / pivots).T

    shape = jax.ShapeDtypeStruct((order, order), jnp.float32)
    return run(
        kernel, after, [corner], [VMEM_SPEC], [VMEM_SPEC] * 3, [shape] * 3, order * order * 16, 2e9,
        scratch=[pltpu.VMEM((order, order), jnp.float32)] * 4,
    )


def exact_dot(left, right):
    return jnp.dot(left, right, precision=HIGHEST, preferred_element_type=jnp.float32)


def low_dot(left, right):
    return jnp.dot(left, right, preferred_element_type=jnp.float32)


def permuted_codes(order_block, codes, scale):
    codes = codes.astype(jnp.int32)
    high = (codes >> 8).astype(jnp.float32).astype(jnp.bfloat16)
    low = (codes & 255).astype(jnp.float32).astype(jnp.bfloat16)
    both = jnp.concatenate([high, low], axis=0)
    return low_dot(jnp.concatenate([order_block * 256.0, order_block], axis=1).astype(jnp.bfloat16), both) * scale


def lower_panel(after, flags, order, own, received, upper_inverse):
    rows = own.shape[0] - EXTRA

    def kernel(flag_ref, order_ref, own_ref, got_ref, inverse_ref, slab_ref, low_ref):
        cols = pl.ds(0, PANEL)
        own_scale = scales(own_ref, rows, cols)
        got_scale = scales(got_ref, rows, cols)
        first_col = flag_ref[3] == 0

        @pl.loop(0, rows // BLK, unroll=4)
        def _(i):
            here = pl.ds(pl.multiple_of(i * BLK, BLK), BLK)
            order_block = order_ref[here, :]
            slab_ref[here, :] = permuted_codes(order_block, own_ref[here, :], own_scale) + permuted_codes(
                order_block, got_ref[here, :], got_scale
            )

        panel = exact_dot(slab_ref[...], inverse_ref[...])
        low_ref[...] = panel.astype(jnp.bfloat16)

        @pl.when(first_col)
        def _():
            slab_ref[...] = panel

    return run(
        kernel, after, [flags, order, own, received, upper_inverse], [SMEM_SPEC] + [VMEM_SPEC] * 4, [VMEM_SPEC] * 2,
        [jax.ShapeDtypeStruct((rows, PANEL), jnp.float32), jax.ShapeDtypeStruct((rows, PANEL), jnp.bfloat16)],
        rows * PANEL * 14, rows * PANEL * PANEL * 20,
    )


def upper_panel(after, flags, order, slab, own, received, lower_inverse):
    rows, rest = own.shape[0] - EXTRA, own.shape[1]
    width = rest + PANEL

    def kernel(flag_ref, order_ref, slab_ref, own_ref, own_scale, got_ref, got_scale, inverse_ref, up_ref, low_ref):
        first = exact_dot(inverse_ref[...], slab_ref[...])
        up_ref[:, :PANEL] = first
        low_ref[:, :PANEL] = first.astype(jnp.bfloat16)

        def write(code_ref, scale_ref):
            scale = jnp.exp2(scale_ref[...].astype(jnp.int32).astype(jnp.float32)[0:1])
            value = permuted_codes(order_ref[...], code_ref[...], scale)
            value = exact_dot(inverse_ref[...], value)
            up_ref[:, PANEL:] = value
            low_ref[:, PANEL:] = value.astype(jnp.bfloat16)

        pl.when(flag_ref[1] == 0)(lambda: write(own_ref, own_scale))
        pl.when(flag_ref[1] == 1)(lambda: write(got_ref, got_scale))

    first_block = lambda g: (0, 0)
    code_spec = pl.BlockSpec((BLK, rest), first_block)
    scale_spec = pl.BlockSpec((EXTRA, rest), lambda g: (rows // EXTRA, 0))
    square = pl.BlockSpec((BLK, BLK), first_block)
    return run(
        kernel, after, [flags, order, slab, own, own, received, received, lower_inverse],
        [SMEM_SPEC, square, square, code_spec, scale_spec, code_spec, scale_spec, square],
        [pl.BlockSpec((BLK, width), first_block)] * 2,
        [jax.ShapeDtypeStruct((PANEL, width), jnp.float32), jax.ShapeDtypeStruct((PANEL, width), jnp.bfloat16)],
        BLK * width * 10, BLK * BLK * width * 16,
    )


def top_total(after, flags, order, codes, slab, lower_low, upper_low, upper, packed):
    total_rows = slab.shape[0]
    rows, rest = codes[0].shape[0] - EXTRA, codes[0].shape[1]
    width = rest + PANEL
    part_blocks = rows // BLK

    def kernel(flag_ref, order_ref, own_a, got_a, own_b, got_b, slab_ref, low_ref, up_low_ref, up_ref, packed_ref, out_ref):
        def block_rows(sub):
            i = 2 * pl.program_id(0) + sub
            here = pl.ds(sub * BLK, BLK)
            part = i // part_blocks
            row = pl.multiple_of((i % part_blocks) * BLK, BLK)
            first_row = (flag_ref[2] == 0) & (i == 0)
            first_col = flag_ref[3] == 0
            rest_cols = pl.ds(0, rest)

            @pl.when(jnp.logical_not(first_row))
            def _():
                low = low_ref[here, :]

                def write(code_ref):
                    scale = scales(code_ref, rows, rest_cols)
                    value = permuted_codes(order_ref[here, :], code_ref[pl.ds(row, BLK), :], scale)
                    out_ref[here, PANEL:] = value - low_dot(low, up_low_ref[:, PANEL:])

                owned_b = part == flag_ref[1]
                owned_a = part == 2 + flag_ref[0]
                pl.when(owned_b)(lambda: write(own_b))
                pl.when((part < 2) & jnp.logical_not(owned_b))(lambda: write(got_b))
                pl.when(owned_a)(lambda: write(own_a))
                pl.when((part >= 2) & jnp.logical_not(owned_a))(lambda: write(got_a))
                product = low_dot(low, up_low_ref[:, :PANEL])
                out_ref[here, :PANEL] = jnp.where(first_col, slab_ref[here, :], slab_ref[here, :] - product)

            @pl.when(first_row)
            def _():
                out_ref[here, PANEL:] = up_ref[:, PANEL:]
                out_ref[here, :PANEL] = jnp.where(first_col, packed_ref[...], up_ref[:, :PANEL])

        for sub in range(2):
            block_rows(sub)

    square = pl.BlockSpec((2 * BLK, BLK), lambda i: (i, 0))
    return run(
        kernel, after, [flags, order, *codes, slab, lower_low, upper_low, upper, packed],
        [SMEM_SPEC, square] + [VMEM_SPEC] * 4 + [square, square] + [VMEM_SPEC] * 3,
        pl.BlockSpec((2 * BLK, width), lambda i: (i, 0)),
        jax.ShapeDtypeStruct((total_rows, width), jnp.float32),
        total_rows * width * 6, total_rows * width * BLK * 6, grid=(total_rows // (2 * BLK),),
    )


def on_device(partial_top, partial_mid, partial_low, pattern_top, pattern_mid, pattern_low, pivots):
    layer, row, col = (lax.axis_index(name) for name in ("layer", "row", "col"))
    bits = list(range(lax.axis_size("layer").bit_length() - 1))
    low_bit, high_bit = layer & 1, (layer >> 1) & 1
    flags = jnp.stack([low_bit, high_bit, row, col]).astype(jnp.int32)
    order = ((pivots % BLK)[:, None] == jnp.arange(BLK, dtype=jnp.int32)[None, :]).astype(jnp.bfloat16)

    def sender(partial, pattern, rows, first_block, blocks):
        corner_block = [row * pattern.shape[1], col * pattern.shape[2]]

        def encode(after, part, received=(), pieces=1):
            place = jnp.stack([jnp.asarray(part, jnp.int32), *corner_block]).astype(jnp.int32)
            return encode_partial(after, partial, pattern[0], place, rows, first_block, blocks, received, pieces)

        return encode

    def exchanged(after, own, got, some):
        own = merge(after, own, got)
        for bit in some:
            own = merge([], own, swapped(own, bit))
        return own

    top_rows, top_blocks = partial_top.shape[1], partial_top.shape[2] // BLK
    mid_blocks, low_blocks = partial_mid.shape[2] // BLK, partial_low.shape[2] // BLK
    low_rows = partial_low.shape[1]
    encode_mid = sender(partial_mid, pattern_mid, partial_mid.shape[1] // 2, 0, mid_blocks)
    encode_slab = sender(partial_top, pattern_top, top_rows, 0, 1)
    encode_top = sender(partial_top, pattern_top, top_rows // 4, 1, top_blocks - 1)
    encode_low = sender(partial_low, pattern_low, low_rows, 0, low_blocks)

    count = lax.axis_size("layer")
    corner = corner_rows([], pivots, partial_top)
    beside = [lax.ppermute(corner, "layer", [(i, i ^ apart) for i in range(count)]) for apart in (1, 2, 3)]
    slab = encode_slab([*[corner]], 0)
    slab_got = swapped(slab, 0)
    mid_sent = encode_mid([*slab, *beside], 1 - high_bit, (), 1)
    mid_got = swapped(mid_sent, 1)
    a_sent = encode_top([*mid_sent], 3 - low_bit)
    a_got = swapped(a_sent, 0)
    summed = corner_sum([*a_sent], [corner, *beside])
    corner = summed
    for bit in bits[2:]:
        corner = corner + swapped(corner, bit)
    corner_row = broadcast_stages(corner, "row")
    corner_col = broadcast_stages(corner_row[-1], "col")
    corner_all = corner_col[-1]
    b_sent = encode_top([*[summed]], 1 - high_bit)
    b_got = swapped(b_sent, 1)
    slab = exchanged([*b_sent, corner_row[-1]], slab, slab_got, bits[1:-1])
    slab_got = swapped(slab, bits[-1])
    mid = encode_mid([*slab, corner_col[0]], high_bit, mid_got, 2)
    mid_got = swapped(mid, 0)
    packed, lower_inverse, upper_inverse = factor([*mid], corner_all)
    b = encode_top([*[packed]], high_bit, b_got)
    b_got = swapped(b, 0)
    a = encode_top([*b], 2 + low_bit, a_got)
    a_got = swapped(a, 1)
    panel, lower_low = lower_panel([*a, *mid_got], flags, order, *slab, *slab_got, upper_inverse)
    lower_stages = broadcast_stages(lower_low, "col")
    lower_low = lower_stages[-1]
    mid = merge([*[panel]], mid, mid_got, 1)
    mid_got = swapped(mid, 1)
    b = exchanged([*mid], b, b_got, bits[2:])
    b_got = swapped(b, 1)
    a = exchanged([*b], a, a_got, bits[2:])
    a_got = swapped(a, 0)
    mid_sums = mid_half([*a], high_bit[None].astype(jnp.int32), mid)
    low = encode_low([*[mid_sums]], 0, (), 1)
    low_got = swapped(low, 0)
    upper, upper_low = upper_panel([*low, *a_got], flags, order, panel, *b, *b_got, lower_inverse)
    upper_low = broadcast_stages(upper_low, "row")[-1]
    top_factor = top_total([*[upper]], flags, order, (*a, *a_got, *b, *b_got), panel, lower_low, upper_low, upper, packed)
    low_place = jnp.stack([jnp.int32(0), row * pattern_low.shape[1], col * pattern_low.shape[2]]).astype(jnp.int32)
    low_sums = low_total([*[top_factor]], partial_low, pattern_low[0], low_place, low_got)
    mid_sums = mid_half([top_factor], (1 - high_bit)[None].astype(jnp.int32), mid_got, mid_sums)
    return top_factor, mid_sums, low_sums


def solution(mesh):
    placed = (
        P("layer", "row", "col"),
        P("layer", "row", "col"),
        P("layer", "row", "col"),
        P("layer", "row", "col"),
        P("layer", "row", "col"),
        P("layer", "row", "col"),
        P("row"),
    )
    return jax.shard_map(
        on_device,
        mesh=mesh,
        in_specs=placed,
        out_specs=(P("row", "col"), P("layer", "row", "col"), P("layer", "row", "col")),
        check_vma=False,
    )
```

```python
import jax
import jax.numpy as jnp
from jax import lax
from jax.experimental import pallas as pl
from jax.experimental.pallas import tpu as pltpu
from jax.sharding import PartitionSpec as P

PANEL = 128
BLK = 128
EXTRA = 16
HIGHEST = lax.Precision.HIGHEST
VMEM_LIMIT = 48 * 1024 * 1024

SMEM_SPEC = pl.BlockSpec(memory_space=pltpu.SMEM)
VMEM_SPEC = pl.BlockSpec(memory_space=pltpu.VMEM)


def swapped(value, bit):
    count = lax.axis_size("layer")
    pairs = [(i, i ^ (1 << bit)) for i in range(count)]
    return jax.tree.map(lambda piece: lax.ppermute(piece, "layer", pairs), value)


def broadcast_stages(value, axis):
    count = lax.axis_size(axis)
    own = lax.axis_index(axis)
    span = count // 2
    stages = []
    while span >= 1:
        got = lax.ppermute(value, axis, [(i, i + span) for i in range(0, count, 2 * span)])
        takes = own % (2 * span) == span
        value = jnp.where(takes, got, value)
        stages.append(value)
        span //= 2
    return stages


def exponents(largest):
    return jnp.floor(jnp.log2(jnp.maximum(largest, 1e-30))) - 14.0


def coded(value, inverse):
    scaled = jnp.round(value * inverse)
    scaled = jnp.minimum(jnp.maximum(scaled, -32767.0), 32767.0)
    return scaled.astype(jnp.int32).astype(jnp.int16)


def scales(code_ref, rows, cols):
    held = code_ref[pl.ds(rows, EXTRA), cols].astype(jnp.int32).astype(jnp.float32)
    return jnp.exp2(held[0:1])


def decoded(code_ref, row, scale, cols):
    return code_ref[pl.ds(row, BLK), cols].astype(jnp.int32).astype(jnp.float32) * scale


def run(kernel, after, operands, specs, out_specs, out_shape, nbytes, flops=0, grid=(1,), scalars=(), scratch=(), aliases=None):
    taken = len(scalars) + len(operands)

    def body(*refs):
        kernel(*refs[:taken], *refs[taken + len(after):])

    return pl.pallas_call(
        body,
        grid_spec=pltpu.PrefetchScalarGridSpec(
            num_scalar_prefetch=len(scalars),
            grid=grid,
            in_specs=list(specs) + [pl.BlockSpec(memory_space=pl.ANY)] * len(after),
            out_specs=out_specs,
            scratch_shapes=list(scratch),
        ),
        out_shape=out_shape,
        input_output_aliases=aliases or {},
        compiler_params=pltpu.CompilerParams(vmem_limit_bytes=VMEM_LIMIT),
        cost_estimate=pl.CostEstimate(flops=0, bytes_accessed=1024, transcendentals=0),
    )(*scalars, *operands, *after)


def spans(pieces):
    first, result = 0, []
    for piece in pieces:
        blocks = piece.shape[1] // BLK
        result.append((piece, first, blocks))
        first += blocks
    return result


def encode_all(segments, out_refs, value_ref, scale_ref, rows):
    for first, blocks, load in segments:

        @pl.loop(0, blocks)
        def _(j):
            cols = pl.ds(pl.multiple_of((j + first) * BLK, BLK), BLK)
            fetch = load(j)
            largest = jnp.zeros((1, BLK), jnp.float32)
            for i in range(rows // BLK):
                value = fetch(i)
                value_ref[pl.ds(i * BLK, BLK), cols] = value
                largest = jnp.maximum(largest, jnp.max(jnp.abs(value), axis=0, keepdims=True))
            scale_ref[0:1, cols] = largest

    for out_ref, first, blocks in spans(out_refs):
        width = pl.ds(first * BLK, blocks * BLK)
        power = exponents(scale_ref[0:1, width])
        scale_ref[0:1, width] = jnp.exp2(-power)
        held = jnp.broadcast_to(power, (EXTRA, blocks * BLK))
        out_ref[pl.ds(rows, EXTRA), :] = held.astype(jnp.int32).astype(jnp.int16)

        @pl.loop(0, blocks)
        def _(j):
            source = pl.ds(pl.multiple_of((j + first) * BLK, BLK), BLK)
            cols = pl.ds(pl.multiple_of(j * BLK, BLK), BLK)
            inverse = scale_ref[0:1, source]
            for i in range(rows // BLK):
                here = pl.ds(i * BLK, BLK)
                out_ref[here, cols] = coded(value_ref[here, source], inverse)


def message_shapes(rows, blocks, pieces):
    counts = [blocks] if pieces == 1 else [blocks // 2, blocks - blocks // 2]
    return [jax.ShapeDtypeStruct((rows + EXTRA, count * BLK), jnp.int16) for count in counts]


def message_scratch(rows, blocks):
    return [pltpu.VMEM((rows, blocks * BLK), jnp.float32), pltpu.VMEM((8, blocks * BLK), jnp.float32)]


def masked_load(place, pattern_ref, x_ref, rows, block_col):
    col = pl.ds(pl.multiple_of(block_col * BLK, BLK), BLK)

    def load(i):
        block_row = place[0] * (rows // BLK) + i
        kept = (pattern_ref[block_row, block_col] == 1) | (place[1] + block_row == place[2] + block_col)
        value = x_ref[0, pl.ds(i * BLK, BLK), col]
        return jnp.where(kept, value, 0.0)

    return load


def encode_partial(after, partial, pattern, place, rows, first_block, blocks, received=(), pieces=1):
    width = partial.shape[2] if first_block > 0 else blocks * BLK

    def kernel(place_ref, pattern_ref, x_ref, *refs):
        got_refs, out_refs, (value_ref, scale_ref) = refs[:len(received)], refs[len(received):-2], refs[-2:]

        def segment(code_ref, first):
            def load(j):
                own = masked_load(place_ref, pattern_ref, x_ref, rows, j + first + first_block)
                if code_ref is None:
                    return own
                cols = pl.ds(pl.multiple_of(j * BLK, BLK), BLK)
                scale = scales(code_ref, rows, cols)
                return lambda i: own(i) + decoded(code_ref, i * BLK, scale, cols)

            return load

        segments = [(first, count, segment(code_ref, first)) for code_ref, first, count in spans(got_refs)]
        encode_all(segments or [(0, blocks, segment(None, 0))], out_refs, value_ref, scale_ref, rows)

    shapes = message_shapes(rows, blocks, pieces)
    return run(
        kernel, after, [partial, *received],
        [pl.BlockSpec((1, rows, width), lambda g, place_ref, pattern_ref: (0, place_ref[0], 0))]
        + [VMEM_SPEC] * len(received),
        [VMEM_SPEC] * len(shapes), shapes, rows * width * 4 + rows * blocks * BLK * 2 * (1 + len(received)),
        scalars=(place, pattern), scratch=message_scratch(rows, blocks),
    )


def merge(after, first, second, pieces=1):
    rows, blocks = first[0].shape[0] - EXTRA, sum(piece.shape[1] for piece in first) // BLK

    def kernel(*refs):
        count = len(first)
        out_refs, (value_ref, scale_ref) = refs[2 * count:-2], refs[-2:]

        def segment(a_ref, b_ref):
            def load(j):
                cols = pl.ds(pl.multiple_of(j * BLK, BLK), BLK)
                a_scale = scales(a_ref, rows, cols)
                b_scale = scales(b_ref, rows, cols)
                return lambda i: decoded(a_ref, i * BLK, a_scale, cols) + decoded(b_ref, i * BLK, b_scale, cols)

            return load

        segments = [
            (start, blocks, segment(a_ref, b_ref))
            for (a_ref, start, blocks), b_ref in zip(spans(refs[:count]), refs[count:2 * count])
        ]
        encode_all(segments, out_refs, value_ref, scale_ref, rows)

    shapes = message_shapes(rows, blocks, pieces)
    return run(
        kernel, after, [*first, *second], [VMEM_SPEC] * (2 * len(first)), [VMEM_SPEC] * len(shapes), shapes,
        rows * blocks * BLK * 6, scratch=message_scratch(rows, blocks),
    )


def low_total(after, partial, pattern, place, received):
    _, rows, width = partial.shape

    def kernel(place_ref, pattern_ref, x_ref, *refs):
        for code_ref, first, blocks in spans(refs[:-1]):

            @pl.loop(0, blocks)
            def _(j):
                cols = pl.ds(pl.multiple_of(j * BLK, BLK), BLK)
                target = pl.ds(pl.multiple_of((j + first) * BLK, BLK), BLK)
                scale = scales(code_ref, rows, cols)
                load = masked_load(place_ref, pattern_ref, x_ref, rows, j + first)
                for i in range(rows // BLK):
                    refs[-1][0, pl.ds(i * BLK, BLK), target] = load(i) + decoded(code_ref, i * BLK, scale, cols)

    return run(
        kernel, after, [partial, *received], [VMEM_SPEC] * (1 + len(received)), VMEM_SPEC,
        jax.ShapeDtypeStruct(partial.shape, jnp.float32), partial.size * 10, scalars=(place, pattern),
    )


def mid_half(after, owner, code, base=None):
    rows, width = code[0].shape[0] - EXTRA, sum(piece.shape[1] for piece in code)
    extra = [] if base is None else [base]

    def kernel(owner_ref, *refs):
        for code_ref, first, blocks in spans(refs[:len(code)]):

            @pl.loop(0, blocks)
            def _(j):
                cols = pl.ds(pl.multiple_of(j * BLK, BLK), BLK)
                target = pl.ds(pl.multiple_of((j + first) * BLK, BLK), BLK)
                scale = scales(code_ref, rows, cols)
                for i in range(rows // BLK):
                    refs[-1][0, pl.ds(i * BLK, BLK), target] = decoded(code_ref, i * BLK, scale, cols)

    return run(
        kernel, after, [*code] + extra,
        [VMEM_SPEC] * len(code) + [pl.BlockSpec(memory_space=pl.ANY)] * len(extra),
        pl.BlockSpec((1, rows, width), lambda g, owner_ref: (0, owner_ref[0], 0)),
        jax.ShapeDtypeStruct((1, 2 * rows, width), jnp.float32), rows * width * 6, scalars=(owner,),
        aliases={1 + len(code): 0} if extra else None,
    )


def corner_rows(after, pivots, partial):
    lines = pivots.reshape(-1, BLK)

    def kernel(pivot_ref, x_ref, out_ref):
        source = pivot_ref[0:1, :] % BLK
        turned = (lax.broadcasted_iota(jnp.int32, (BLK, BLK), 0) == source).astype(jnp.float32)
        out_ref[...] = lax.dot_general(
            turned, x_ref[0], (((0,), (0,)), ((), ())), precision=HIGHEST, preferred_element_type=jnp.float32
        )

    return run(
        kernel, after, [lines, partial],
        [pl.BlockSpec((8, BLK), lambda g: (0, 0)), pl.BlockSpec((1, BLK, BLK), lambda g: (0, 0, 0))],
        pl.BlockSpec((BLK, BLK), lambda g: (0, 0)), jax.ShapeDtypeStruct((BLK, BLK), jnp.float32), BLK * BLK * 8,
    )


def corner_sum(after, parts):
    def kernel(a_ref, b_ref, c_ref, d_ref, out_ref):
        out_ref[...] = (a_ref[...] + b_ref[...]) + (c_ref[...] + d_ref[...])

    shape = jax.ShapeDtypeStruct((BLK, BLK), jnp.float32)
    return run(kernel, after, parts, [VMEM_SPEC] * 4, VMEM_SPEC, shape, BLK * BLK * 20)


def factor(after, corner):
    order = corner.shape[0]

    def kernel(a_ref, packed_ref, lower_ref, upper_ref, direct, direct_unit, turned, turned_unit):
        lane = lax.broadcasted_iota(jnp.int32, (order, order), 1)
        sub = lax.broadcasted_iota(jnp.int32, (order, order), 0)
        lane_row = lax.broadcasted_iota(jnp.int32, (1, order), 1)
        sub_col = lax.broadcasted_iota(jnp.int32, (order, 1), 0)
        unit = (lane == sub).astype(jnp.float32)
        direct[...] = a_ref[...]
        direct_unit[...] = unit
        turned[...] = a_ref[...].T
        turned_unit[...] = unit

        @pl.loop(0, order - 1)
        def _(k):
            for held, held_unit in ((direct, direct_unit), (turned, turned_unit)):
                left = held[...]
                row_left = held[pl.ds(k, 1), :]
                row_right = held_unit[pl.ds(k, 1), :]
                col = jnp.sum(jnp.where(lane == k, left, 0.0), axis=1, keepdims=True)
                pivot = jnp.sum(jnp.where(lane_row == k, row_left, 0.0), axis=1, keepdims=True)
                below = sub_col > k
                multipliers = jnp.where(below, col / pivot, 0.0)
                fresh = left - multipliers * jnp.where(lane_row > k, row_left, 0.0)
                held[...] = jnp.where((lane == k) & below, multipliers, fresh)
                held_unit[...] = held_unit[...] - multipliers * row_right

        packed_ref[...] = direct[...]
        lower_ref[...] = direct_unit[...]
        pivots = jnp.sum(jnp.where(lane == sub, turned[...], 0.0), axis=1, keepdims=True)
        upper_ref[...] = (turned_unit[...] / pivots).T

    shape = jax.ShapeDtypeStruct((order, order), jnp.float32)
    return run(
        kernel, after, [corner], [VMEM_SPEC], [VMEM_SPEC] * 3, [shape] * 3, order * order * 16, 2e9,
        scratch=[pltpu.VMEM((order, order), jnp.float32)] * 4,
    )


def exact_dot(left, right):
    return jnp.dot(left, right, precision=HIGHEST, preferred_element_type=jnp.float32)


def low_dot(left, right):
    return jnp.dot(left, right, preferred_element_type=jnp.float32)


def permuted_codes(order_block, codes, scale):
    codes = codes.astype(jnp.int32)
    high = (codes >> 8).astype(jnp.float32).astype(jnp.bfloat16)
    low = (codes & 255).astype(jnp.float32).astype(jnp.bfloat16)
    both = jnp.concatenate([high, low], axis=0)
    return low_dot(jnp.concatenate([order_block * 256.0, order_block], axis=1).astype(jnp.bfloat16), both) * scale


def lower_panel(after, flags, order, own, received, upper_inverse):
    rows = own.shape[0] - EXTRA

    def kernel(flag_ref, order_ref, own_ref, got_ref, inverse_ref, slab_ref, low_ref):
        cols = pl.ds(0, PANEL)
        own_scale = scales(own_ref, rows, cols)
        got_scale = scales(got_ref, rows, cols)
        first_col = flag_ref[3] == 0

        @pl.loop(0, rows // BLK, unroll=4)
        def _(i):
            here = pl.ds(pl.multiple_of(i * BLK, BLK), BLK)
            order_block = order_ref[here, :]
            slab_ref[here, :] = permuted_codes(order_block, own_ref[here, :], own_scale) + permuted_codes(
                order_block, got_ref[here, :], got_scale
            )

        panel = exact_dot(slab_ref[...], inverse_ref[...])
        low_ref[...] = panel.astype(jnp.bfloat16)

        @pl.when(first_col)
        def _():
            slab_ref[...] = panel

    return run(
        kernel, after, [flags, order, own, received, upper_inverse], [SMEM_SPEC] + [VMEM_SPEC] * 4, [VMEM_SPEC] * 2,
        [jax.ShapeDtypeStruct((rows, PANEL), jnp.float32), jax.ShapeDtypeStruct((rows, PANEL), jnp.bfloat16)],
        rows * PANEL * 14, rows * PANEL * PANEL * 20,
    )


def upper_panel(after, flags, order, slab, own, received, lower_inverse):
    rows, rest = own.shape[0] - EXTRA, own.shape[1]
    width = rest + PANEL

    def kernel(flag_ref, order_ref, slab_ref, own_ref, own_scale, got_ref, got_scale, inverse_ref, up_ref, low_ref):
        first = exact_dot(inverse_ref[...], slab_ref[...])
        up_ref[:, :PANEL] = first
        low_ref[:, :PANEL] = first.astype(jnp.bfloat16)

        def write(code_ref, scale_ref):
            scale = jnp.exp2(scale_ref[...].astype(jnp.int32).astype(jnp.float32)[0:1])
            value = permuted_codes(order_ref[...], code_ref[...], scale)
            value = exact_dot(inverse_ref[...], value)
            up_ref[:, PANEL:] = value
            low_ref[:, PANEL:] = value.astype(jnp.bfloat16)

        pl.when(flag_ref[1] == 0)(lambda: write(own_ref, own_scale))
        pl.when(flag_ref[1] == 1)(lambda: write(got_ref, got_scale))

    first_block = lambda g: (0, 0)
    code_spec = pl.BlockSpec((BLK, rest), first_block)
    scale_spec = pl.BlockSpec((EXTRA, rest), lambda g: (rows // EXTRA, 0))
    square = pl.BlockSpec((BLK, BLK), first_block)
    return run(
        kernel, after, [flags, order, slab, own, own, received, received, lower_inverse],
        [SMEM_SPEC, square, square, code_spec, scale_spec, code_spec, scale_spec, square],
        [pl.BlockSpec((BLK, width), first_block)] * 2,
        [jax.ShapeDtypeStruct((PANEL, width), jnp.float32), jax.ShapeDtypeStruct((PANEL, width), jnp.bfloat16)],
        BLK * width * 10, BLK * BLK * width * 16,
    )


def top_total(after, flags, order, codes, slab, lower_low, upper_low, upper, packed):
    total_rows = slab.shape[0]
    rows, rest = codes[0].shape[0] - EXTRA, codes[0].shape[1]
    width = rest + PANEL
    part_blocks = rows // BLK

    def kernel(flag_ref, order_ref, own_a, got_a, own_b, got_b, slab_ref, low_ref, up_low_ref, up_ref, packed_ref, out_ref):
        def block_rows(sub):
            i = part_blocks * pl.program_id(0) + sub
            here = pl.ds(sub * BLK, BLK)
            part = i // part_blocks
            row = pl.multiple_of((i % part_blocks) * BLK, BLK)
            first_row = (flag_ref[2] == 0) & (i == 0)
            first_col = flag_ref[3] == 0
            rest_cols = pl.ds(0, rest)

            @pl.when(jnp.logical_not(first_row))
            def _():
                low = low_ref[here, :]

                def write(code_ref):
                    scale = scales(code_ref, rows, rest_cols)
                    value = permuted_codes(order_ref[here, :], code_ref[pl.ds(row, BLK), :], scale)
                    out_ref[here, PANEL:] = value - low_dot(low, up_low_ref[:, PANEL:])

                owned_b = part == flag_ref[1]
                owned_a = part == 2 + flag_ref[0]
                pl.when(owned_b)(lambda: write(own_b))
                pl.when((part < 2) & jnp.logical_not(owned_b))(lambda: write(got_b))
                pl.when(owned_a)(lambda: write(own_a))
                pl.when((part >= 2) & jnp.logical_not(owned_a))(lambda: write(got_a))
                product = low_dot(low, up_low_ref[:, :PANEL])
                out_ref[here, :PANEL] = jnp.where(first_col, slab_ref[here, :], slab_ref[here, :] - product)

            @pl.when(first_row)
            def _():
                out_ref[here, PANEL:] = up_ref[:, PANEL:]
                out_ref[here, :PANEL] = jnp.where(first_col, packed_ref[...], up_ref[:, :PANEL])

        for sub in range(part_blocks):
            block_rows(sub)

    square = pl.BlockSpec((rows, BLK), lambda i: (i, 0))
    return run(
        kernel, after, [flags, order, *codes, slab, lower_low, upper_low, upper, packed],
        [SMEM_SPEC, square] + [VMEM_SPEC] * 4 + [square, square] + [VMEM_SPEC] * 3,
        pl.BlockSpec((rows, width), lambda i: (i, 0)),
        jax.ShapeDtypeStruct((total_rows, width), jnp.float32),
        total_rows * width * 6, total_rows * width * BLK * 6, grid=(total_rows // rows,),
    )


def on_device(partial_top, partial_mid, partial_low, pattern_top, pattern_mid, pattern_low, pivots):
    layer, row, col = (lax.axis_index(name) for name in ("layer", "row", "col"))
    bits = list(range(lax.axis_size("layer").bit_length() - 1))
    low_bit, high_bit = layer & 1, (layer >> 1) & 1
    flags = jnp.stack([low_bit, high_bit, row, col]).astype(jnp.int32)
    order = ((pivots % BLK)[:, None] == jnp.arange(BLK, dtype=jnp.int32)[None, :]).astype(jnp.bfloat16)

    def sender(partial, pattern, rows, first_block, blocks):
        corner_block = [row * pattern.shape[1], col * pattern.shape[2]]

        def encode(after, part, received=(), pieces=1):
            place = jnp.stack([jnp.asarray(part, jnp.int32), *corner_block]).astype(jnp.int32)
            return encode_partial(after, partial, pattern[0], place, rows, first_block, blocks, received, pieces)

        return encode

    def exchanged(after, own, got, some):
        own = merge(after, own, got)
        for bit in some:
            own = merge([], own, swapped(own, bit))
        return own

    top_rows, top_blocks = partial_top.shape[1], partial_top.shape[2] // BLK
    mid_blocks, low_blocks = partial_mid.shape[2] // BLK, partial_low.shape[2] // BLK
    low_rows = partial_low.shape[1]
    encode_mid = sender(partial_mid, pattern_mid, partial_mid.shape[1] // 2, 0, mid_blocks)
    encode_slab = sender(partial_top, pattern_top, top_rows, 0, 1)
    encode_top = sender(partial_top, pattern_top, top_rows // 4, 1, top_blocks - 1)
    encode_low = sender(partial_low, pattern_low, low_rows, 0, low_blocks)

    count = lax.axis_size("layer")
    corner = corner_rows([], pivots, partial_top)
    beside = [lax.ppermute(corner, "layer", [(i, i ^ apart) for i in range(count)]) for apart in (1, 2, 3)]
    slab = encode_slab([*[corner]], 0)
    slab_got = swapped(slab, 0)
    mid_sent = encode_mid([*slab, *beside], 1 - high_bit, (), 1)
    mid_got = swapped(mid_sent, 1)
    a_sent = encode_top([*mid_sent], 3 - low_bit)
    a_got = swapped(a_sent, 0)
    summed = corner_sum([*a_sent], [corner, *beside])
    corner = summed
    for bit in bits[2:]:
        corner = corner + swapped(corner, bit)
    corner_row = broadcast_stages(corner, "row")
    corner_col = broadcast_stages(corner_row[-1], "col")
    corner_all = corner_col[-1]
    b_sent = encode_top([*[summed]], 1 - high_bit)
    b_got = swapped(b_sent, 1)
    slab = exchanged([*b_sent, corner_row[-1]], slab, slab_got, bits[1:-1])
    slab_got = swapped(slab, bits[-1])
    mid = encode_mid([*slab, corner_col[0]], high_bit, mid_got, 2)
    mid_got = swapped(mid, 0)
    packed, lower_inverse, upper_inverse = factor([*mid], corner_all)
    b = encode_top([*[packed]], high_bit, b_got)
    b_got = swapped(b, 0)
    a = encode_top([*b], 2 + low_bit, a_got)
    a_got = swapped(a, 1)
    panel, lower_low = lower_panel([*a, *mid_got], flags, order, *slab, *slab_got, upper_inverse)
    lower_stages = broadcast_stages(lower_low, "col")
    lower_low = lower_stages[-1]
    mid = merge([*[panel]], mid, mid_got, 1)
    mid_got = swapped(mid, 1)
    b = exchanged([*mid], b, b_got, bits[2:])
    b_got = swapped(b, 1)
    a = exchanged([*b], a, a_got, bits[2:])
    a_got = swapped(a, 0)
    mid_sums = mid_half([*a], high_bit[None].astype(jnp.int32), mid)
    low = encode_low([*[mid_sums]], 0, (), 1)
    low_got = swapped(low, 0)
    upper, upper_low = upper_panel([*low, *a_got], flags, order, panel, *b, *b_got, lower_inverse)
    upper_low = broadcast_stages(upper_low, "row")[-1]
    top_factor = top_total([*[upper]], flags, order, (*a, *a_got, *b, *b_got), panel, lower_low, upper_low, upper, packed)
    low_place = jnp.stack([jnp.int32(0), row * pattern_low.shape[1], col * pattern_low.shape[2]]).astype(jnp.int32)
    low_sums = low_total([*[top_factor]], partial_low, pattern_low[0], low_place, low_got)
    mid_sums = mid_half([top_factor], (1 - high_bit)[None].astype(jnp.int32), mid_got, mid_sums)
    return top_factor, mid_sums, low_sums


def solution(mesh):
    placed = (
        P("layer", "row", "col"),
        P("layer", "row", "col"),
        P("layer", "row", "col"),
        P("layer", "row", "col"),
        P("layer", "row", "col"),
        P("layer", "row", "col"),
        P("row"),
    )
    return jax.shard_map(
        on_device,
        mesh=mesh,
        in_specs=placed,
        out_specs=(P("row", "col"), P("layer", "row", "col"), P("layer", "row", "col")),
        check_vma=False,
    )
```
